32 devices in a mesh: groups: 2 (over y), tm: 4 (over z), mp: 4 (over x, core).
Axes of the slice: x: 2, y: 2, z: 4, core: 2. Of those that a mesh axis runs over, the one named last changes fastest.
Arguments:
- waveform: float32 [1310720], P(('groups', 'tm', 'mp')), parts along dimension 0, may hold values from -0.8 to 0.8
- segment_start: int32 [2048], P(('groups', 'tm')), parts along dimension 0, may hold values from 0 to 1023, as said below
- segment_end: int32 [2048], P(('groups', 'tm')), parts along dimension 0, may hold values from 1 to 1024, as said below
- w_subsample: bfloat16 [512, 1536], replicated, may hold values from -0.25 to 0.25
- w_attention: bfloat16 [3, 1536, 1536], P(None, None, 'mp')
- w_output: bfloat16 [1536, 1536], P('mp'), may hold values from -0.15625 to 0.15625
- gain_convolution: float32 [1536], replicated, may hold values from 0.1 to 1.9
- w_depthwise: bfloat16 [31, 1536], replicated, may hold values from -1 to 1
Outputs:
- encoded: bfloat16 [2048, 1536], P(('groups', 'tm', 'mp')), parts along dimension 0
The draws below stay inside these ranges and needn't reach their ends.
There are 2 independent parts, one for each index of `groups`. The reference program is written for one: setup_inputs(seed, part) draws one part's arguments, and reference() takes and returns one part's arrays. A program takes and returns all parts, laid end to end along the dimension named above; an argument that names none is the same for every part. Nothing has to cross between parts.
Inputs may be any that keep to these rules, and one draw needn't show every extreme that they name: Segments are contiguous runs of frames that tile the slab: segment_start[i] <= i < segment_end[i], and all frames of a run share both values; every run has 150 to 750 frames except the first and the last, which may be shorter; one run of exactly 750 frames lies in every draw. `segment_end`: the end of the run holding each frame, as described for segment_start.
All inputs are finite; a program needn't handle non-finite values.
Results may differ from the reference program's by a relative error of at most 0.015.
Values may be sent and summed in bfloat16 or wider, within the bound.
No kernel may reach another device: no remote copies, remote signals or barrier semaphores. Data moves between devices by JAX's collectives and lax.ppermute only.
A program may use at most 64 MiB of HBM per device.

```python
import math
import jax
import jax.numpy as jnp
from jax import lax

D = 1536
HEADS = 24
HD = 64
NMEL = 128
NFFT = 400
HOP = 160
BINS = 256
SUB = 4
KERNEL = 31
SEG_MAX = 750
FT = 256
FRAMES = 1024
SAMPLES = 655360
N_MP = 4


def segment_bounds(key):
    shortest = SEG_MAX // 5
    run_count = FRAMES // shortest + 2
    offset = jax.random.randint(jax.random.fold_in(key, 12), (), 0, FRAMES - SEG_MAX + 1, dtype=jnp.int32)
    left_lengths = jax.random.randint(jax.random.fold_in(key, 11), (run_count,), shortest, SEG_MAX + 1, dtype=jnp.int32)
    right_lengths = jax.random.randint(jax.random.fold_in(key, 13), (run_count,), shortest, SEG_MAX + 1, dtype=jnp.int32)
    left_bounds = jnp.maximum(offset - jnp.cumsum(left_lengths).astype(jnp.int32), 0)
    right_bounds = jnp.minimum(offset + SEG_MAX + jnp.cumsum(right_lengths).astype(jnp.int32), FRAMES)
    fixed_bounds = jnp.stack([jnp.zeros((), jnp.int32), offset, offset + SEG_MAX, jnp.full((), FRAMES, jnp.int32)]).astype(jnp.int32)
    bounds = jnp.concatenate([fixed_bounds, left_bounds, right_bounds]).astype(jnp.int32)
    frame_index = jnp.arange(FRAMES, dtype=jnp.int32)
    starts = jnp.max(jnp.where(bounds[None, :] <= frame_index[:, None], bounds[None, :], 0), axis=1).astype(jnp.int32)
    finish = jnp.min(jnp.where(bounds[None, :] > frame_index[:, None], bounds[None, :], FRAMES), axis=1).astype(jnp.int32)
    return (starts, finish)


def draw_segment_start(key, part):
    return segment_bounds(jax.random.fold_in(key, 5))[0]


def draw_segment_end(key, part):
    return segment_bounds(jax.random.fold_in(key, 5))[1]


def draw_w_attention(key, part):
    base = jax.random.normal(jax.random.fold_in(key, 1), (3, D, D), jnp.float32) / math.sqrt(D)
    value_part = base[2] * 3.0
    return jnp.stack([base[0], base[1], value_part]).astype(jnp.bfloat16)


def shard_levels(own_key, shape, cuts, low, largest):
    def one(dim, parts):
        steps = jax.random.uniform(jax.random.fold_in(jax.random.fold_in(own_key, 6), dim), (parts,), jnp.float32, low / len(cuts), largest / len(cuts))
        return jnp.repeat(jnp.exp(steps), shape[dim] // parts).reshape((-1,) + (1,) * (len(shape) - dim - 1))

    gain = one(*cuts[0])
    for cut in cuts[1:]:
        gain = gain * one(*cut)
    return gain


def centred(stream_key, dims, width, reach, cuts=(), held_as=jnp.bfloat16):
    gain = shard_levels(stream_key, dims, cuts, -0.22, 0.18) if cuts else 1.0
    drawn = jax.random.normal(stream_key, dims, jnp.float32) * width * gain
    return jnp.minimum(jnp.maximum(drawn, -reach), reach).astype(held_as)


def setup_inputs(seed: int = 0, part: int = 0) -> dict:
    seeds = jax.random.split(jax.random.key(seed), 9)
    part_keys = jax.random.split(jax.random.fold_in(seeds[8], part), 9)
    return {
        "waveform": centred(part_keys[0], (SAMPLES,), 0.1, 0.8, ((0, 16),), jnp.float32),
        "segment_start": draw_segment_start(jax.random.fold_in(jax.random.fold_in(seeds[8], part), 71), part),
        "segment_end": draw_segment_end(jax.random.fold_in(jax.random.fold_in(seeds[8], part), 71), part),
        "w_subsample": centred(seeds[3], (SUB * NMEL, D), (SUB * NMEL) ** -0.5, 0.25),
        "w_attention": draw_w_attention(jax.random.fold_in(seeds[8], 71), part),
        "w_output": centred(seeds[5], (D, D), D ** -0.5, 0.15625, ((0, 4),)),
        "gain_convolution": jnp.clip(1.0 + 0.18 * jax.random.normal(seeds[6], (D,), jnp.float32), 0.1, 1.9),
        "w_depthwise": centred(seeds[7], (KERNEL, D), KERNEL ** -0.5, 1.0),
    }


def fourier_table():
    sample_index = jnp.arange(NFFT, dtype=jnp.int32)[:, None]
    bin_index = jnp.arange(BINS, dtype=jnp.int32)[None, :]
    phase_int = sample_index * bin_index % NFFT
    angle_rad = phase_int.astype(jnp.float32) * (2.0 * math.pi / NFFT)
    window_row = 0.5 - 0.5 * jnp.cos(jnp.arange(NFFT, dtype=jnp.float32) * (2.0 * math.pi / NFFT))
    kept_bins = bin_index <= NFFT // 2
    cosine_part = jnp.where(kept_bins, jnp.cos(angle_rad), 0.0) * window_row[:, None]
    sine_part = jnp.where(kept_bins, -jnp.sin(angle_rad), 0.0) * window_row[:, None]
    return jnp.concatenate([cosine_part, sine_part], axis=1)

def mel_bank():
    mel_top = 2595.0 * math.log10(1.0 + 8000.0 / 700.0)
    mel_points = jnp.arange(NMEL + 2, dtype=jnp.float32) * (mel_top / (NMEL + 1))
    hertz_points = 700.0 * (jnp.power(10.0, mel_points / 2595.0) - 1.0)
    edges = hertz_points * (NFFT / 16000.0)
    centers = edges[1:-1]
    widths = jnp.maximum(edges[2:] - edges[1:-1], 1.0)
    bin_value = jnp.arange(BINS, dtype=jnp.float32)[:, None]
    triangle = jnp.maximum(0.0, 1.0 - jnp.abs(bin_value - centers[None, :]) / widths[None, :])
    return jnp.where(bin_value <= NFFT // 2, triangle, 0.0)

def frame_rows(padded, frame_count):
    blocks_needed = -(-NFFT // HOP)
    blocks = padded[:(frame_count + blocks_needed - 1) * HOP].reshape(frame_count + blocks_needed - 1, HOP)
    pieces = [blocks[offset:offset + frame_count] for offset in range(blocks_needed)]
    return jnp.concatenate(pieces, axis=1)[:, :NFFT]

def log_mel(frames):
    spectrum = jnp.dot(frames, fourier_table(), precision=lax.Precision.HIGHEST, preferred_element_type=jnp.float32)
    spectral_power = jnp.square(spectrum[:, :BINS]) + jnp.square(spectrum[:, BINS:])
    energy = jnp.dot(spectral_power, mel_bank(), precision=lax.Precision.HIGHEST, preferred_element_type=jnp.float32)
    return jnp.log(energy + 1e-06)

def normalize(values):
    values = values.astype(jnp.float32)
    center = lax.optimization_barrier(jnp.mean(values, axis=-1, keepdims=True))
    spread = lax.optimization_barrier(jnp.mean(jnp.square(values - center), axis=-1, keepdims=True))
    return (values - center) * lax.rsqrt(spread + 1e-05)

def layer_norm(values, gain_row):
    return normalize(values) * gain_row.astype(jnp.float32)

def reference(waveform, segment_start, segment_end, w_subsample, w_attention, w_output, gain_convolution, w_depthwise):
    blocks_needed = -(-NFFT // HOP)
    padded = jnp.concatenate([waveform, jnp.zeros((blocks_needed * HOP,), waveform.dtype)])
    stacked = log_mel(frame_rows(padded, FRAMES * SUB)).reshape(FRAMES, SUB * NMEL).astype(jnp.bfloat16)
    features = lax.optimization_barrier(jnp.dot(stacked, w_subsample, preferred_element_type=jnp.float32).astype(jnp.bfloat16))
    normed = normalize(features).astype(jnp.bfloat16)
    queries = lax.optimization_barrier(jnp.dot(normed, w_attention[0], preferred_element_type=jnp.float32).astype(jnp.bfloat16))
    key_rows = lax.optimization_barrier(jnp.dot(normed, w_attention[1], preferred_element_type=jnp.float32).astype(jnp.bfloat16))
    value_rows = lax.optimization_barrier(jnp.dot(normed, w_attention[2], preferred_element_type=jnp.float32).astype(jnp.bfloat16))
    key_pad = jnp.pad(key_rows, ((SEG_MAX, SEG_MAX), (0, 0)))
    value_pad = jnp.pad(value_rows, ((SEG_MAX, SEG_MAX), (0, 0)))
    scale_factor = 1.0 / math.sqrt(HD)
    window_len = FT + 2 * SEG_MAX

    def attend_block(block_index):
        begin_row = block_index * FT
        query_block = lax.dynamic_slice_in_dim(queries, begin_row, FT, 0).astype(jnp.float32).reshape(FT, HEADS, HD)
        key_block = lax.dynamic_slice_in_dim(key_pad, begin_row, window_len, 0).astype(jnp.float32).reshape(window_len, HEADS, HD)
        value_block = lax.dynamic_slice_in_dim(value_pad, begin_row, window_len, 0).astype(jnp.float32).reshape(window_len, HEADS, HD)
        positions = begin_row - SEG_MAX + jnp.arange(window_len, dtype=jnp.int32)
        starts = lax.dynamic_slice_in_dim(segment_start, begin_row, FT, 0)
        finish = lax.dynamic_slice_in_dim(segment_end, begin_row, FT, 0)
        scores = jnp.einsum('qhd,khd->qhk', query_block, key_block) * scale_factor
        allowed = (positions[None, :] >= starts[:, None]) & (positions[None, :] < finish[:, None])
        scores = jnp.where(allowed[:, None, :], scores, -1e+30)
        row_max = lax.optimization_barrier(jnp.max(scores, axis=-1, keepdims=True))
        weights = jnp.exp(scores - row_max)
        rounded = lax.optimization_barrier(weights.astype(jnp.bfloat16)).astype(jnp.float32)
        numerator = jnp.einsum('qhk,khd->qhd', rounded, value_block)
        denominator = lax.optimization_barrier(jnp.sum(weights, axis=-1))
        return (numerator / denominator[..., None]).reshape(FT, D).astype(jnp.bfloat16)
    attended = lax.map(attend_block, jnp.arange(FRAMES // FT, dtype=jnp.int32)).reshape(FRAMES, D)
    group_width = D // N_MP
    branch = jnp.zeros((FRAMES, D), jnp.float32)
    for group_index in range(N_MP):
        lower = group_index * group_width
        partial_sum = jnp.dot(attended[:, lower:lower + group_width], w_output[lower:lower + group_width], preferred_element_type=jnp.float32)
        branch = branch + lax.optimization_barrier(partial_sum.astype(jnp.bfloat16)).astype(jnp.float32)
    mixed_rows = lax.optimization_barrier((features.astype(jnp.float32) + branch).astype(jnp.bfloat16))
    conv_input = lax.optimization_barrier(layer_norm(mixed_rows, gain_convolution).astype(jnp.bfloat16))
    half_kernel = KERNEL // 2
    padded_conv = jnp.pad(conv_input.astype(jnp.float32), ((half_kernel, half_kernel), (0, 0)))
    convolved = jnp.zeros((FRAMES, D), jnp.float32)
    for tap_index in range(KERNEL):
        convolved = convolved + padded_conv[tap_index:tap_index + FRAMES] * w_depthwise[tap_index].astype(jnp.float32)
    return (mixed_rows.astype(jnp.float32) + jax.nn.silu(convolved)).astype(jnp.bfloat16)
```

```python
import math

import jax
import jax.numpy as jnp
import numpy as np
from jax import lax
from jax.experimental import pallas as pl
from jax.experimental.pallas import tpu as pltpu
from jax.sharding import PartitionSpec as P

HD = 64
NMEL = 128
NFFT = 400
HOP = 160
BINS = 256
SUB = 4
KERNEL = 31
SEG_MAX = 750
LANES = 128
HALO = 16
FRAME_ROWS = SUB * HOP // LANES
WIDE = -(-NFFT // LANES) * LANES
VMEM_BYTES = 40 * 1024 * 1024


def split_high_low(table):
    high = table.astype(jnp.bfloat16)
    low = (table - high.astype(np.float32)).astype(jnp.bfloat16)
    return high, low


def fourier_table():
    sample_index = np.arange(NFFT)[:, None]
    bin_index = np.arange(BINS)[None, :]
    angle = (sample_index * bin_index % NFFT) * (2.0 * math.pi / NFFT)
    window = 0.5 - 0.5 * np.cos(np.arange(NFFT) * (2.0 * math.pi / NFFT))
    kept = bin_index <= NFFT // 2
    cosine = np.where(kept, np.cos(angle), 0.0) * window[:, None]
    sine = np.where(kept, -np.sin(angle), 0.0) * window[:, None]
    table = np.concatenate([cosine, sine], axis=1).astype(np.float32)
    return np.pad(table, ((0, WIDE - NFFT), (0, 0)))


def mel_bank():
    mel_top = 2595.0 * math.log10(1.0 + 8000.0 / 700.0)
    mel_points = np.arange(NMEL + 2) * (mel_top / (NMEL + 1))
    edges = 700.0 * (np.power(10.0, mel_points / 2595.0) - 1.0) * (NFFT / 16000.0)
    widths = np.maximum(edges[2:] - edges[1:-1], 1.0)
    bin_value = np.arange(BINS)[:, None]
    triangle = np.maximum(0.0, 1.0 - np.abs(bin_value - edges[None, 1:-1]) / widths[None, :])
    return np.where(bin_value <= NFFT // 2, triangle, 0.0).astype(np.float32)


def dot32(left, right):
    return jnp.dot(left, right, preferred_element_type=jnp.float32)


def dot_split(values, high_ref, low_ref):
    high = values.astype(jnp.bfloat16)
    low = (values - high.astype(jnp.float32)).astype(jnp.bfloat16)
    return dot32(high, high_ref[...]) + (dot32(low, high_ref[...]) + dot32(high, low_ref[...]))


def normalize(values):
    center = jnp.mean(values, axis=-1, keepdims=True)
    shifted = values - center
    spread = jnp.mean(jnp.square(shifted), axis=-1, keepdims=True)
    return shifted * lax.rsqrt(spread + 1e-05)


def call(kernel, out_shape, operands, scratch=(), scalars=0, flops=0):
    specs = [pl.BlockSpec(memory_space=pltpu.SMEM)] * scalars
    specs += [pl.BlockSpec(memory_space=pltpu.VMEM)] * (len(operands) - scalars)
    return pl.pallas_call(
        kernel,
        out_shape=out_shape,
        in_specs=specs,
        out_specs=jax.tree.map(lambda _: pl.BlockSpec(memory_space=pltpu.VMEM), out_shape),
        scratch_shapes=list(scratch),
        compiler_params=pltpu.CompilerParams(vmem_limit_bytes=VMEM_BYTES),
        cost_estimate=pl.CostEstimate(flops=flops, bytes_accessed=1000000, transcendentals=0),
    )(*operands)


def log_mel_rows(samples, next_samples, frames_local):
    table_high, table_low = split_high_low(fourier_table())
    bank_high, bank_low = split_high_low(mel_bank())
    rows = frames_local * FRAME_ROWS
    extra = next_samples.shape[0]

    def kernel(wave, following, th, tl, bh, bl, out, held):
        held[0:rows, :] = wave[...]
        held[rows : rows + extra, :] = following[...]
        lines = [
            held[pl.ds(j, frames_local, stride=FRAME_ROWS), :] for j in range(FRAME_ROWS + extra)
        ]
        windows = []
        for sub in range(SUB):
            line, lane = divmod(sub * HOP, LANES)
            taken = jnp.concatenate(lines[line : line + WIDE // LANES], axis=1)
            windows.append(pltpu.roll(taken, WIDE - lane, axis=1) if lane else taken)
        spectrum = dot_split(jnp.concatenate(windows, axis=0), th, tl)
        power = jnp.square(spectrum[:, :BINS]) + jnp.square(spectrum[:, BINS:])
        mel = jnp.log(dot_split(power, bh, bl) + 1e-06)
        for sub in range(SUB):
            out[:, sub * NMEL : (sub + 1) * NMEL] = mel[
                sub * frames_local : (sub + 1) * frames_local
            ].astype(jnp.bfloat16)

    return call(
        kernel,
        jax.ShapeDtypeStruct((frames_local, SUB * NMEL), jnp.bfloat16),
        (samples, next_samples, table_high, table_low, bank_high, bank_low),
        scratch=[pltpu.VMEM((rows + 8, LANES), jnp.float32)],
        flops=6 * frames_local * SUB * WIDE * 2 * BINS,
    )


def project_rows(stacks, w_subsample, w_attention):
    counts = [stack.shape[0] for stack in stacks]
    rows, width = sum(counts), w_attention.shape[2]
    model = w_subsample.shape[1]

    def kernel(*refs):
        stack_refs, (w_sub, w_att), outs = refs[: len(counts)], refs[len(counts) : -3], refs[-3:]
        begin = 0
        for stack_ref, count in zip(stack_refs, counts):
            features = dot32(stack_ref[...], w_sub[...]).astype(jnp.bfloat16)
            normed = normalize(features.astype(jnp.float32)).astype(jnp.bfloat16)
            for part in range(3):
                outs[part][begin : begin + count, :] = dot32(normed, w_att[part]).astype(
                    jnp.bfloat16
                )
            begin += count

    shape = jax.ShapeDtypeStruct((rows, width), jnp.bfloat16)
    return call(
        kernel,
        (shape, shape, shape),
        (*stacks, w_subsample, w_attention),
        flops=2 * rows * model * (w_subsample.shape[0] + 3 * width),
    )


def attend(indices, bounds, key_positions, queries, keys, values, frames_local, parts):
    counts = [q.shape[0] for q in queries]
    rows, width = sum(counts), queries[0].shape[1]
    groups = len(counts)
    frames_shard = frames_local * parts
    extended = frames_shard + 2 * HALO
    window = frames_local + 2 * HALO

    def kernel(*refs):
        index_ref, bound_ref, position_ref = refs[:3]
        q_refs, k_refs, v_refs = (
            refs[3 + groups * part : 3 + groups * (part + 1)] for part in range(3)
        )
        outs = refs[3 + 3 * groups : 3 + 3 * groups + parts]
        q_all, q_rows, result, bias = refs[3 + 3 * groups + parts :]
        begin = 0
        for q_ref, count in zip(q_refs, counts):
            q_all[begin : begin + count, :] = q_ref[...]
            begin += count

        def source(slot, offset, count):
            start = pl.multiple_of(index_ref[slot] * frames_local + offset, HALO)
            return q_all[pl.ds(start, count), :]

        q_rows[0:HALO, :] = source(0, frames_local - HALO, HALO)
        for part in range(parts):
            begin = HALO + part * frames_local
            q_rows[begin : begin + frames_local, :] = source(1 + part, 0, frames_local)
        q_rows[HALO + frames_shard : extended, :] = source(1 + parts, 0, HALO)
        first, last = (
            jnp.transpose(
                jnp.broadcast_to(bound_ref[line : line + 1, :].astype(jnp.float32), (LANES, extended))
            )
            for line in range(2)
        )
        for begin in range(0, rows, LANES):
            at = position_ref[0:1, begin : begin + LANES].astype(jnp.float32)
            allowed = (at >= first) & (at < last)
            bias[:, begin : begin + LANES] = jnp.where(allowed, 0.0, -1e30)
        for lane in range(0, width, LANES):
            span = min(LANES, width - lane)
            q_pair = q_rows[:, lane : lane + span]
            k_pairs = [k_ref[:, lane : lane + span] for k_ref in k_refs]
            v_pairs = [v_ref[:, lane : lane + span] for v_ref in v_refs]
            head_of = lax.broadcasted_iota(jnp.int32, (extended, span), 1) // HD
            merged = jnp.zeros((extended, span), jnp.float32)
            for head in range(span // HD):
                mine = head_of == head
                q_head = jnp.where(mine, q_pair, jnp.zeros_like(q_pair)) * jnp.bfloat16(
                    1.0 / math.sqrt(HD)
                )
                scores = jnp.concatenate(
                    [
                        lax.dot_general(
                            q_head,
                            k_pair,
                            (((1,), (1,)), ((), ())),
                            preferred_element_type=jnp.float32,
                        )
                        for k_pair in k_pairs
                    ],
                    axis=1,
                )
                scores = scores + bias[...]
                weights = jnp.exp(scores - jnp.max(scores, axis=1, keepdims=True))
                total = jnp.sum(weights, axis=1, keepdims=True)
                rounded = weights.astype(jnp.bfloat16)
                numerator = jnp.zeros((extended, span), jnp.float32)
                begin = 0
                for v_pair, count in zip(v_pairs, counts):
                    numerator += dot32(rounded[:, begin : begin + count], v_pair)
                    begin += count
                merged = jnp.where(mine, numerator / total, merged)
            result[:, lane : lane + span] = merged.astype(jnp.bfloat16)
        for part in range(parts):
            start = pl.multiple_of(index_ref[2 + parts + part] * frames_local, HALO)
            outs[part][...] = result[pl.ds(start, window), :]

    return call(
        kernel,
        [jax.ShapeDtypeStruct((window, width), jnp.bfloat16)] * parts,
        (indices, bounds, key_positions, *queries, *keys, *values),
        scratch=[
            pltpu.VMEM((rows, width), jnp.bfloat16),
            pltpu.VMEM((extended, width), jnp.bfloat16),
            pltpu.VMEM((extended, width), jnp.bfloat16),
            pltpu.VMEM((extended, rows), jnp.float32),
        ],
        scalars=1,
        flops=4 * extended * rows * width * 4,
    )


def window_features(indices, stacks, w_subsample, frames_local):
    counts = [stack.shape[0] for stack in stacks]
    depth, model = w_subsample.shape
    window = frames_local + 2 * HALO

    def kernel(index_ref, *refs):
        stack_refs, w_sub, out, held, taken = refs[:-4], refs[-4], refs[-3], refs[-2], refs[-1]
        begin = 0
        for stack_ref, count in zip(stack_refs, counts):
            held[begin : begin + count, :] = stack_ref[...]
            begin += count

        def source(slot, offset, count):
            start = pl.multiple_of(index_ref[slot] * frames_local + offset, HALO)
            return held[pl.ds(start, count), :]

        taken[0:HALO, :] = source(0, frames_local - HALO, HALO)
        taken[HALO : HALO + frames_local, :] = source(1, 0, frames_local)
        taken[HALO + frames_local : window, :] = source(2, 0, HALO)
        out[...] = dot32(taken[...], w_sub[...]).astype(jnp.bfloat16)

    return call(
        kernel,
        jax.ShapeDtypeStruct((window, model), jnp.bfloat16),
        (indices, *stacks, w_subsample),
        scratch=[
            pltpu.VMEM((sum(counts), depth), jnp.bfloat16),
            pltpu.VMEM((window, depth), jnp.bfloat16),
        ],
        scalars=1,
        flops=2 * window * depth * model,
    )


def finish_rows(inside, features, attended, w_rows, gain, taps, frames_local):
    parts = len(attended)
    model = features.shape[1]
    window = frames_local + 2 * HALO
    chunk = 2 * LANES
    offset = HALO - KERNEL // 2

    def kernel(inside_ref, *refs):
        feature_ref, a_refs, w_refs = refs[0], refs[1 : 1 + parts], refs[1 + parts : 1 + 2 * parts]
        gain_ref, tap_ref, out, held, mixed_rows = refs[1 + 2 * parts :]
        branch = jnp.zeros((window, model), jnp.float32)
        for a_ref, w_ref in zip(a_refs, w_refs):
            branch += dot32(a_ref[...], w_ref[...]).astype(jnp.bfloat16).astype(jnp.float32)
        mixed = (feature_ref[...].astype(jnp.float32) + branch).astype(jnp.bfloat16)
        mixed = mixed.astype(jnp.float32)
        mixed_rows[...] = mixed[HALO : HALO + frames_local]
        conv_in = (normalize(mixed) * gain_ref[...]).astype(jnp.bfloat16).astype(jnp.float32)
        held[HALO : HALO + frames_local, :] = conv_in[HALO : HALO + frames_local]
        before = inside_ref[0] > 0
        held[0:HALO, :] = jnp.where(before, conv_in[0:HALO], 0.0)
        after = inside_ref[1] > 0
        held[HALO + frames_local : window, :] = jnp.where(after, conv_in[HALO + frames_local :], 0.0)
        for lane in range(0, model, chunk):
            here = slice(lane, lane + chunk)
            total = jnp.zeros((frames_local, chunk), jnp.float32)
            tap_rows = tap_ref[:, here].astype(jnp.float32)
            for phase in range(8):
                taken = [tap for tap in range(KERNEL) if (tap + offset) % 8 == phase]
                reach = (taken[-1] + offset) // 8 * 8 + frames_local
                moved = held[pl.ds(phase, reach), here]
                for tap in taken:
                    begin = (tap + offset) // 8 * 8
                    total += moved[begin : begin + frames_local] * tap_rows[tap : tap + 1]
            silu = total / (1.0 + jnp.exp(-total))
            out[:, here] = (mixed_rows[:, here] + silu).astype(jnp.bfloat16)

    return call(
        kernel,
        jax.ShapeDtypeStruct((frames_local, model), jnp.bfloat16),
        (inside, features, *attended, *w_rows, gain, taps),
        scratch=[
            pltpu.VMEM((window, model), jnp.float32),
            pltpu.VMEM((frames_local, model), jnp.float32),
        ],
        scalars=1,
        flops=2 * window * model * model,
    )


def exchange(block, axis, bit):
    return lax.ppermute(block, axis, [(i, i ^ bit) for i in range(lax.axis_size(axis))])


def shifted(block, axis, distance):
    count = lax.axis_size(axis)
    route = [(i - distance, i) for i in range(count) if 0 <= i - distance < count]
    return lax.ppermute(block, axis, route)


def shards(
    waveform,
    segment_start,
    segment_end,
    w_subsample,
    w_attention,
    w_output,
    gain_convolution,
    w_depthwise,
):
    frames_local = waveform.shape[0] // (SUB * HOP)
    frames_shard = segment_start.shape[0]
    parts, shards_total = lax.axis_size("mp"), lax.axis_size("tm")
    time_index = lax.axis_index("tm")
    model_index = lax.axis_index("mp")
    bits = [1 << b for b in reversed(range((parts - 1).bit_length()))]

    ahead = -(-(NFFT - HOP) // LANES) * LANES
    next_samples = shifted(waveform[:ahead], ("tm", "mp"), -1)
    own_bounds = jnp.stack([segment_start, segment_end])
    bounds = jnp.concatenate(
        [
            shifted(own_bounds[:, frames_shard - HALO :], "tm", 1),
            own_bounds,
            shifted(own_bounds[:, :HALO], "tm", -1),
        ],
        axis=1,
    )
    stacked = log_mel_rows(
        waveform.reshape(-1, LANES), next_samples.reshape(-1, LANES), frames_local
    )

    reach = min((SEG_MAX + HALO - 2) // frames_shard + 1, shards_total - 1)
    whole = reach == shards_total - 1 and shards_total & (shards_total - 1) == 0
    column, places = [stacked], [(time_index, model_index)]
    if whole:
        for bit in range(1, shards_total):
            column.append(exchange(stacked, "tm", bit))
            places.append((time_index ^ bit, model_index))
    else:
        for distance in range(1, reach + 1):
            for step in (distance, -distance):
                column.append(shifted(stacked, "tm", step))
                places.append((time_index - step, model_index))
    column = jnp.concatenate(column)

    gathered = [column]
    for bit in bits:
        gathered += [exchange(block, "mp", bit) for block in gathered]
        places += [(tm, mp ^ bit) for tm, mp in places]

    w_rows = [w_output]
    for bit in bits:
        w_rows += [exchange(block, "mp", bit) for block in w_rows]

    half = len(gathered) // 2
    projected = [project_rows([block], w_subsample, w_attention) for block in gathered[:half]]
    projected.append(project_rows(gathered[half:], w_subsample, w_attention))
    queries, keys, values = zip(*projected)

    key_positions = jnp.concatenate(
        [
            tm * frames_shard + mp * frames_local + jnp.arange(frames_local, dtype=jnp.int32)
            for tm, mp in places
        ]
    )[None, :]

    def place(tm, mp):
        found = 0
        for slot, (slot_tm, slot_mp) in enumerate(places):
            found += jnp.where((slot_tm == tm) & (slot_mp == mp), slot, 0)
        return found

    indices = [place(time_index - 1, parts - 1)]
    indices += [place(time_index, mp) for mp in range(parts)]
    indices += [place(time_index + 1, 0)]
    indices += [model_index ^ bit for bit in range(parts)]
    indices = jnp.stack(indices).astype(jnp.int32)
    attended = attend(indices, bounds, key_positions, queries, keys, values, frames_local, parts)
    arrived = [attended[0]] + [exchange(attended[bit], "mp", bit) for bit in range(1, parts)]
    w_order = [0]
    for bit in bits:
        w_order += [other ^ bit for other in w_order]
    w_rows = [w_rows[w_order.index(bit)] for bit in range(parts)]

    block = time_index * parts + model_index
    around = [block - 1, block, block + 1]
    around = jnp.stack([place(b // parts, b % parts) for b in around]).astype(jnp.int32)
    features = window_features(around, gathered, w_subsample, frames_local)
    inside = jnp.stack([block > 0, block < shards_total * parts - 1]).astype(jnp.int32)
    return finish_rows(
        inside, features, arrived, w_rows, gain_convolution[None, :], w_depthwise, frames_local
    )


def solution(mesh):
    placed = (
        P(("groups", "tm", "mp")),
        P(("groups", "tm")),
        P(("groups", "tm")),
        P(),
        P(None, None, "mp"),
        P("mp", None),
        P(),
        P(),
    )
    return jax.shard_map(
        shards,
        mesh=mesh,
        in_specs=placed,
        out_specs=P(("groups", "tm", "mp"), None),
        check_vma=False,
    )
```

```python
import itertools
import math

import jax
import jax.numpy as jnp
import numpy as np
from jax import lax
from jax.experimental import pallas as pl
from jax.experimental.pallas import tpu as pltpu
from jax.sharding import PartitionSpec as P

HD = 64
NMEL = 128
NFFT = 400
HOP = 160
BINS = 256
SUB = 4
KERNEL = 31
SEG_MAX = 750
LANES = 128
HALO = 16
EXTRA = 8
TAIL_LINES = 3
HEAD_LINES = 2
DIGIT = 128
VMEM_MOST = 54
FRAME_ROWS = SUB * HOP // LANES
WIDE = -(-NFFT // LANES) * LANES


def split_high_low(table):
    high = table.astype(jnp.bfloat16)
    low = (table - high.astype(np.float32)).astype(jnp.bfloat16)
    return high, low


def fourier_table():
    sample_index = np.arange(NFFT)[:, None]
    bin_index = np.arange(BINS)[None, :]
    angle = (sample_index * bin_index % NFFT) * (2.0 * math.pi / NFFT)
    window = 0.5 - 0.5 * np.cos(np.arange(NFFT) * (2.0 * math.pi / NFFT))
    kept = bin_index <= NFFT // 2
    cosine = np.where(kept, np.cos(angle), 0.0) * window[:, None]
    sine = np.where(kept, -np.sin(angle), 0.0) * window[:, None]
    table = np.concatenate([cosine, sine], axis=1).astype(np.float32)
    return np.pad(table, ((0, WIDE - NFFT), (0, 0)))


def mel_bank():
    mel_top = 2595.0 * math.log10(1.0 + 8000.0 / 700.0)
    mel_points = np.arange(NMEL + 2) * (mel_top / (NMEL + 1))
    edges = 700.0 * (np.power(10.0, mel_points / 2595.0) - 1.0) * (NFFT / 16000.0)
    widths = np.maximum(edges[2:] - edges[1:-1], 1.0)
    bin_value = np.arange(BINS)[:, None]
    triangle = np.maximum(0.0, 1.0 - np.abs(bin_value - edges[None, 1:-1]) / widths[None, :])
    return np.where(bin_value <= NFFT // 2, triangle, 0.0).astype(np.float32)


def dot32(left, right):
    return jnp.dot(left, right, preferred_element_type=jnp.float32)


def dot_split(values, high_ref, low_ref):
    high = values.astype(jnp.bfloat16)
    low = (values - high.astype(jnp.float32)).astype(jnp.bfloat16)
    return dot32(high, high_ref[...]) + (dot32(low, high_ref[...]) + dot32(high, low_ref[...]))


def normalize(values):
    center = jnp.mean(values, axis=-1, keepdims=True)
    shifted = values - center
    spread = jnp.mean(jnp.square(shifted), axis=-1, keepdims=True)
    return shifted * lax.rsqrt(spread + 1e-05)


def call(kernel, out_shape, operands, scratch=(), flops=0, remote=0, vmem=16):
    specs = [pl.BlockSpec(memory_space=pltpu.VMEM)] * (len(operands) - remote)
    specs += [pl.BlockSpec(memory_space=pltpu.HBM)] * remote
    return pl.pallas_call(
        kernel,
        out_shape=out_shape,
        in_specs=specs,
        out_specs=jax.tree.map(lambda _: pl.BlockSpec(memory_space=pltpu.VMEM), out_shape),
        scratch_shapes=list(scratch),
        compiler_params=pltpu.CompilerParams(vmem_limit_bytes=vmem * 1024 * 1024),
        cost_estimate=pl.CostEstimate(flops=flops, bytes_accessed=1000000, transcendentals=0),
    )(*operands)


def spread_axes():
    return [axis for axis in ("groups", "tm") if lax.axis_size(axis) % 2 == 0]


def piece_number():
    number = 0
    for place_value, axis in enumerate(spread_axes()):
        number += lax.rem(lax.axis_index(axis), 2) << place_value
    return number


def fetch(after, arrays):
    count = len(arrays)

    def kernel(_, *refs):
        sources, outs, sems = refs[:count], refs[count:-1], refs[-1]
        copies = [
            pltpu.make_async_copy(source, target, sems.at[slot])
            for slot, (source, target) in enumerate(zip(sources, outs))
        ]
        for copy in copies:
            copy.start()
        for copy in copies:
            copy.wait()

    return call(
        kernel,
        [jax.ShapeDtypeStruct(array.shape, array.dtype) for array in arrays],
        (after, *arrays),
        scratch=[pltpu.SemaphoreType.DMA((count,))],
        remote=count,
    )


def padded_row(row):
    return jnp.concatenate([row, jnp.zeros((1, SUB * NMEL - row.shape[1]), row.dtype)], axis=1)


def log_mel(windows, th, tl, bh, bl):
    spectrum = dot_split(windows, th, tl)
    power = jnp.square(spectrum[:, :BINS]) + jnp.square(spectrum[:, BINS:])
    return jnp.log(dot_split(power, bh, bl) + 1e-06)


def log_mel_rows(starts, ends, samples, w_output, tables, frames_local):
    rows = frames_local * FRAME_ROWS
    frames_shard = starts.shape[1]
    pieces = 1 << len(spread_axes())
    piece_rows = w_output.shape[0] // pieces

    def kernel(start_ref, end_ref, wave, weight, *refs):
        sources, (out, out_piece), (held, th, tl, bh, bl, sems) = refs[:4], refs[4:6], refs[6:]
        copies = [pltpu.make_async_copy(wave, held.at[pl.ds(0, rows)], sems.at[0])]
        for slot, (source, target) in enumerate(zip(sources, (th, tl, bh, bl))):
            copies.append(pltpu.make_async_copy(source, target, sems.at[1 + slot]))
        begin = pl.multiple_of(piece_number() * piece_rows, HALO)
        copies.append(
            pltpu.make_async_copy(weight.at[pl.ds(begin, piece_rows)], out_piece, sems.at[5])
        )
        for copy in copies:
            copy.start()
        held[rows : rows + 8, :] = jnp.zeros((8, LANES), jnp.float32)
        copies[0].wait()
        lines = [held[pl.ds(j, frames_local, stride=FRAME_ROWS), :] for j in range(FRAME_ROWS + 2)]
        windows = []
        for sub in range(SUB):
            line, lane = divmod(sub * HOP, LANES)
            taken = jnp.concatenate(lines[line : line + WIDE // LANES], axis=1)
            windows.append(pltpu.roll(taken, WIDE - lane, axis=1) if lane else taken)
        extras = []
        for taken in (range(rows - TAIL_LINES, rows), range(HEAD_LINES)):
            line = jnp.concatenate([held[row : row + 1, :] for row in taken], axis=1)
            high = line.astype(jnp.bfloat16).astype(jnp.float32)
            extras += [padded_row(high), padded_row(line - high)]
        for ref in (start_ref, end_ref):
            edge = jnp.concatenate([ref[:, :HALO], ref[:, frames_shard - HALO :]], axis=1)
            high = edge // DIGIT
            low = edge - high * DIGIT
            extras += [padded_row(digit.astype(jnp.float32)) for digit in (high, low)]
        out[0, frames_local:, :] = jnp.concatenate(extras, axis=0).astype(jnp.bfloat16)
        for copy in copies[1:]:
            copy.wait()
        mel = log_mel(jnp.concatenate(windows, axis=0), th, tl, bh, bl)
        for sub in range(SUB):
            out[0, 0:frames_local, sub * NMEL : (sub + 1) * NMEL] = mel[
                sub * frames_local : (sub + 1) * frames_local
            ].astype(jnp.bfloat16)

    return call(
        kernel,
        (
            jax.ShapeDtypeStruct((1, frames_local + EXTRA, SUB * NMEL), jnp.bfloat16),
            jax.ShapeDtypeStruct((piece_rows, w_output.shape[1]), w_output.dtype),
        ),
        (starts, ends, samples, w_output, *tables),
        scratch=[pltpu.VMEM((rows + 8, LANES), jnp.float32)]
        + [pltpu.VMEM(table.shape, jnp.bfloat16) for table in tables]
        + [pltpu.SemaphoreType.DMA((6,))],
        remote=6,
        vmem=VMEM_MOST,
        flops=6 * frames_local * SUB * WIDE * 2 * BINS,
    )


def boundary_rows(places, starts, ends, stacks, tables, frames_local):
    counts = [stack.shape[0] for stack in stacks]
    slots = len(places)
    rows = -(-slots // HALO) * HALO
    frames_shard = starts.shape[1]
    parts = lax.axis_size("mp")
    final = lax.axis_size("tm") * parts - 1

    def kernel(start_ref, end_ref, *refs):
        stack_refs, refs = refs[: len(counts)], refs[len(counts) :]
        (th, tl, bh, bl), (out, bounds, tails, heads, nexts, edges) = refs[:4], refs[4:]
        time_index, model_index = lax.axis_index("tm"), lax.axis_index("mp")
        tails[...] = jnp.zeros_like(tails)
        nexts[...] = jnp.zeros_like(nexts)
        slot = 0
        for stack_ref, count in zip(stack_refs, counts):
            for block in range(count):
                kept = stack_ref[block, frames_local:, :].astype(jnp.float32)
                here = slice(slot, slot + 1)
                tails[here, :] = (kept[0:1] + kept[1:2])[:, : TAIL_LINES * LANES]
                heads[here, :] = (kept[2:3] + kept[3:4])[:, : HEAD_LINES * LANES]
                for line in range(2):
                    edge = kept[4 + 2 * line : 5 + 2 * line] * DIGIT + kept[5 + 2 * line : 6 + 2 * line]
                    edges[line, here, :] = edge[:, :LANES]
                slot += 1
        for slot, (slot_tm, slot_mp) in enumerate(places):
            following = slot_tm(time_index) * parts + (model_index ^ slot_mp) + 1
            found = slot_of(places, following // parts, lax.rem(following, parts))
            taken = heads[pl.ds(found, 1), :]
            nexts[slot : slot + 1, :] = jnp.where(following > final, 0.0, taken)
        line = jnp.concatenate([tails[...], nexts[...]], axis=1)
        windows = []
        for sub in range(SUB - 2, SUB):
            skip, lane = divmod(sub * HOP - (FRAME_ROWS - TAIL_LINES) * LANES, LANES)
            windows.append(
                pltpu.roll(line[:, skip * LANES : skip * LANES + WIDE], WIDE - lane, axis=1)
            )
        mel = log_mel(jnp.concatenate(windows, axis=0), th, tl, bh, bl).astype(jnp.bfloat16)
        for number in range(2):
            lane = number * NMEL
            out[:, lane : lane + NMEL] = mel[number * rows : (number + 1) * rows]
        left = slot_of(places, time_index - 1, model_index)
        right = slot_of(places, time_index + 1, model_index)
        for number, ref in enumerate((start_ref, end_ref)):
            bounds[number : number + 1, :] = jnp.concatenate(
                [
                    edges[number, pl.ds(left, 1), :][:, HALO : 2 * HALO],
                    ref[...].astype(jnp.float32),
                    edges[number, pl.ds(right, 1), :][:, 0:HALO],
                ],
                axis=1,
            )

    return call(
        kernel,
        (
            jax.ShapeDtypeStruct((rows, 2 * NMEL), jnp.bfloat16),
            jax.ShapeDtypeStruct((2, frames_shard + 2 * HALO), jnp.float32),
        ),
        (starts, ends, *stacks, *tables),
        scratch=[
            pltpu.VMEM((rows, TAIL_LINES * LANES), jnp.float32),
            pltpu.VMEM((rows, HEAD_LINES * LANES), jnp.float32),
            pltpu.VMEM((rows, HEAD_LINES * LANES), jnp.float32),
            pltpu.VMEM((2, rows, LANES), jnp.float32),
        ],
        flops=12 * rows * WIDE * 2 * BINS,
    )


def last_rows(stack_refs, counts, frames_local, fixed, rows):
    lasts = []
    for stack_ref, count in zip(stack_refs, counts):
        for block in range(count):
            kept = stack_ref[block, frames_local - HALO : frames_local, 0 : 2 * NMEL]
            lasts.append(kept.astype(jnp.float32)[HALO - 1 : HALO])
    if len(lasts) < rows:
        lasts.append(jnp.zeros((rows - len(lasts), 2 * NMEL), jnp.float32))
    return jnp.concatenate([jnp.concatenate(lasts, axis=0).astype(jnp.bfloat16), fixed], axis=1)


def patch(held, fixed, slots, frames_local):
    fixed = fixed.astype(jnp.float32)
    for slot in range(slots):
        here = slice((slot + 1) * frames_local - HALO, (slot + 1) * frames_local)
        kept = held[here, :].astype(jnp.float32)
        last = lax.broadcasted_iota(jnp.int32, kept.shape, 0) == HALO - 1
        held[here, :] = jnp.where(last, fixed[slot : slot + 1, :], kept).astype(held.dtype)


def assemble(parts):
    counts = [part.shape[0] for part in parts]

    def kernel(*refs):
        begin = 0
        for ref, count in zip(refs, counts):
            refs[-1][begin : begin + count] = ref[...]
            begin += count

    shape = jax.ShapeDtypeStruct((sum(counts), *parts[0].shape[1:]), parts[0].dtype)
    return call(kernel, shape, parts)


def project_rows(stack, w_subsample, w_attention, frames_local, every=(), fixed=None):
    count = stack.shape[0]
    rows, width = count * frames_local, w_attention.shape[2]
    model = w_subsample.shape[1]
    counts = [block.shape[0] for block in every]
    sizes = [rows] if fixed is None else [rows, fixed.shape[0]]

    def kernel(stack_ref, w_sub, w_att, *refs):
        stack_rows = [stack_ref[block, 0:frames_local, :] for block in range(count)]
        if fixed is not None:
            every_refs, fixed_ref, refs = refs[: len(every)], refs[len(every)], refs[len(every) + 1 :]
            stack_rows.append(
                last_rows(every_refs, counts, frames_local, fixed_ref[...], sizes[1])
            )
        features = dot32(jnp.concatenate(stack_rows, axis=0), w_sub[...]).astype(jnp.bfloat16)
        normed = normalize(features.astype(jnp.float32)).astype(jnp.bfloat16)
        for part in range(3):
            projected = dot32(normed, w_att[part]).astype(jnp.bfloat16)
            begin = 0
            for number, size in enumerate(sizes):
                refs[3 * number + part][...] = projected[begin : begin + size]
                begin += size

    return call(
        kernel,
        [jax.ShapeDtypeStruct((size, width), jnp.bfloat16) for size in sizes for _ in range(3)],
        (stack, w_subsample, w_attention) + (() if fixed is None else (*every, fixed)),
        flops=2 * sum(sizes) * model * (w_subsample.shape[0] + 3 * width),
    )


def slot_of(places, tm, mp):
    found = jnp.int32(0)
    for slot, (slot_tm, slot_mp) in enumerate(places):
        here = (slot_tm(lax.axis_index("tm")) == tm) & (lax.axis_index("mp") ^ slot_mp == mp)
        found = jnp.where(here, slot, found)
    return found


def attend(places, bounds, queries, keys, values, fixed, frames_local):
    counts = [q.shape[0] for q in queries]
    rows, width = sum(counts), queries[0].shape[1]
    groups = len(counts)
    parts = lax.axis_size("mp")
    frames_shard = frames_local * parts
    extended = frames_shard + 2 * HALO
    window = frames_local + 2 * HALO

    def kernel(*refs):
        bound_ref, refs = refs[0], refs[1:]
        sources, refs = refs[: 3 * groups], refs[3 * groups :]
        fixed_refs, refs = refs[:3], refs[3:]
        outs, (q_all, k_all, v_all, q_rows, result, bias) = refs[:parts], refs[parts:]
        for part, held in enumerate((q_all, k_all, v_all)):
            begin = 0
            for source, count in zip(sources[groups * part : groups * (part + 1)], counts):
                held[begin : begin + count, :] = source[...]
                begin += count
            patch(held, fixed_refs[part][...], len(places), frames_local)
        time_index, model_index = lax.axis_index("tm"), lax.axis_index("mp")

        def source(tm, mp, offset, count):
            start = pl.multiple_of(slot_of(places, tm, mp) * frames_local + offset, HALO)
            return q_all[pl.ds(start, count), :]

        q_rows[0:HALO, :] = source(time_index - 1, parts - 1, frames_local - HALO, HALO)
        for part in range(parts):
            begin = HALO + part * frames_local
            q_rows[begin : begin + frames_local, :] = source(time_index, part, 0, frames_local)
        q_rows[HALO + frames_shard : extended, :] = source(time_index + 1, 0, 0, HALO)
        first, last = (
            jnp.transpose(
                jnp.broadcast_to(bound_ref[line : line + 1, :], (LANES, extended))
            )
            for line in range(2)
        )
        lanes = lax.broadcasted_iota(jnp.int32, (1, LANES), 1)
        for begin in range(0, rows, LANES):
            at = jnp.zeros((1, LANES), jnp.int32)
            for slot in range(begin // frames_local, -(-(begin + LANES) // frames_local)):
                if slot < len(places):
                    slot_tm, slot_mp = places[slot]
                    base = slot_tm(time_index) * frames_shard
                    base += (model_index ^ slot_mp) * frames_local - slot * frames_local + begin
                    at = jnp.where(lanes >= slot * frames_local - begin, lanes + base, at)
            at = at.astype(jnp.float32)
            allowed = (at >= first) & (at < last)
            bias[:, begin : begin + LANES] = jnp.where(allowed, 0.0, -1e30)
        for lane in range(0, width, LANES):
            span = min(LANES, width - lane)
            q_pair = q_rows[:, lane : lane + span]
            k_pair = k_all[:, lane : lane + span]
            v_pair = v_all[:, lane : lane + span]
            head_of = lax.broadcasted_iota(jnp.int32, (extended, span), 1) // HD
            merged = jnp.zeros((extended, span), jnp.float32)
            for head in range(span // HD):
                mine = head_of == head
                q_head = jnp.where(mine, q_pair, jnp.zeros_like(q_pair)) * jnp.bfloat16(
                    1.0 / math.sqrt(HD)
                )
                scores = lax.dot_general(
                    q_head, k_pair, (((1,), (1,)), ((), ())), preferred_element_type=jnp.float32
                )
                scores = scores + bias[...]
                weights = jnp.exp(scores - jnp.max(scores, axis=1, keepdims=True))
                total = jnp.sum(weights, axis=1, keepdims=True)
                rounded = weights.astype(jnp.bfloat16)
                numerator = dot32(rounded, v_pair)
                merged = jnp.where(mine, numerator / total, merged)
            result[:, lane : lane + span] = merged.astype(jnp.bfloat16)
        for part in range(parts):
            start = pl.multiple_of((model_index ^ part) * frames_local, HALO)
            outs[part][...] = result[pl.ds(start, window), :]

    return call(
        kernel,
        [jax.ShapeDtypeStruct((window, width), jnp.bfloat16)] * parts,
        (bounds, *queries, *keys, *values, *fixed),
        scratch=[
            pltpu.VMEM((rows, width), jnp.bfloat16),
            pltpu.VMEM((rows, width), jnp.bfloat16),
            pltpu.VMEM((rows, width), jnp.bfloat16),
            pltpu.VMEM((extended, width), jnp.bfloat16),
            pltpu.VMEM((extended, width), jnp.bfloat16),
            pltpu.VMEM((extended, rows), jnp.float32),
        ],
        flops=4 * extended * rows * width * 4,
        vmem=16 + extended * rows * 20 // 1024 // 1024,
    )


def window_features(after, places, stacks, fixed, pieces, w_subsample, frames_local):
    counts = [stack.shape[0] for stack in stacks]
    depth, model = w_subsample.shape
    window = frames_local + 2 * HALO
    piece_slots = len(pieces[0])
    piece_rows = pieces[0][0].shape[0]
    flat = [piece for shard in pieces for piece in shard]
    slots = len(places)

    def kernel(_, *refs):
        stack_refs, refs = refs[: len(counts)], refs[len(counts) :]
        piece_refs, refs = refs[: len(flat)], refs[len(flat) :]
        fixed_ref, w_sub, out, *whole, held, taken = refs
        for number, piece_ref in enumerate(piece_refs):
            shard, slot = divmod(number, piece_slots)
            start = pl.multiple_of((piece_number() ^ slot) * piece_rows, HALO)
            whole[shard][pl.ds(start, piece_rows), :] = piece_ref[...]
        begin = 0
        for stack_ref, count in zip(stack_refs, counts):
            for block in range(count):
                held[begin : begin + frames_local, :] = stack_ref[block, 0:frames_local, :]
                begin += frames_local
        rows = last_rows(stack_refs, counts, frames_local, fixed_ref[...], fixed.shape[0])
        patch(held, rows, slots, frames_local)
        parts = lax.axis_size("mp")
        block = lax.axis_index("tm") * parts + lax.axis_index("mp") + parts

        def source(number, offset, count):
            slot = slot_of(places, number // parts - 1, lax.rem(number, parts))
            start = pl.multiple_of(slot * frames_local + offset, HALO)
            return held[pl.ds(start, count), :]

        taken[0:HALO, :] = source(block - 1, frames_local - HALO, HALO)
        taken[HALO : HALO + frames_local, :] = source(block, 0, frames_local)
        taken[HALO + frames_local : window, :] = source(block + 1, 0, HALO)
        out[...] = dot32(taken[...], w_sub[...]).astype(jnp.bfloat16)

    return call(
        kernel,
        [jax.ShapeDtypeStruct((window, model), jnp.bfloat16)]
        + [jax.ShapeDtypeStruct((piece_slots * piece_rows, model), jnp.bfloat16)] * len(pieces),
        (after, *stacks, *flat, fixed, w_subsample),
        scratch=[
            pltpu.VMEM((slots * frames_local, depth), jnp.bfloat16),
            pltpu.VMEM((window, depth), jnp.bfloat16),
        ],
        flops=2 * window * depth * model,
    )


def finish_rows(features, attended, w_rows, gain, taps, frames_local):
    parts = len(attended)
    model = features.shape[1]
    window = frames_local + 2 * HALO
    chunk = 2 * LANES
    offset = HALO - KERNEL // 2

    def kernel(*refs):
        feature_ref, a_refs, w_refs = refs[0], refs[1 : 1 + parts], refs[1 + parts : 1 + 2 * parts]
        gain_ref, tap_ref, out, held, mixed_rows = refs[1 + 2 * parts :]
        branch = jnp.zeros((window, model), jnp.float32)
        for a_ref, w_ref in zip(a_refs, w_refs):
            branch += dot32(a_ref[...], w_ref[...]).astype(jnp.bfloat16).astype(jnp.float32)
        mixed = (feature_ref[...].astype(jnp.float32) + branch).astype(jnp.bfloat16)
        mixed = mixed.astype(jnp.float32)
        mixed_rows[...] = mixed[HALO : HALO + frames_local]
        conv_in = (normalize(mixed) * gain_ref[...]).astype(jnp.bfloat16).astype(jnp.float32)
        held[HALO : HALO + frames_local, :] = conv_in[HALO : HALO + frames_local]
        block = lax.axis_index("tm") * parts + lax.axis_index("mp")
        before = block > 0
        held[0:HALO, :] = jnp.where(before, conv_in[0:HALO], 0.0)
        after = block < lax.axis_size("tm") * parts - 1
        held[HALO + frames_local : window, :] = jnp.where(after, conv_in[HALO + frames_local :], 0.0)
        for lane in range(0, model, chunk):
            here = slice(lane, lane + chunk)
            total = jnp.zeros((frames_local, chunk), jnp.float32)
            tap_rows = tap_ref[:, here].astype(jnp.float32)
            for phase in range(8):
                taken = [tap for tap in range(KERNEL) if (tap + offset) % 8 == phase]
                reach = (taken[-1] + offset) // 8 * 8 + frames_local
                moved = held[pl.ds(phase, reach), here]
                for tap in taken:
                    begin = (tap + offset) // 8 * 8
                    total += moved[begin : begin + frames_local] * tap_rows[tap : tap + 1]
            silu = total / (1.0 + jnp.exp(-total))
            out[:, here] = (mixed_rows[:, here] + silu).astype(jnp.bfloat16)

    return call(
        kernel,
        jax.ShapeDtypeStruct((frames_local, model), jnp.bfloat16),
        (features, *attended, *w_rows, gain, taps),
        scratch=[
            pltpu.VMEM((window, model), jnp.float32),
            pltpu.VMEM((frames_local, model), jnp.float32),
        ],
        flops=2 * window * model * model,
    )


def exchange(block, axis, bit):
    return lax.ppermute(block, axis, [(i, i ^ bit) for i in range(lax.axis_size(axis))])


def spread_piece(piece):
    axes = spread_axes()
    sizes = [lax.axis_size(axis) for axis in axes]
    pieces = [piece]
    for slot in range(1, 1 << len(axes)):
        route = []
        for source in itertools.product(*(range(size) for size in sizes)):
            target = [place ^ (slot >> number & 1) for number, place in enumerate(source)]
            route.append(tuple(np.ravel_multi_index(at, sizes).item() for at in (source, target)))
        pieces.append(lax.ppermute(piece, tuple(axes), route))
    return pieces


def shifted(block, axis, distance):
    count = lax.axis_size(axis)
    route = [(i - distance, i) for i in range(count) if 0 <= i - distance < count]
    return lax.ppermute(block, axis, route)


def shards(
    waveform,
    segment_start,
    segment_end,
    w_subsample,
    w_attention,
    w_output,
    gain_convolution,
    w_depthwise,
):
    frames_local = waveform.shape[0] // (SUB * HOP)
    frames_shard = segment_start.shape[0]
    parts, shards_total = lax.axis_size("mp"), lax.axis_size("tm")
    bits = [1 << b for b in reversed(range((parts - 1).bit_length()))]

    samples = waveform.reshape(-1, LANES)
    starts, ends = segment_start[None, :], segment_end[None, :]
    tables = (*split_high_low(fourier_table()), *split_high_low(mel_bank()))
    stacked, own_piece = log_mel_rows(starts, ends, samples, w_output, tables, frames_local)
    w_subsample, w_attention, *tables = fetch(stacked, (w_subsample, w_attention, *tables))

    received = [own_piece]
    for bit in bits[:-1]:
        received += [exchange(piece, "mp", bit) for piece in received]
    received = [spread_piece(piece) for piece in received[1:]]
    w_near = exchange(w_output, "mp", bits[-1])

    reach = min((SEG_MAX + HALO - 2) // frames_shard + 1, shards_total - 1)
    whole = reach == shards_total - 1 and shards_total & (shards_total - 1) == 0
    if whole:
        moves = [lambda tm, bit=bit: tm ^ bit for bit in range(1, shards_total)]
        column = [exchange(stacked, "tm", bit) for bit in range(1, shards_total)]
    else:
        steps = [sign * d for d in range(1, reach + 1) for sign in (1, -1)]
        moves = [lambda tm, step=step: tm - step for step in steps]
        column = [shifted(stacked, "tm", step) for step in steps]
    early = [(stacked, [(lambda tm: tm, 0)])]
    late = [(assemble(column), [(move, 0) for move in moves])]

    def across(blocks, bit):
        return [
            (exchange(block, "mp", bit), [(move, mp ^ bit) for move, mp in held])
            for block, held in blocks
        ]

    for bit in bits[:-1]:
        early, late = early + across(early, bit), late + across(late, bit)
    ready = early + late[:1]
    joined = (assemble([block for block, _ in ready]), sum([held for _, held in ready], []))
    groups = [joined] + across([joined], bits[-1]) + late[1:] + across(late[1:], bits[-1])
    stacks, held = zip(*groups)
    places = sum(held, [])
    projected = [
        project_rows(block, w_subsample, w_attention, frames_local) for block in stacks[:-1]
    ]
    fixed, bounds = boundary_rows(places, starts, ends, stacks, tables, frames_local)
    *outs, fixed_query, fixed_key, fixed_value = project_rows(
        stacks[-1], w_subsample, w_attention, frames_local, stacks, fixed
    )
    queries, keys, values = zip(*projected, outs)
    fixed_rows = (fixed_query, fixed_key, fixed_value)

    attended = attend(places, bounds, queries, keys, values, fixed_rows, frames_local)
    arrived = [attended[0]] + [exchange(attended[bit], "mp", bit) for bit in range(1, parts)]
    features, *far = window_features(
        attended[0], places, stacks, fixed, received, w_subsample, frames_local
    )
    w_rows = [w_output, *far, w_near, *(exchange(rows, "mp", bits[-1]) for rows in far)]
    w_order = [0]
    for bit in bits:
        w_order += [other ^ bit for other in w_order]
    w_rows = [w_rows[w_order.index(bit)] for bit in range(parts)]
    return finish_rows(
        features, arrived, w_rows, gain_convolution[None, :], w_depthwise, frames_local
    )


def solution(mesh):
    placed = (
        P(("groups", "tm", "mp")),
        P(("groups", "tm")),
        P(("groups", "tm")),
        P(),
        P(None, None, "mp"),
        P("mp", None),
        P(),
        P(),
    )
    return jax.shard_map(
        shards,
        mesh=mesh,
        in_specs=placed,
        out_specs=P(("groups", "tm", "mp"), None),
        check_vma=False,
    )
```

```python
import math

import jax
import jax.numpy as jnp
import ml_dtypes
import numpy as np
from jax import lax
from jax.experimental import pallas as pl
from jax.experimental.pallas import tpu as pltpu
from jax.sharding import PartitionSpec as P

HD = 64
NMEL = 128
NFFT = 400
HOP = 160
BINS = 256
SUB = 4
KERNEL = 31
SEG_MAX = 750
LANES = 128
HALO = 16
EXTRA = 8
FLOPS_PER_MICRO = 1000000000
TAIL_LINES = 3
HEAD_LINES = 2
DIGIT = 128
FRAME_ROWS = SUB * HOP // LANES
WIDE = -(-NFFT // LANES) * LANES


def split_high_low(table):
    high = table.astype(ml_dtypes.bfloat16)
    low = (table - high.astype(np.float32)).astype(ml_dtypes.bfloat16)
    return high, low


def fourier_table():
    sample_index = np.arange(NFFT)[:, None]
    bin_index = np.arange(BINS)[None, :]
    angle = (sample_index * bin_index % NFFT) * (2.0 * math.pi / NFFT)
    window = 0.5 - 0.5 * np.cos(np.arange(NFFT) * (2.0 * math.pi / NFFT))
    kept = bin_index <= NFFT // 2
    cosine = np.where(kept, np.cos(angle), 0.0) * window[:, None]
    sine = np.where(kept, -np.sin(angle), 0.0) * window[:, None]
    table = np.concatenate([cosine, sine], axis=1).astype(np.float32)
    return np.pad(table, ((0, WIDE - NFFT), (0, 0)))


def mel_bank():
    mel_top = 2595.0 * math.log10(1.0 + 8000.0 / 700.0)
    mel_points = np.arange(NMEL + 2) * (mel_top / (NMEL + 1))
    edges = 700.0 * (np.power(10.0, mel_points / 2595.0) - 1.0) * (NFFT / 16000.0)
    widths = np.maximum(edges[2:] - edges[1:-1], 1.0)
    bin_value = np.arange(BINS)[:, None]
    triangle = np.maximum(0.0, 1.0 - np.abs(bin_value - edges[None, 1:-1]) / widths[None, :])
    return np.where(bin_value <= NFFT // 2, triangle, 0.0).astype(np.float32)


def front_tables():
    high, low = split_high_low(fourier_table())
    bank = np.concatenate(split_high_low(mel_bank()), axis=0)
    return np.concatenate([high, low, bank], axis=1)


def dot32(left, right):
    return jnp.dot(left, right, preferred_element_type=jnp.float32)


def dot_split(values, table_high, table_low):
    high = values.astype(jnp.bfloat16)
    low = (values - high.astype(jnp.float32)).astype(jnp.bfloat16)
    return dot32(high, table_high) + (dot32(low, table_high) + dot32(high, table_low))


def normalize(values):
    center = jnp.mean(values, axis=-1, keepdims=True)
    shifted = values - center
    spread = jnp.mean(jnp.square(shifted), axis=-1, keepdims=True)
    return shifted * lax.rsqrt(spread + 1e-05)


def call(kernel, out_shape, operands, scratch=(), micros=1.0, remote=0, vmem=16):
    specs = [pl.BlockSpec(memory_space=pltpu.VMEM)] * (len(operands) - remote)
    specs += [pl.BlockSpec(memory_space=pltpu.HBM)] * remote
    return pl.pallas_call(
        kernel,
        out_shape=out_shape,
        in_specs=specs,
        out_specs=jax.tree.map(lambda _: pl.BlockSpec(memory_space=pltpu.VMEM), out_shape),
        scratch_shapes=list(scratch),
        compiler_params=pltpu.CompilerParams(vmem_limit_bytes=vmem * 1024 * 1024),
        cost_estimate=pl.CostEstimate(
            flops=int(micros * FLOPS_PER_MICRO), bytes_accessed=1000000, transcendentals=0
        ),
    )(*operands)


def fetch(after, arrays):
    count = len(arrays)

    def kernel(_, *refs):
        sources, outs, sems = refs[:count], refs[count:-1], refs[-1]
        copies = [
            pltpu.make_async_copy(source, target, sems.at[slot])
            for slot, (source, target) in enumerate(zip(sources, outs))
        ]
        for copy in copies:
            copy.start()
        for copy in copies:
            copy.wait()

    return call(
        kernel,
        [jax.ShapeDtypeStruct(array.shape, array.dtype) for array in arrays],
        (after, *arrays),
        scratch=[pltpu.SemaphoreType.DMA((count,))],
        remote=count,
    )


def padded_row(row):
    return jnp.concatenate([row, jnp.zeros((1, SUB * NMEL - row.shape[1]), row.dtype)], axis=1)


def log_mel(windows, tables):
    wide, bank = 2 * BINS, slice(4 * BINS, 4 * BINS + NMEL)
    spectrum = dot_split(windows, tables[:, 0:wide], tables[:, wide : 2 * wide])
    power = jnp.square(spectrum[:, :BINS]) + jnp.square(spectrum[:, BINS:])
    return jnp.log(dot_split(power, tables[0:BINS, bank], tables[BINS:, bank]) + 1e-06)


def log_mel_rows(starts, ends, samples, tables, frames_local):
    rows = frames_local * FRAME_ROWS
    frames_shard = starts.shape[1]

    def kernel(start_ref, end_ref, wave, tables_ref, out, held):
        held[0:rows, :] = wave[...]
        held[rows : rows + 8, :] = jnp.zeros((8, LANES), jnp.float32)
        lines = [held[pl.ds(j, frames_local, stride=FRAME_ROWS), :] for j in range(FRAME_ROWS + 2)]
        windows = []
        for sub in range(SUB):
            line, lane = divmod(sub * HOP, LANES)
            taken = jnp.concatenate(lines[line : line + WIDE // LANES], axis=1)
            windows.append(pltpu.roll(taken, WIDE - lane, axis=1) if lane else taken)
        extras = []
        for taken in (range(rows - TAIL_LINES, rows), range(HEAD_LINES)):
            line = jnp.concatenate([held[row : row + 1, :] for row in taken], axis=1)
            high = line.astype(jnp.bfloat16).astype(jnp.float32)
            extras += [padded_row(high), padded_row(line - high)]
        for ref in (start_ref, end_ref):
            edge = jnp.concatenate([ref[:, :HALO], ref[:, frames_shard - HALO :]], axis=1)
            high = edge // DIGIT
            low = edge - high * DIGIT
            extras += [padded_row(digit.astype(jnp.float32)) for digit in (high, low)]
        out[0, frames_local:, :] = jnp.concatenate(extras, axis=0).astype(jnp.bfloat16)
        mel = log_mel(jnp.concatenate(windows, axis=0), tables_ref)
        for sub in range(SUB):
            out[0, 0:frames_local, sub * NMEL : (sub + 1) * NMEL] = mel[
                sub * frames_local : (sub + 1) * frames_local
            ].astype(jnp.bfloat16)

    return call(
        kernel,
        jax.ShapeDtypeStruct((1, frames_local + EXTRA, SUB * NMEL), jnp.bfloat16),
        (starts, ends, samples, tables),
        scratch=[pltpu.VMEM((rows + 8, LANES), jnp.float32)],
        micros=1.0,
    )


def boundary_rows(places, starts, ends, stacks, tables, frames_local):
    counts = [stack.shape[0] for stack in stacks]
    slots = len(places)
    rows = -(-slots // HALO) * HALO
    frames_shard = starts.shape[1]
    parts = lax.axis_size("mp")
    final = lax.axis_size("tm") * parts - 1

    def kernel(start_ref, end_ref, *refs):
        stack_refs, refs = refs[: len(counts)], refs[len(counts) :]
        tables_ref, out, bounds, tails, heads, nexts, edges = refs
        time_index, model_index = lax.axis_index("tm"), lax.axis_index("mp")
        tails[...] = jnp.zeros_like(tails)
        nexts[...] = jnp.zeros_like(nexts)
        slot = 0
        for stack_ref, count in zip(stack_refs, counts):
            for block in range(count):
                kept = stack_ref[block, frames_local:, :].astype(jnp.float32)
                here = slice(slot, slot + 1)
                tails[here, :] = (kept[0:1] + kept[1:2])[:, : TAIL_LINES * LANES]
                heads[here, :] = (kept[2:3] + kept[3:4])[:, : HEAD_LINES * LANES]
                for line in range(2):
                    edge = kept[4 + 2 * line : 5 + 2 * line] * DIGIT + kept[5 + 2 * line : 6 + 2 * line]
                    edges[line, here, :] = edge[:, :LANES]
                slot += 1
        for slot, (slot_tm, slot_mp) in enumerate(places):
            following = slot_tm(time_index) * parts + (model_index ^ slot_mp) + 1
            found = slot_of(places, following // parts, lax.rem(following, parts))
            taken = heads[pl.ds(found, 1), :]
            nexts[slot : slot + 1, :] = jnp.where(following > final, 0.0, taken)
        line = jnp.concatenate([tails[...], nexts[...]], axis=1)
        windows = []
        for sub in range(SUB - 2, SUB):
            skip, lane = divmod(sub * HOP - (FRAME_ROWS - TAIL_LINES) * LANES, LANES)
            windows.append(
                pltpu.roll(line[:, skip * LANES : skip * LANES + WIDE], WIDE - lane, axis=1)
            )
        mel = log_mel(jnp.concatenate(windows, axis=0), tables_ref).astype(jnp.bfloat16)
        for number in range(2):
            lane = number * NMEL
            out[:, lane : lane + NMEL] = mel[number * rows : (number + 1) * rows]
        left = slot_of(places, time_index - 1, model_index)
        right = slot_of(places, time_index + 1, model_index)
        for number, ref in enumerate((start_ref, end_ref)):
            bounds[number : number + 1, :] = jnp.concatenate(
                [
                    edges[number, pl.ds(left, 1), :][:, HALO : 2 * HALO],
                    ref[...].astype(jnp.float32),
                    edges[number, pl.ds(right, 1), :][:, 0:HALO],
                ],
                axis=1,
            )

    return call(
        kernel,
        (
            jax.ShapeDtypeStruct((rows, 2 * NMEL), jnp.bfloat16),
            jax.ShapeDtypeStruct((2, frames_shard + 2 * HALO), jnp.float32),
        ),
        (starts, ends, *stacks, tables),
        scratch=[
            pltpu.VMEM((rows, TAIL_LINES * LANES), jnp.float32),
            pltpu.VMEM((rows, HEAD_LINES * LANES), jnp.float32),
            pltpu.VMEM((rows, HEAD_LINES * LANES), jnp.float32),
            pltpu.VMEM((2, rows, LANES), jnp.float32),
        ],
        micros=0.9,
    )


def last_rows(stack_refs, counts, frames_local, fixed, rows):
    lasts = []
    for stack_ref, count in zip(stack_refs, counts):
        for block in range(count):
            kept = stack_ref[block, frames_local - HALO : frames_local, 0 : 2 * NMEL]
            lasts.append(kept.astype(jnp.float32)[HALO - 1 : HALO])
    if len(lasts) < rows:
        lasts.append(jnp.zeros((rows - len(lasts), 2 * NMEL), jnp.float32))
    return jnp.concatenate([jnp.concatenate(lasts, axis=0).astype(jnp.bfloat16), fixed], axis=1)


def patch(held, fixed, slots, frames_local):
    fixed = fixed.astype(jnp.float32)
    for slot in range(slots):
        here = slice((slot + 1) * frames_local - HALO, (slot + 1) * frames_local)
        kept = held[here, :].astype(jnp.float32)
        last = lax.broadcasted_iota(jnp.int32, kept.shape, 0) == HALO - 1
        held[here, :] = jnp.where(last, fixed[slot : slot + 1, :], kept).astype(held.dtype)


def assemble(parts, after=()):
    counts = [part.shape[0] for part in parts]

    def kernel(*refs):
        begin = 0
        for ref, count in zip(refs, counts):
            refs[-1][begin : begin + count] = ref[...]
            begin += count

    shape = jax.ShapeDtypeStruct((sum(counts), *parts[0].shape[1:]), parts[0].dtype)
    return call(kernel, shape, (*parts, *after))


def project_rows(stack, w_subsample, w_attention, frames_local, every=(), fixed=None):
    count = stack.shape[0]
    rows, width = count * frames_local, w_attention.shape[2]
    model = w_subsample.shape[1]
    counts = [block.shape[0] for block in every]
    sizes = [rows] if fixed is None else [rows, fixed.shape[0]]

    def kernel(stack_ref, w_sub, w_att, *refs):
        stack_rows = [stack_ref[block, 0:frames_local, :] for block in range(count)]
        if fixed is not None:
            every_refs, fixed_ref, refs = refs[: len(every)], refs[len(every)], refs[len(every) + 1 :]
            stack_rows.append(
                last_rows(every_refs, counts, frames_local, fixed_ref[...], sizes[1])
            )
        features = dot32(jnp.concatenate(stack_rows, axis=0), w_sub[...]).astype(jnp.bfloat16)
        normed = normalize(features.astype(jnp.float32)).astype(jnp.bfloat16)
        for part in range(3):
            projected = dot32(normed, w_att[part]).astype(jnp.bfloat16)
            begin = 0
            for number, size in enumerate(sizes):
                refs[3 * number + part][...] = projected[begin : begin + size]
                begin += size

    return call(
        kernel,
        [jax.ShapeDtypeStruct((size, width), jnp.bfloat16) for size in sizes for _ in range(3)],
        (stack, w_subsample, w_attention) + (() if fixed is None else (*every, fixed)),
        micros=0.5 + 0.007 * sum(sizes),
    )


def slot_of(places, tm, mp):
    found = jnp.int32(0)
    for slot, (slot_tm, slot_mp) in enumerate(places):
        here = (slot_tm(lax.axis_index("tm")) == tm) & (lax.axis_index("mp") ^ slot_mp == mp)
        found = jnp.where(here, slot, found)
    return found


def gather_rows(places, bounds, queries, keys, values, fixed, frames_local, window, outs):
    q_rows, k_all, v_all, q_all, first, last = outs
    parts = lax.axis_size("mp")
    frames_shard = frames_local * parts
    for held, sources, fixed_ref in zip((q_all, k_all, v_all), (queries, keys, values), fixed):
        begin = 0
        for source in sources:
            held[begin : begin + source.shape[0], :] = source[...]
            begin += source.shape[0]
        patch(held, fixed_ref[...], len(places), frames_local)
    time_index = lax.axis_index("tm")

    def source(tm, mp, offset, count):
        start = pl.multiple_of(slot_of(places, tm, mp) * frames_local + offset, HALO)
        return q_all[pl.ds(start, count), :]

    q_rows[0:HALO, :] = source(time_index - 1, parts - 1, frames_local - HALO, HALO)
    for part in range(parts):
        begin = HALO + part * frames_local
        q_rows[begin : begin + frames_local, :] = source(time_index, part, 0, frames_local)
    q_rows[HALO + frames_shard :, :] = source(time_index + 1, 0, 0, HALO)
    for line, ref in enumerate((first, last)):
        row = bounds[line : line + 1, :]
        ref[...] = jnp.transpose(jnp.broadcast_to(row, (LANES, row.shape[1])))


def attend_rows(places, begin, q_rows, k_all, v_all, first, last, frames_local, result, bias):
    count, width = result.shape
    rows = k_all.shape[0]
    time_index, model_index = lax.axis_index("tm"), lax.axis_index("mp")
    frames_shard = frames_local * lax.axis_size("mp")
    lows, highs = first[pl.ds(begin, count), :], last[pl.ds(begin, count), :]
    lanes = lax.broadcasted_iota(jnp.int32, (1, LANES), 1)
    for lane in range(0, rows, LANES):
        at = jnp.zeros((1, LANES), jnp.int32)
        for slot in range(lane // frames_local, -(-(lane + LANES) // frames_local)):
            if slot < len(places):
                slot_tm, slot_mp = places[slot]
                base = slot_tm(time_index) * frames_shard
                base += (model_index ^ slot_mp) * frames_local - slot * frames_local + lane
                at = jnp.where(lanes >= slot * frames_local - lane, lanes + base, at)
        at = at.astype(jnp.float32)
        bias[:, lane : lane + LANES] = jnp.where((at >= lows) & (at < highs), 0.0, -1e30)
    for lane in range(0, width, LANES):
        span = min(LANES, width - lane)
        q_pair = q_rows[pl.ds(begin, count), lane : lane + span]
        k_pair = k_all[:, lane : lane + span]
        v_pair = v_all[:, lane : lane + span]
        head_of = lax.broadcasted_iota(jnp.int32, (count, span), 1) // HD
        merged = jnp.zeros((count, span), jnp.float32)
        for head in range(span // HD):
            mine = head_of == head
            q_head = jnp.where(mine, q_pair, jnp.zeros_like(q_pair)) * jnp.bfloat16(
                1.0 / math.sqrt(HD)
            )
            scores = lax.dot_general(
                q_head, k_pair, (((1,), (1,)), ((), ())), preferred_element_type=jnp.float32
            )
            scores = scores + bias[...]
            weights = jnp.exp(scores - jnp.max(scores, axis=1, keepdims=True))
            total = jnp.sum(weights, axis=1, keepdims=True)
            numerator = dot32(weights.astype(jnp.bfloat16), v_pair)
            merged = jnp.where(mine, numerator / total, merged)
        result[:, lane : lane + span] = merged.astype(jnp.bfloat16)


def split_pair(model_index, result, mine, other, frames_local):
    window = mine.shape[0]
    place = lax.rem(model_index, 2) * frames_local
    mine[...] = result[pl.ds(pl.multiple_of(place, HALO), window), :]
    place = frames_local - place
    other[...] = result[pl.ds(pl.multiple_of(place, HALO), window), :]


def attend_far(places, far, bounds, queries, keys, values, fixed, frames_local):
    counts = [q.shape[0] for q in queries]
    rows, width = sum(counts), queries[0].shape[1]
    groups = len(counts)
    extended = frames_local * lax.axis_size("mp") + 2 * HALO
    window = frames_local + 2 * HALO
    pair = 2 * frames_local + 2 * HALO

    def kernel(bound_ref, *refs):
        sources, refs = refs[: 3 * groups], refs[3 * groups :]
        fixed_refs, refs = refs[:3], refs[3:]
        windows, refs = refs[: 2 * len(far)], refs[2 * len(far) :]
        q_rows, k_all, v_all, first, last, q_all, result, bias = refs
        gather_rows(
            places,
            bound_ref,
            sources[:groups],
            sources[groups : 2 * groups],
            sources[2 * groups :],
            fixed_refs,
            frames_local,
            window,
            (q_rows, k_all, v_all, q_all, first, last),
        )
        model_index = lax.axis_index("mp")
        for number, bit in enumerate(far):
            begin = pl.multiple_of((model_index ^ bit) // 2 * (2 * frames_local), HALO)
            attend_rows(
                places, begin, q_rows, k_all, v_all, first, last, frames_local, result, bias
            )
            split_pair(
                model_index, result, windows[2 * number], windows[2 * number + 1], frames_local
            )

    def shape(count, wide=width, dtype=jnp.bfloat16):
        return jax.ShapeDtypeStruct((count, wide), dtype)

    return call(
        kernel,
        [shape(window)] * (2 * len(far))
        + [shape(extended), shape(rows), shape(rows)]
        + [shape(extended, LANES, jnp.float32)] * 2,
        (bounds, *queries, *keys, *values, *fixed),
        scratch=[
            pltpu.VMEM((rows, width), jnp.bfloat16),
            pltpu.VMEM((pair, width), jnp.bfloat16),
            pltpu.VMEM((pair, rows), jnp.float32),
        ],
        micros=2.5 * len(far),
        vmem=16 + pair * rows * 20 // 1024 // 1024,
    )


def attend_near(places, after, q_rows, k_all, v_all, first, last, frames_local):
    rows, width = k_all.shape
    window = frames_local + 2 * HALO
    pair = 2 * frames_local + 2 * HALO

    def kernel(_, q_ref, k_ref, v_ref, first_ref, last_ref, mine, other, result, bias):
        model_index = lax.axis_index("mp")
        begin = pl.multiple_of(model_index // 2 * (2 * frames_local), HALO)
        attend_rows(
            places, begin, q_ref, k_ref, v_ref, first_ref, last_ref, frames_local, result, bias
        )
        split_pair(model_index, result, mine, other, frames_local)

    return call(
        kernel,
        [jax.ShapeDtypeStruct((window, width), jnp.bfloat16)] * 2,
        (after, q_rows, k_all, v_all, first, last),
        scratch=[
            pltpu.VMEM((pair, width), jnp.bfloat16),
            pltpu.VMEM((pair, rows), jnp.float32),
        ],
        micros=2.0,
        vmem=16 + pair * rows * 20 // 1024 // 1024,
    )


def far_branch(windows, w_rows):
    count = len(windows) // 2

    def kernel(*refs):
        windows, (w_own, w_near), outs = refs[: 2 * count], refs[2 * count :][:2], refs[-count:]
        for number in range(count):
            own, near = windows[2 * number : 2 * number + 2]
            share = dot32(own[...], w_own[...]) + dot32(near[...], w_near[...])
            outs[number][...] = share.astype(jnp.bfloat16)

    shape = jax.ShapeDtypeStruct((windows[0].shape[0], w_rows[0].shape[1]), jnp.bfloat16)
    return call(kernel, [shape] * count, (*windows, *w_rows), micros=0.9 * count)


def near_branch(places, windows, w_rows, stacks, fixed, w_subsample, frames_local):
    counts = [stack.shape[0] for stack in stacks]
    depth, model = w_subsample.shape
    window = frames_local + 2 * HALO
    slots = len(places)

    def kernel(own, near, w_own, w_near, *refs):
        stack_refs, (fixed_ref, w_sub, out, held, taken) = refs[: len(counts)], refs[len(counts) :]
        begin = 0
        for stack_ref, count in zip(stack_refs, counts):
            for block in range(count):
                held[begin : begin + frames_local, :] = stack_ref[block, 0:frames_local, :]
                begin += frames_local
        rows = last_rows(stack_refs, counts, frames_local, fixed_ref[...], fixed.shape[0])
        patch(held, rows, slots, frames_local)
        parts = lax.axis_size("mp")
        block = lax.axis_index("tm") * parts + lax.axis_index("mp") + parts

        def source(number, offset, count):
            slot = slot_of(places, number // parts - 1, lax.rem(number, parts))
            start = pl.multiple_of(slot * frames_local + offset, HALO)
            return held[pl.ds(start, count), :]

        taken[0:HALO, :] = source(block - 1, frames_local - HALO, HALO)
        taken[HALO : HALO + frames_local, :] = source(block, 0, frames_local)
        taken[HALO + frames_local : window, :] = source(block + 1, 0, HALO)
        features = dot32(taken[...], w_sub[...]).astype(jnp.bfloat16).astype(jnp.float32)
        share = dot32(own[...], w_own[...]) + dot32(near[...], w_near[...])
        out[...] = features + share

    return call(
        kernel,
        jax.ShapeDtypeStruct((window, model), jnp.float32),
        (*windows, *w_rows, *stacks, fixed, w_subsample),
        scratch=[
            pltpu.VMEM((slots * frames_local, depth), jnp.bfloat16),
            pltpu.VMEM((window, depth), jnp.bfloat16),
        ],
        micros=1.2,
    )


def finish_rows(base, shares, gain, taps, frames_local):
    count = len(shares)
    parts = lax.axis_size("mp")
    window, model = base.shape
    chunk = 2 * LANES
    offset = HALO - KERNEL // 2

    def kernel(base_ref, *refs):
        share_refs, (gain_ref, tap_ref, out, held, mixed_rows) = refs[:count], refs[count:]
        mixed = base_ref[...]
        for share_ref in share_refs:
            mixed += share_ref[...].astype(jnp.float32)
        mixed = mixed.astype(jnp.bfloat16).astype(jnp.float32)
        mixed_rows[...] = mixed[HALO : HALO + frames_local]
        conv_in = (normalize(mixed) * gain_ref[...]).astype(jnp.bfloat16).astype(jnp.float32)
        held[HALO : HALO + frames_local, :] = conv_in[HALO : HALO + frames_local]
        block = lax.axis_index("tm") * parts + lax.axis_index("mp")
        before = block > 0
        held[0:HALO, :] = jnp.where(before, conv_in[0:HALO], 0.0)
        after = block < lax.axis_size("tm") * parts - 1
        held[HALO + frames_local : window, :] = jnp.where(after, conv_in[HALO + frames_local :], 0.0)
        for lane in range(0, model, chunk):
            here = slice(lane, lane + chunk)
            total = jnp.zeros((frames_local, chunk), jnp.float32)
            tap_rows = tap_ref[:, here].astype(jnp.float32)
            for phase in range(8):
                taken = [tap for tap in range(KERNEL) if (tap + offset) % 8 == phase]
                reach = (taken[-1] + offset) // 8 * 8 + frames_local
                moved = held[pl.ds(phase, reach), here]
                for tap in taken:
                    begin = (tap + offset) // 8 * 8
                    total += moved[begin : begin + frames_local] * tap_rows[tap : tap + 1]
            silu = total / (1.0 + jnp.exp(-total))
            out[:, here] = (mixed_rows[:, here] + silu).astype(jnp.bfloat16)

    return call(
        kernel,
        jax.ShapeDtypeStruct((frames_local, model), jnp.bfloat16),
        (base, *shares, gain, taps),
        scratch=[
            pltpu.VMEM((window, model), jnp.float32),
            pltpu.VMEM((frames_local, model), jnp.float32),
        ],
        micros=2.8,
    )


def exchange(block, axis, bit):
    return lax.ppermute(block, axis, [(i, i ^ bit) for i in range(lax.axis_size(axis))])


def shifted(block, axis, distance):
    count = lax.axis_size(axis)
    route = [(i - distance, i) for i in range(count) if 0 <= i - distance < count]
    return lax.ppermute(block, axis, route)


def shards(
    waveform,
    segment_start,
    segment_end,
    w_subsample,
    w_attention,
    w_output,
    gain_convolution,
    w_depthwise,
):
    frames_local = waveform.shape[0] // (SUB * HOP)
    frames_shard = segment_start.shape[0]
    parts, shards_total = lax.axis_size("mp"), lax.axis_size("tm")
    bits = [1 << b for b in reversed(range((parts - 1).bit_length()))]

    samples = waveform.reshape(-1, LANES)
    starts, ends = segment_start[None, :], segment_end[None, :]
    tables = jnp.asarray(front_tables())
    stacked = log_mel_rows(starts, ends, samples, tables, frames_local)
    w_subsample, w_attention = fetch(stacked, (w_subsample, w_attention))

    w_near = exchange(w_output, "mp", bits[-1])

    reach = min((SEG_MAX + HALO - 2) // frames_shard + 1, shards_total - 1)
    whole = reach == shards_total - 1 and shards_total & (shards_total - 1) == 0
    if whole:
        moves = [lambda tm, bit=bit: tm ^ bit for bit in range(1, shards_total)]
        column = [exchange(stacked, "tm", bit) for bit in range(1, shards_total)]
    else:
        steps = [sign * d for d in range(1, reach + 1) for sign in (1, -1)]
        moves = [lambda tm, step=step: tm - step for step in steps]
        column = [shifted(stacked, "tm", step) for step in steps]
    early = [(stacked, [(lambda tm: tm, 0)])]
    late = [(assemble(column, (w_subsample,)), [(move, 0) for move in moves])]

    def across(blocks, bit):
        return [
            (exchange(block, "mp", bit), [(move, mp ^ bit) for move, mp in held])
            for block, held in blocks
        ]

    for bit in bits[:-1]:
        early, late = early + across(early, bit), late + across(late, bit)
    ready = early + late[:1]
    joined = (assemble([block for block, _ in ready]), sum([held for _, held in ready], []))
    groups = [joined] + across([joined], bits[-1]) + late[1:] + across(late[1:], bits[-1])
    stacks, held = zip(*groups)
    places = sum(held, [])
    projected = [
        project_rows(block, w_subsample, w_attention, frames_local) for block in stacks[:-1]
    ]
    fixed, bounds = boundary_rows(places, starts, ends, stacks, tables, frames_local)
    *outs, fixed_query, fixed_key, fixed_value = project_rows(
        stacks[-1], w_subsample, w_attention, frames_local, stacks, fixed
    )
    queries, keys, values = zip(*projected, outs)
    fixed_rows = (fixed_query, fixed_key, fixed_value)

    far = list(range(2, parts, 2))
    outs = attend_far(places, far, bounds, queries, keys, values, fixed_rows, frames_local)
    windows, shared = outs[: 2 * len(far)], outs[2 * len(far) :]
    windows = [
        exchange(block, "mp", 1) if number % 2 else block for number, block in enumerate(windows)
    ]
    w_rows = (w_output, w_near)
    shares = far_branch(windows, w_rows)
    mine, other = attend_near(places, shares[0], *shared, frames_local)
    shares = [exchange(share, "mp", bit) for share, bit in zip(shares, far)]
    base = near_branch(
        places, (mine, exchange(other, "mp", 1)), w_rows, stacks, fixed, w_subsample, frames_local
    )
    return finish_rows(base, shares, gain_convolution[None, :], w_depthwise, frames_local)


def solution(mesh):
    placed = (
        P(("groups", "tm", "mp")),
        P(("groups", "tm")),
        P(("groups", "tm")),
        P(),
        P(None, None, "mp"),
        P("mp", None),
        P(),
        P(),
    )
    return jax.shard_map(
        shards,
        mesh=mesh,
        in_specs=placed,
        out_specs=P(("groups", "tm", "mp"), None),
        check_vma=False,
    )
```

```python
import math

import jax
import jax.numpy as jnp
import ml_dtypes
import numpy as np
from jax import lax
from jax.experimental import pallas as pl
from jax.experimental.pallas import tpu as pltpu
from jax.sharding import PartitionSpec as P

HD = 64
NMEL = 128
NFFT = 400
HOP = 160
BINS = 256
SUB = 4
KERNEL = 31
SEG_MAX = 750
LANES = 128
HALO = 16
EXTRA = 8
FLOPS_PER_MICRO = 1000000000
TAIL_LINES = 3
HEAD_LINES = 2
DIGIT = 128
FRAME_ROWS = SUB * HOP // LANES
WIDE = -(-NFFT // LANES) * LANES


def split_high_low(table):
    high = table.astype(ml_dtypes.bfloat16)
    low = (table - high.astype(np.float32)).astype(ml_dtypes.bfloat16)
    return high, low


def fourier_table():
    sample_index = np.arange(NFFT)[:, None]
    bin_index = np.arange(BINS)[None, :]
    angle = (sample_index * bin_index % NFFT) * (2.0 * math.pi / NFFT)
    window = 0.5 - 0.5 * np.cos(np.arange(NFFT) * (2.0 * math.pi / NFFT))
    kept = bin_index <= NFFT // 2
    cosine = np.where(kept, np.cos(angle), 0.0) * window[:, None]
    sine = np.where(kept, -np.sin(angle), 0.0) * window[:, None]
    table = np.concatenate([cosine, sine], axis=1).astype(np.float32)
    return np.pad(table, ((0, WIDE - NFFT), (0, 0)))


def mel_bank():
    mel_top = 2595.0 * math.log10(1.0 + 8000.0 / 700.0)
    mel_points = np.arange(NMEL + 2) * (mel_top / (NMEL + 1))
    edges = 700.0 * (np.power(10.0, mel_points / 2595.0) - 1.0) * (NFFT / 16000.0)
    widths = np.maximum(edges[2:] - edges[1:-1], 1.0)
    bin_value = np.arange(BINS)[:, None]
    triangle = np.maximum(0.0, 1.0 - np.abs(bin_value - edges[None, 1:-1]) / widths[None, :])
    return np.where(bin_value <= NFFT // 2, triangle, 0.0).astype(np.float32)


def front_tables():
    high, low = split_high_low(fourier_table())
    bank = np.concatenate(split_high_low(mel_bank()), axis=0)
    return np.concatenate([high, low, bank], axis=1)


def dot32(left, right):
    return jnp.dot(left, right, preferred_element_type=jnp.float32)


def dot_split(values, table_high, table_low):
    high = values.astype(jnp.bfloat16)
    low = (values - high.astype(jnp.float32)).astype(jnp.bfloat16)
    return dot32(high, table_high) + (dot32(low, table_high) + dot32(high, table_low))


def normalize(values):
    center = jnp.mean(values, axis=-1, keepdims=True)
    shifted = values - center
    spread = jnp.mean(jnp.square(shifted), axis=-1, keepdims=True)
    return shifted * lax.rsqrt(spread + 1e-05)


def call(kernel, out_shape, operands, scratch=(), micros=1.0, remote=0, vmem=16):
    specs = [pl.BlockSpec(memory_space=pltpu.VMEM)] * (len(operands) - remote)
    specs += [pl.BlockSpec(memory_space=pltpu.HBM)] * remote
    return pl.pallas_call(
        kernel,
        out_shape=out_shape,
        in_specs=specs,
        out_specs=jax.tree.map(lambda _: pl.BlockSpec(memory_space=pltpu.VMEM), out_shape),
        scratch_shapes=list(scratch),
        compiler_params=pltpu.CompilerParams(vmem_limit_bytes=vmem * 1024 * 1024),
        cost_estimate=pl.CostEstimate(
            flops=int(micros * FLOPS_PER_MICRO), bytes_accessed=1000000, transcendentals=0
        ),
    )(*operands)


def fetch(after, w_subsample, w_attention):
    parts, _, width = w_attention.shape

    def kernel(_, w_sub, w_att, out_sub, out_att, sums, sems):
        copies = [
            pltpu.make_async_copy(w_att, out_att, sems.at[0]),
            pltpu.make_async_copy(w_sub, out_sub, sems.at[1]),
        ]
        for copy in copies:
            copy.start()
        for copy in copies:
            copy.wait()
        sums[...] = jnp.zeros_like(sums)
        for part in range(parts):
            columns = out_att[part].astype(jnp.float32)
            sums[part : part + 1, :] = jnp.sum(columns, axis=0, keepdims=True)

    return call(
        kernel,
        [jax.ShapeDtypeStruct(array.shape, array.dtype) for array in (w_subsample, w_attention)]
        + [jax.ShapeDtypeStruct((8, width), jnp.float32)],
        (after, w_subsample, w_attention),
        scratch=[pltpu.SemaphoreType.DMA((2,))],
        remote=2,
    )


def padded_row(row):
    return jnp.concatenate([row, jnp.zeros((1, SUB * NMEL - row.shape[1]), row.dtype)], axis=1)


def log_mel(windows, tables):
    wide, bank = 2 * BINS, slice(4 * BINS, 4 * BINS + NMEL)
    spectrum = dot_split(windows, tables[:, 0:wide], tables[:, wide : 2 * wide])
    power = jnp.square(spectrum[:, :BINS]) + jnp.square(spectrum[:, BINS:])
    return jnp.log(dot_split(power, tables[0:BINS, bank], tables[BINS:, bank]) + 1e-06)


def log_mel_rows(starts, ends, samples, tables, frames_local):
    rows = frames_local * FRAME_ROWS
    frames_shard = starts.shape[1]

    def kernel(start_ref, end_ref, wave, tables_ref, out, held):
        held[0:rows, :] = wave[...]
        held[rows : rows + 8, :] = jnp.zeros((8, LANES), jnp.float32)
        lines = [held[pl.ds(j, frames_local, stride=FRAME_ROWS), :] for j in range(FRAME_ROWS + 2)]
        windows = []
        for sub in range(SUB):
            line, lane = divmod(sub * HOP, LANES)
            taken = jnp.concatenate(lines[line : line + WIDE // LANES], axis=1)
            windows.append(pltpu.roll(taken, WIDE - lane, axis=1) if lane else taken)
        extras = []
        for taken in (range(rows - TAIL_LINES, rows), range(HEAD_LINES)):
            line = jnp.concatenate([held[row : row + 1, :] for row in taken], axis=1)
            high = line.astype(jnp.bfloat16).astype(jnp.float32)
            extras += [padded_row(high), padded_row(line - high)]
        for ref in (start_ref, end_ref):
            edge = jnp.concatenate([ref[:, :HALO], ref[:, frames_shard - HALO :]], axis=1)
            high = edge // DIGIT
            low = edge - high * DIGIT
            extras += [padded_row(digit.astype(jnp.float32)) for digit in (high, low)]
        out[0, frames_local:, :] = jnp.concatenate(extras, axis=0).astype(jnp.bfloat16)
        mel = log_mel(jnp.concatenate(windows, axis=0), tables_ref)
        for sub in range(SUB):
            out[0, 0:frames_local, sub * NMEL : (sub + 1) * NMEL] = mel[
                sub * frames_local : (sub + 1) * frames_local
            ].astype(jnp.bfloat16)

    return call(
        kernel,
        jax.ShapeDtypeStruct((1, frames_local + EXTRA, SUB * NMEL), jnp.bfloat16),
        (starts, ends, samples, tables),
        scratch=[pltpu.VMEM((rows + 8, LANES), jnp.float32)],
        micros=1.0,
    )


def boundary_rows(places, starts, ends, stacks, tables, frames_local):
    counts = [stack.shape[0] for stack in stacks]
    slots = len(places)
    rows = -(-slots // HALO) * HALO
    frames_shard = starts.shape[1]
    parts = lax.axis_size("mp")
    final = lax.axis_size("tm") * parts - 1

    def kernel(start_ref, end_ref, *refs):
        stack_refs, refs = refs[: len(counts)], refs[len(counts) :]
        tables_ref, out, bounds, tails, heads, nexts, edges = refs
        time_index, model_index = lax.axis_index("tm"), lax.axis_index("mp")
        tails[...] = jnp.zeros_like(tails)
        nexts[...] = jnp.zeros_like(nexts)
        slot = 0
        for stack_ref, count in zip(stack_refs, counts):
            for block in range(count):
                kept = stack_ref[block, frames_local:, :].astype(jnp.float32)
                here = slice(slot, slot + 1)
                tails[here, :] = (kept[0:1] + kept[1:2])[:, : TAIL_LINES * LANES]
                heads[here, :] = (kept[2:3] + kept[3:4])[:, : HEAD_LINES * LANES]
                for line in range(2):
                    edge = kept[4 + 2 * line : 5 + 2 * line] * DIGIT + kept[5 + 2 * line : 6 + 2 * line]
                    edges[line, here, :] = edge[:, :LANES]
                slot += 1
        for slot, (slot_tm, slot_mp) in enumerate(places):
            following = slot_tm(time_index) * parts + (model_index ^ slot_mp) + 1
            found = slot_of(places, following // parts, lax.rem(following, parts))
            taken = heads[pl.ds(found, 1), :]
            nexts[slot : slot + 1, :] = jnp.where(following > final, 0.0, taken)
        line = jnp.concatenate([tails[...], nexts[...]], axis=1)
        windows = []
        for sub in range(SUB - 2, SUB):
            skip, lane = divmod(sub * HOP - (FRAME_ROWS - TAIL_LINES) * LANES, LANES)
            windows.append(
                pltpu.roll(line[:, skip * LANES : skip * LANES + WIDE], WIDE - lane, axis=1)
            )
        mel = log_mel(jnp.concatenate(windows, axis=0), tables_ref).astype(jnp.bfloat16)
        for number in range(2):
            lane = number * NMEL
            out[:, lane : lane + NMEL] = mel[number * rows : (number + 1) * rows]
        left = slot_of(places, time_index - 1, model_index)
        right = slot_of(places, time_index + 1, model_index)
        for number, ref in enumerate((start_ref, end_ref)):
            bounds[number : number + 1, :] = jnp.concatenate(
                [
                    edges[number, pl.ds(left, 1), :][:, HALO : 2 * HALO],
                    ref[...].astype(jnp.float32),
                    edges[number, pl.ds(right, 1), :][:, 0:HALO],
                ],
                axis=1,
            )

    return call(
        kernel,
        (
            jax.ShapeDtypeStruct((rows, 2 * NMEL), jnp.bfloat16),
            jax.ShapeDtypeStruct((2, frames_shard + 2 * HALO), jnp.float32),
        ),
        (starts, ends, *stacks, tables),
        scratch=[
            pltpu.VMEM((rows, TAIL_LINES * LANES), jnp.float32),
            pltpu.VMEM((rows, HEAD_LINES * LANES), jnp.float32),
            pltpu.VMEM((rows, HEAD_LINES * LANES), jnp.float32),
            pltpu.VMEM((2, rows, LANES), jnp.float32),
        ],
        micros=0.9,
    )


def last_rows(stack_refs, counts, frames_local, fixed, rows):
    lasts = []
    for stack_ref, count in zip(stack_refs, counts):
        for block in range(count):
            kept = stack_ref[block, frames_local - HALO : frames_local, 0 : 2 * NMEL]
            lasts.append(kept.astype(jnp.float32)[HALO - 1 : HALO])
    if len(lasts) < rows:
        lasts.append(jnp.zeros((rows - len(lasts), 2 * NMEL), jnp.float32))
    return jnp.concatenate([jnp.concatenate(lasts, axis=0).astype(jnp.bfloat16), fixed], axis=1)


def patch(held, fixed, slots, frames_local):
    fixed = fixed.astype(jnp.float32)
    for number, slot in enumerate(slots):
        here = slice((number + 1) * frames_local - HALO, (number + 1) * frames_local)
        kept = held[here, :].astype(jnp.float32)
        last = lax.broadcasted_iota(jnp.int32, kept.shape, 0) == HALO - 1
        held[here, :] = jnp.where(last, fixed[slot : slot + 1, :], kept).astype(held.dtype)


def assemble(parts, after=()):
    counts = [part.shape[0] for part in parts]

    def kernel(*refs):
        begin = 0
        for ref, count in zip(refs, counts):
            refs[-1][begin : begin + count] = ref[...]
            begin += count

    shape = jax.ShapeDtypeStruct((sum(counts), *parts[0].shape[1:]), parts[0].dtype)
    return call(kernel, shape, (*parts, *after))


def slot_of(places, tm, mp):
    found = jnp.int32(0)
    for slot, (slot_tm, slot_mp) in enumerate(places):
        here = (slot_tm(lax.axis_index("tm")) == tm) & (lax.axis_index("mp") ^ slot_mp == mp)
        found = jnp.where(here, slot, found)
    return found


def project_rows(stack, weights, frames_local, query_blocks, boundary=None):
    count = stack.shape[0]
    rows, width = count * frames_local, weights[1].shape[2]
    query_rows = query_blocks * frames_local
    places, every, fixed = boundary or ((), (), jnp.zeros((0, 2 * NMEL), jnp.bfloat16))
    counts = [block.shape[0] for block in every]
    last_count = fixed.shape[0]
    extra_rows = last_count + 2 * HALO if boundary else 0

    def boundary_stack(every_refs, fixed_ref, lasts, heads, tails):
        lasts[...] = last_rows(
            every_refs, counts, frames_local, fixed_ref[...], last_count
        ).astype(jnp.float32)
        slot = 0
        for ref, blocks in zip(every_refs, counts):
            for block in range(blocks):
                heads[slot] = ref[block, 0:HALO, :]
                tails[slot] = ref[block, frames_local - HALO : frames_local, :]
                slot += 1
        time_index, parts = lax.axis_index("tm"), lax.axis_size("mp")
        left = slot_of(places, time_index - 1, parts - 1)
        right = slot_of(places, time_index + 1, 0)
        tail = tails[left].astype(jnp.float32)
        final = lax.broadcasted_iota(jnp.int32, tail.shape, 0) == HALO - 1
        tail = jnp.where(final, lasts[pl.ds(left, 1), :], tail).astype(jnp.bfloat16)
        return [lasts[...].astype(jnp.bfloat16), tail, heads[right]]

    def kernel(stack_ref, w_sub, w_att, sums, *refs):
        stack_rows = [stack_ref[block, 0:frames_local, :] for block in range(count)]
        if boundary:
            every_refs, refs = refs[: len(every)], refs[len(every) :]
            fixed_ref, *refs = refs
            refs, scratch = refs[:-3], refs[-3:]
            stack_rows += boundary_stack(every_refs, fixed_ref, *scratch)
        features = dot32(jnp.concatenate(stack_rows, axis=0), w_sub[...]).astype(jnp.bfloat16)
        wide = features.astype(jnp.float32)
        center = jnp.mean(wide, axis=-1, keepdims=True)
        spread = jnp.mean(jnp.square(wide - center), axis=-1, keepdims=True)
        scale = lax.rsqrt(spread + 1e-05)

        def projected(part, begin, end):
            product = dot32(features[begin:end], w_att[part])
            shifted = product - center[begin:end] * sums[part : part + 1, :]
            return (shifted * scale[begin:end]).astype(jnp.bfloat16)

        refs = list(refs)
        if query_rows:
            refs.pop(0)[...] = projected(0, 0, query_rows)
        if extra_rows:
            refs.pop(0)[...] = projected(0, rows, rows + extra_rows)
        for part in (1, 2):
            both = projected(part, 0, rows + extra_rows)
            refs.pop(0)[...] = both[:rows]
            if extra_rows:
                refs.pop(0)[...] = both[rows:]

    def shape(size):
        return jax.ShapeDtypeStruct((size, width), jnp.bfloat16)

    shapes = [shape(query_rows)] * bool(query_rows) + [shape(extra_rows)] * bool(extra_rows)
    shapes += ([shape(rows)] + [shape(extra_rows)] * bool(extra_rows)) * 2
    depth = stack.shape[2]
    return call(
        kernel,
        shapes,
        (stack, *weights, *every) + ((fixed,) if boundary else ()),
        scratch=[
            pltpu.VMEM((last_count, depth), jnp.float32),
            pltpu.VMEM((len(places), HALO, depth), jnp.bfloat16),
            pltpu.VMEM((len(places), HALO, depth), jnp.bfloat16),
        ]
        if boundary
        else [],
        micros=0.5 + 0.006 * (rows + extra_rows),
    )


def gather_rows(places, query_slots, bounds, sources, extras, frames_local, outs):
    q_rows, k_all, v_all, q_all, first, last = outs
    parts = lax.axis_size("mp")
    frames_shard = frames_local * parts
    last_count = extras[0].shape[0] - 2 * HALO
    slots = range(len(places))
    for held, group, extra, held_slots in zip(
        (q_all, k_all, v_all), sources, extras, (query_slots, slots, slots)
    ):
        begin = 0
        for source in group:
            held[begin : begin + source.shape[0], :] = source[...]
            begin += source.shape[0]
        patch(held, extra[0:last_count, :], held_slots, frames_local)
    query_places = [places[slot] for slot in query_slots]
    q_rows[0:HALO, :] = extras[0][last_count : last_count + HALO, :]
    for part in range(parts):
        begin = HALO + part * frames_local
        slot = slot_of(query_places, lax.axis_index("tm"), part)
        start = pl.multiple_of(slot * frames_local, HALO)
        q_rows[begin : begin + frames_local, :] = q_all[pl.ds(start, frames_local), :]
    q_rows[HALO + frames_shard :, :] = extras[0][last_count + HALO :, :]
    for line, ref in enumerate((first, last)):
        row = bounds[line : line + 1, :]
        ref[...] = jnp.transpose(jnp.broadcast_to(row, (LANES, row.shape[1])))


def attend_rows(places, begin, q_rows, k_all, v_all, first, last, frames_local, result, bias):
    count, width = result.shape
    rows = k_all.shape[0]
    time_index, model_index = lax.axis_index("tm"), lax.axis_index("mp")
    frames_shard = frames_local * lax.axis_size("mp")
    lows, highs = first[pl.ds(begin, count), :], last[pl.ds(begin, count), :]
    lanes = lax.broadcasted_iota(jnp.int32, (1, LANES), 1)
    for lane in range(0, rows, LANES):
        at = jnp.zeros((1, LANES), jnp.int32)
        for slot in range(lane // frames_local, -(-(lane + LANES) // frames_local)):
            if slot < len(places):
                slot_tm, slot_mp = places[slot]
                base = slot_tm(time_index) * frames_shard
                base += (model_index ^ slot_mp) * frames_local - slot * frames_local + lane
                at = jnp.where(lanes >= slot * frames_local - lane, lanes + base, at)
        at = at.astype(jnp.float32)
        bias[:, lane : lane + LANES] = jnp.where((at >= lows) & (at < highs), 0.0, -1e30)
    for lane in range(0, width, LANES):
        span = min(LANES, width - lane)
        q_pair = q_rows[pl.ds(begin, count), lane : lane + span]
        k_pair = k_all[:, lane : lane + span]
        v_pair = v_all[:, lane : lane + span]
        heads = span // HD
        head_of = lax.broadcasted_iota(jnp.int32, (count, span), 1) // HD
        scaled = q_pair * jnp.bfloat16(1.0 / math.sqrt(HD))
        stacked = jnp.concatenate(
            [jnp.where(head_of == head, scaled, jnp.zeros_like(scaled)) for head in range(heads)],
            axis=0,
        )
        scores = lax.dot_general(
            stacked, k_pair, (((1,), (1,)), ((), ())), preferred_element_type=jnp.float32
        )
        scores = scores + jnp.concatenate([bias[...]] * heads, axis=0)
        weights = jnp.exp(scores - jnp.max(scores, axis=1, keepdims=True))
        total = jnp.sum(weights, axis=1, keepdims=True)
        ratio = dot32(weights.astype(jnp.bfloat16), v_pair) / total
        merged = ratio[0:count]
        for head in range(1, heads):
            merged = jnp.where(head_of == head, ratio[head * count : (head + 1) * count], merged)
        result[:, lane : lane + span] = merged.astype(jnp.bfloat16)


def split_pair(model_index, result, mine, other, frames_local):
    window = mine.shape[0]
    place = lax.rem(model_index, 2) * frames_local
    mine[...] = result[pl.ds(pl.multiple_of(place, HALO), window), :]
    place = frames_local - place
    other[...] = result[pl.ds(pl.multiple_of(place, HALO), window), :]


def attend_far(places, query_slots, far, bounds, sources, extras, frames_local):
    width = sources[0][0].shape[1]
    query_count, rows = (sum(group.shape[0] for group in groups) for groups in sources[:2])
    sizes = [len(groups) for groups in sources]
    extended = frames_local * lax.axis_size("mp") + 2 * HALO
    window = frames_local + 2 * HALO
    pair = 2 * frames_local + 2 * HALO

    def kernel(bound_ref, *refs):
        groups = []
        for size in sizes:
            groups.append(refs[:size])
            refs = refs[size:]
        extra_refs, refs = refs[:3], refs[3:]
        windows, refs = refs[: 2 * len(far)], refs[2 * len(far) :]
        q_rows, k_all, v_all, first, last, q_all, result, bias = refs
        gather_rows(
            places,
            query_slots,
            bound_ref,
            groups,
            extra_refs,
            frames_local,
            (q_rows, k_all, v_all, q_all, first, last),
        )
        model_index = lax.axis_index("mp")
        for number, bit in enumerate(far):
            begin = pl.multiple_of((model_index ^ bit) // 2 * (2 * frames_local), HALO)
            attend_rows(
                places, begin, q_rows, k_all, v_all, first, last, frames_local, result, bias
            )
            split_pair(
                model_index, result, windows[2 * number], windows[2 * number + 1], frames_local
            )

    def shape(count, wide=width, dtype=jnp.bfloat16):
        return jax.ShapeDtypeStruct((count, wide), dtype)

    return call(
        kernel,
        [shape(window)] * (2 * len(far))
        + [shape(extended), shape(rows), shape(rows)]
        + [shape(extended, LANES, jnp.float32)] * 2,
        (bounds, *(array for groups in sources for array in groups), *extras),
        scratch=[
            pltpu.VMEM((query_count, width), jnp.bfloat16),
            pltpu.VMEM((pair, width), jnp.bfloat16),
            pltpu.VMEM((pair, rows), jnp.float32),
        ],
        micros=2.5 * len(far),
        vmem=16 + pair * rows * 20 // 1024 // 1024,
    )


def attend_near(places, after, q_rows, k_all, v_all, first, last, frames_local):
    rows, width = k_all.shape
    window = frames_local + 2 * HALO
    pair = 2 * frames_local + 2 * HALO

    def kernel(_, q_ref, k_ref, v_ref, first_ref, last_ref, mine, other, result, bias):
        model_index = lax.axis_index("mp")
        begin = pl.multiple_of(model_index // 2 * (2 * frames_local), HALO)
        attend_rows(
            places, begin, q_ref, k_ref, v_ref, first_ref, last_ref, frames_local, result, bias
        )
        split_pair(model_index, result, mine, other, frames_local)

    return call(
        kernel,
        [jax.ShapeDtypeStruct((window, width), jnp.bfloat16)] * 2,
        (after, q_rows, k_all, v_all, first, last),
        scratch=[
            pltpu.VMEM((pair, width), jnp.bfloat16),
            pltpu.VMEM((pair, rows), jnp.float32),
        ],
        micros=2.0,
        vmem=16 + pair * rows * 20 // 1024 // 1024,
    )


def far_branch(windows, w_rows):
    count = len(windows) // 2

    def kernel(*refs):
        windows, (w_own, w_near), outs = refs[: 2 * count], refs[2 * count :][:2], refs[-count:]
        for number in range(count):
            own, near = windows[2 * number : 2 * number + 2]
            share = dot32(own[...], w_own[...]) + dot32(near[...], w_near[...])
            outs[number][...] = share.astype(jnp.bfloat16)

    shape = jax.ShapeDtypeStruct((windows[0].shape[0], w_rows[0].shape[1]), jnp.bfloat16)
    return call(kernel, [shape] * count, (*windows, *w_rows), micros=0.9 * count)


def near_branch(places, windows, w_rows, stacks, fixed, w_subsample, frames_local):
    counts = [stack.shape[0] for stack in stacks]
    depth, model = w_subsample.shape
    window = frames_local + 2 * HALO
    slots = len(places)

    def kernel(own, near, w_own, w_near, *refs):
        stack_refs, (fixed_ref, w_sub, out, held, taken) = refs[: len(counts)], refs[len(counts) :]
        begin = 0
        for stack_ref, count in zip(stack_refs, counts):
            for block in range(count):
                held[begin : begin + frames_local, :] = stack_ref[block, 0:frames_local, :]
                begin += frames_local
        rows = last_rows(stack_refs, counts, frames_local, fixed_ref[...], fixed.shape[0])
        patch(held, rows, range(slots), frames_local)
        parts = lax.axis_size("mp")
        block = lax.axis_index("tm") * parts + lax.axis_index("mp") + parts

        def source(number, offset, count):
            slot = slot_of(places, number // parts - 1, lax.rem(number, parts))
            start = pl.multiple_of(slot * frames_local + offset, HALO)
            return held[pl.ds(start, count), :]

        taken[0:HALO, :] = source(block - 1, frames_local - HALO, HALO)
        taken[HALO : HALO + frames_local, :] = source(block, 0, frames_local)
        taken[HALO + frames_local : window, :] = source(block + 1, 0, HALO)
        features = dot32(taken[...], w_sub[...]).astype(jnp.bfloat16).astype(jnp.float32)
        share = dot32(own[...], w_own[...]) + dot32(near[...], w_near[...])
        out[...] = features + share

    return call(
        kernel,
        jax.ShapeDtypeStruct((window, model), jnp.float32),
        (*windows, *w_rows, *stacks, fixed, w_subsample),
        scratch=[
            pltpu.VMEM((slots * frames_local, depth), jnp.bfloat16),
            pltpu.VMEM((window, depth), jnp.bfloat16),
        ],
        micros=1.2,
    )


def finish_rows(base, shares, gain, taps, frames_local):
    count = len(shares)
    parts = lax.axis_size("mp")
    window, model = base.shape
    chunk = 2 * LANES
    offset = HALO - KERNEL // 2

    def kernel(base_ref, *refs):
        share_refs, (gain_ref, tap_ref, out, held, mixed_rows) = refs[:count], refs[count:]
        mixed = base_ref[...]
        for share_ref in share_refs:
            mixed += share_ref[...].astype(jnp.float32)
        mixed = mixed.astype(jnp.bfloat16).astype(jnp.float32)
        mixed_rows[...] = mixed[HALO : HALO + frames_local]
        conv_in = (normalize(mixed) * gain_ref[...]).astype(jnp.bfloat16).astype(jnp.float32)
        held[HALO : HALO + frames_local, :] = conv_in[HALO : HALO + frames_local]
        block = lax.axis_index("tm") * parts + lax.axis_index("mp")
        before = block > 0
        held[0:HALO, :] = jnp.where(before, conv_in[0:HALO], 0.0)
        after = block < lax.axis_size("tm") * parts - 1
        held[HALO + frames_local : window, :] = jnp.where(after, conv_in[HALO + frames_local :], 0.0)
        for lane in range(0, model, chunk):
            here = slice(lane, lane + chunk)
            total = jnp.zeros((frames_local, chunk), jnp.float32)
            tap_rows = tap_ref[:, here].astype(jnp.float32)
            rows = held[:, here]
            reach = frames_local + 8
            for phase in range(8):
                share = jnp.zeros((reach, chunk), jnp.float32)
                for tap in range(KERNEL):
                    if (tap + offset) % 8 == phase:
                        begin = (tap + offset) // 8 * 8
                        share += rows[begin : begin + reach] * tap_rows[tap : tap + 1]
                moved = pltpu.roll(share, reach - phase, axis=0) if phase else share
                total += moved[0:frames_local]
            silu = total / (1.0 + jnp.exp(-total))
            out[:, here] = (mixed_rows[:, here] + silu).astype(jnp.bfloat16)

    return call(
        kernel,
        jax.ShapeDtypeStruct((frames_local, model), jnp.bfloat16),
        (base, *shares, gain, taps),
        scratch=[
            pltpu.VMEM((window, model), jnp.float32),
            pltpu.VMEM((frames_local, model), jnp.float32),
        ],
        micros=2.8,
    )


def exchange(block, axis, bit):
    return lax.ppermute(block, axis, [(i, i ^ bit) for i in range(lax.axis_size(axis))])


def shifted(block, axis, distance):
    count = lax.axis_size(axis)
    route = [(i - distance, i) for i in range(count) if 0 <= i - distance < count]
    return lax.ppermute(block, axis, route)


def shards(
    waveform,
    segment_start,
    segment_end,
    w_subsample,
    w_attention,
    w_output,
    gain_convolution,
    w_depthwise,
):
    frames_local = waveform.shape[0] // (SUB * HOP)
    frames_shard = segment_start.shape[0]
    parts, shards_total = lax.axis_size("mp"), lax.axis_size("tm")
    bits = [1 << b for b in reversed(range((parts - 1).bit_length()))]

    samples = waveform.reshape(-1, LANES)
    starts, ends = segment_start[None, :], segment_end[None, :]
    tables = jnp.asarray(front_tables())
    stacked = log_mel_rows(starts, ends, samples, tables, frames_local)
    weights = fetch(stacked, w_subsample, w_attention)

    w_near = exchange(w_output, "mp", bits[-1])

    reach = min((SEG_MAX + HALO - 2) // frames_shard + 1, shards_total - 1)
    whole = reach == shards_total - 1 and shards_total & (shards_total - 1) == 0
    if whole:
        moves = [lambda tm, bit=bit: tm ^ bit for bit in range(1, shards_total)]
        column = [exchange(stacked, "tm", bit) for bit in range(1, shards_total)]
    else:
        steps = [sign * d for d in range(1, reach + 1) for sign in (1, -1)]
        moves = [lambda tm, step=step: tm - step for step in steps]
        column = [shifted(stacked, "tm", step) for step in steps]
    early = [(stacked, [(lambda tm: tm, 0)])]
    late = [(assemble(column, weights[-1:]), [(move, 0) for move in moves])]

    def across(blocks, bit):
        return [
            (exchange(block, "mp", bit), [(move, mp ^ bit) for move, mp in held])
            for block, held in blocks
        ]

    for bit in bits[:-1]:
        early, late = early + across(early, bit), late + across(late, bit)
    ready = early + late[:1]
    joined = (assemble([block for block, _ in ready]), sum([held for _, held in ready], []))
    groups = [joined] + across([joined], bits[-1]) + late[1:] + across(late[1:], bits[-1])
    stacks, held = zip(*groups)
    places = sum(held, [])
    joined_slots = range(len(joined[1]), 2 * len(joined[1]))
    query_slots = [*range(len(early)), *joined_slots[: len(early)]]
    fixed, bounds = boundary_rows(places, starts, ends, stacks, tables, frames_local)
    projected = [
        project_rows(block, weights, frames_local, len(early) if number < 2 else 0)
        for number, block in enumerate(stacks[:-1])
    ]
    boundary = (places, stacks, fixed)
    if len(stacks) > 2:
        outs = project_rows(stacks[-1], weights, frames_local, 0, boundary)
    else:
        query, *outs = project_rows(stacks[-1], weights, frames_local, len(early), boundary)
        projected.append([query])
    extras = (outs[0], outs[2], outs[4])
    queries = [group[0] for group in projected[:2]]
    keys = [*(group[-2] for group in projected if len(group) > 1), outs[1]]
    values = [*(group[-1] for group in projected if len(group) > 1), outs[3]]

    far = list(range(2, parts, 2))
    outs = attend_far(
        places, query_slots, far, bounds, (queries, keys, values), extras, frames_local
    )
    windows, shared = outs[: 2 * len(far)], outs[2 * len(far) :]
    windows = [
        exchange(block, "mp", 1) if number % 2 else block for number, block in enumerate(windows)
    ]
    w_rows = (w_output, w_near)
    shares = far_branch(windows, w_rows)
    mine, other = attend_near(places, shares[0], *shared, frames_local)
    shares = [exchange(share, "mp", bit) for share, bit in zip(shares, far)]
    base = near_branch(
        places, (mine, exchange(other, "mp", 1)), w_rows, stacks, fixed, weights[0], frames_local
    )
    return finish_rows(base, shares, gain_convolution[None, :], w_depthwise, frames_local)


def solution(mesh):
    placed = (
        P(("groups", "tm", "mp")),
        P(("groups", "tm")),
        P(("groups", "tm")),
        P(),
        P(None, None, "mp"),
        P("mp", None),
        P(),
        P(),
    )
    return jax.shard_map(
        shards,
        mesh=mesh,
        in_specs=placed,
        out_specs=P(("groups", "tm", "mp"), None),
        check_vma=False,
    )
```

```python
import math

import jax
import jax.numpy as jnp
import ml_dtypes
import numpy as np
from jax import lax
from jax.experimental import pallas as pl
from jax.experimental.pallas import tpu as pltpu
from jax.sharding import PartitionSpec as P

HD = 64
NMEL = 128
NFFT = 400
HOP = 160
BINS = 256
SUB = 4
KERNEL = 31
SEG_MAX = 750
LANES = 128
HALO = 16
EXTRA = 8
FLOPS_PER_MICRO = 2000000000
TAIL_LINES = 3
HEAD_LINES = 2
DIGIT = 128
FRAME_ROWS = SUB * HOP // LANES
WIDE = -(-NFFT // LANES) * LANES


def split_high_low(table):
    high = table.astype(ml_dtypes.bfloat16)
    low = (table - high.astype(np.float32)).astype(ml_dtypes.bfloat16)
    return high, low


def fourier_table():
    sample_index = np.arange(NFFT)[:, None]
    bin_index = np.arange(BINS)[None, :]
    angle = (sample_index * bin_index % NFFT) * (2.0 * math.pi / NFFT)
    window = 0.5 - 0.5 * np.cos(np.arange(NFFT) * (2.0 * math.pi / NFFT))
    kept = bin_index <= NFFT // 2
    cosine = np.where(kept, np.cos(angle), 0.0) * window[:, None]
    sine = np.where(kept, -np.sin(angle), 0.0) * window[:, None]
    table = np.concatenate([cosine, sine], axis=1).astype(np.float32)
    return np.pad(table, ((0, WIDE - NFFT), (0, 0)))


def mel_bank():
    mel_top = 2595.0 * math.log10(1.0 + 8000.0 / 700.0)
    mel_points = np.arange(NMEL + 2) * (mel_top / (NMEL + 1))
    edges = 700.0 * (np.power(10.0, mel_points / 2595.0) - 1.0) * (NFFT / 16000.0)
    widths = np.maximum(edges[2:] - edges[1:-1], 1.0)
    bin_value = np.arange(BINS)[:, None]
    triangle = np.maximum(0.0, 1.0 - np.abs(bin_value - edges[None, 1:-1]) / widths[None, :])
    return np.where(bin_value <= NFFT // 2, triangle, 0.0).astype(np.float32)


def front_tables():
    high, low = split_high_low(fourier_table())
    bank = np.concatenate(split_high_low(mel_bank()), axis=0)
    return np.concatenate([high, low, bank], axis=1)


def dot32(left, right):
    return jnp.dot(left, right, preferred_element_type=jnp.float32)


def dot_split(values, table_high, table_low):
    high = values.astype(jnp.bfloat16)
    low = (values - high.astype(jnp.float32)).astype(jnp.bfloat16)
    return dot32(high, table_high) + (dot32(low, table_high) + dot32(high, table_low))


def normalize(values):
    center = jnp.mean(values, axis=-1, keepdims=True)
    shifted = values - center
    spread = jnp.mean(jnp.square(shifted), axis=-1, keepdims=True)
    return shifted * lax.rsqrt(spread + 1e-05)


def call(kernel, out_shape, operands, scratch=(), micros=1.0, remote=0, vmem=16):
    specs = [pl.BlockSpec(memory_space=pltpu.VMEM)] * (len(operands) - remote)
    specs += [pl.BlockSpec(memory_space=pltpu.HBM)] * remote
    return pl.pallas_call(
        kernel,
        out_shape=out_shape,
        in_specs=specs,
        out_specs=jax.tree.map(lambda _: pl.BlockSpec(memory_space=pltpu.VMEM), out_shape),
        scratch_shapes=list(scratch),
        compiler_params=pltpu.CompilerParams(vmem_limit_bytes=vmem * 1024 * 1024),
        cost_estimate=pl.CostEstimate(
            flops=int(micros * FLOPS_PER_MICRO), bytes_accessed=1000000, transcendentals=0
        ),
    )(*operands)


def fetch(stacked, w_subsample, w_attention):
    parts, _, width = w_attention.shape

    def kernel(stack_ref, w_sub, w_att, out_sub, out_att, sums, out_stack, sems):
        out_stack[...] = stack_ref[...]
        copies = [
            pltpu.make_async_copy(w_att, out_att, sems.at[0]),
            pltpu.make_async_copy(w_sub, out_sub, sems.at[1]),
        ]
        for copy in copies:
            copy.start()
        for copy in copies:
            copy.wait()
        sums[...] = jnp.zeros_like(sums)
        for part in range(parts):
            columns = out_att[part].astype(jnp.float32)
            sums[part : part + 1, :] = jnp.sum(columns, axis=0, keepdims=True)

    return call(
        kernel,
        [jax.ShapeDtypeStruct(array.shape, array.dtype) for array in (w_subsample, w_attention)]
        + [
            jax.ShapeDtypeStruct((8, width), jnp.float32),
            jax.ShapeDtypeStruct(stacked.shape, stacked.dtype),
        ],
        (stacked, w_subsample, w_attention),
        scratch=[pltpu.SemaphoreType.DMA((2,))],
        remote=2,
    )


def padded_row(row):
    return jnp.concatenate([row, jnp.zeros((1, SUB * NMEL - row.shape[1]), row.dtype)], axis=1)


def log_mel(windows, tables):
    wide, bank = 2 * BINS, slice(4 * BINS, 4 * BINS + NMEL)
    spectrum = dot_split(windows, tables[:, 0:wide], tables[:, wide : 2 * wide])
    power = jnp.square(spectrum[:, :BINS]) + jnp.square(spectrum[:, BINS:])
    return jnp.log(dot_split(power, tables[0:BINS, bank], tables[BINS:, bank]) + 1e-06)


def log_mel_rows(starts, ends, samples, tables, frames_local):
    rows = frames_local * FRAME_ROWS
    frames_shard = starts.shape[1]

    def kernel(start_ref, end_ref, wave, tables_ref, out, held):
        held[0:rows, :] = wave[...]
        held[rows : rows + 8, :] = jnp.zeros((8, LANES), jnp.float32)
        lines = [held[pl.ds(j, frames_local, stride=FRAME_ROWS), :] for j in range(FRAME_ROWS + 2)]
        windows = []
        for sub in range(SUB):
            line, lane = divmod(sub * HOP, LANES)
            taken = jnp.concatenate(lines[line : line + WIDE // LANES], axis=1)
            windows.append(pltpu.roll(taken, WIDE - lane, axis=1) if lane else taken)
        extras = []
        for taken in (range(rows - TAIL_LINES, rows), range(HEAD_LINES)):
            line = jnp.concatenate([held[row : row + 1, :] for row in taken], axis=1)
            high = line.astype(jnp.bfloat16).astype(jnp.float32)
            extras += [padded_row(high), padded_row(line - high)]
        for ref in (start_ref, end_ref):
            edge = jnp.concatenate([ref[:, :HALO], ref[:, frames_shard - HALO :]], axis=1)
            high = edge // DIGIT
            low = edge - high * DIGIT
            extras += [padded_row(digit.astype(jnp.float32)) for digit in (high, low)]
        out[0, frames_local:, :] = jnp.concatenate(extras, axis=0).astype(jnp.bfloat16)
        mel = log_mel(jnp.concatenate(windows, axis=0), tables_ref)
        for sub in range(SUB):
            out[0, 0:frames_local, sub * NMEL : (sub + 1) * NMEL] = mel[
                sub * frames_local : (sub + 1) * frames_local
            ].astype(jnp.bfloat16)

    return call(
        kernel,
        jax.ShapeDtypeStruct((1, frames_local + EXTRA, SUB * NMEL), jnp.bfloat16),
        (starts, ends, samples, tables),
        scratch=[pltpu.VMEM((rows + 8, LANES), jnp.float32)],
        micros=1.0,
    )


def boundary_rows(places, starts, ends, stacks, tables, frames_local):
    counts = [stack.shape[0] for stack in stacks]
    slots = len(places)
    rows = -(-slots // HALO) * HALO
    frames_shard = starts.shape[1]
    parts = lax.axis_size("mp")
    final = lax.axis_size("tm") * parts - 1

    def kernel(start_ref, end_ref, *refs):
        stack_refs, refs = refs[: len(counts)], refs[len(counts) :]
        tables_ref, out, bounds, tails, heads, nexts, edges = refs
        time_index, model_index = lax.axis_index("tm"), lax.axis_index("mp")
        tails[...] = jnp.zeros_like(tails)
        nexts[...] = jnp.zeros_like(nexts)
        slot = 0
        for stack_ref, count in zip(stack_refs, counts):
            for block in range(count):
                kept = stack_ref[block, frames_local:, :].astype(jnp.float32)
                here = slice(slot, slot + 1)
                tails[here, :] = (kept[0:1] + kept[1:2])[:, : TAIL_LINES * LANES]
                heads[here, :] = (kept[2:3] + kept[3:4])[:, : HEAD_LINES * LANES]
                for line in range(2):
                    edge = kept[4 + 2 * line : 5 + 2 * line] * DIGIT + kept[5 + 2 * line : 6 + 2 * line]
                    edges[line, here, :] = edge[:, :LANES]
                slot += 1
        for slot, (slot_tm, slot_mp) in enumerate(places):
            following = slot_tm(time_index) * parts + (model_index ^ slot_mp) + 1
            found = slot_of(places, following // parts, lax.rem(following, parts))
            taken = heads[pl.ds(found, 1), :]
            nexts[slot : slot + 1, :] = jnp.where(following > final, 0.0, taken)
        line = jnp.concatenate([tails[...], nexts[...]], axis=1)
        windows = []
        for sub in range(SUB - 2, SUB):
            skip, lane = divmod(sub * HOP - (FRAME_ROWS - TAIL_LINES) * LANES, LANES)
            windows.append(
                pltpu.roll(line[:, skip * LANES : skip * LANES + WIDE], WIDE - lane, axis=1)
            )
        mel = log_mel(jnp.concatenate(windows, axis=0), tables_ref).astype(jnp.bfloat16)
        for number in range(2):
            lane = number * NMEL
            out[:, lane : lane + NMEL] = mel[number * rows : (number + 1) * rows]
        left = slot_of(places, time_index - 1, model_index)
        right = slot_of(places, time_index + 1, model_index)
        for number, ref in enumerate((start_ref, end_ref)):
            bounds[number : number + 1, :] = jnp.concatenate(
                [
                    edges[number, pl.ds(left, 1), :][:, HALO : 2 * HALO],
                    ref[...].astype(jnp.float32),
                    edges[number, pl.ds(right, 1), :][:, 0:HALO],
                ],
                axis=1,
            )

    return call(
        kernel,
        (
            jax.ShapeDtypeStruct((rows, 2 * NMEL), jnp.bfloat16),
            jax.ShapeDtypeStruct((2, frames_shard + 2 * HALO), jnp.float32),
        ),
        (starts, ends, *stacks, tables),
        scratch=[
            pltpu.VMEM((rows, TAIL_LINES * LANES), jnp.float32),
            pltpu.VMEM((rows, HEAD_LINES * LANES), jnp.float32),
            pltpu.VMEM((rows, HEAD_LINES * LANES), jnp.float32),
            pltpu.VMEM((2, rows, LANES), jnp.float32),
        ],
        micros=0.9,
    )


def last_rows(stack_refs, counts, frames_local, fixed, rows):
    lasts = []
    for stack_ref, count in zip(stack_refs, counts):
        for block in range(count):
            kept = stack_ref[block, frames_local - HALO : frames_local, 0 : 2 * NMEL]
            lasts.append(kept.astype(jnp.float32)[HALO - 1 : HALO])
    if len(lasts) < rows:
        lasts.append(jnp.zeros((rows - len(lasts), 2 * NMEL), jnp.float32))
    return jnp.concatenate([jnp.concatenate(lasts, axis=0).astype(jnp.bfloat16), fixed], axis=1)


def patch(held, fixed, slots, frames_local):
    fixed = fixed.astype(jnp.float32)
    for number, slot in enumerate(slots):
        here = slice((number + 1) * frames_local - HALO, (number + 1) * frames_local)
        kept = held[here, :].astype(jnp.float32)
        last = lax.broadcasted_iota(jnp.int32, kept.shape, 0) == HALO - 1
        held[here, :] = jnp.where(last, fixed[slot : slot + 1, :], kept).astype(held.dtype)


def assemble(parts, after=()):
    counts = [part.shape[0] for part in parts]

    def kernel(*refs):
        begin = 0
        for ref, count in zip(refs, counts):
            refs[-1][begin : begin + count] = ref[...]
            begin += count

    shape = jax.ShapeDtypeStruct((sum(counts), *parts[0].shape[1:]), parts[0].dtype)
    return call(kernel, shape, (*parts, *after))


def slot_of(places, tm, mp):
    found = jnp.int32(0)
    for slot, (slot_tm, slot_mp) in enumerate(places):
        here = (slot_tm(lax.axis_index("tm")) == tm) & (lax.axis_index("mp") ^ slot_mp == mp)
        found = jnp.where(here, slot, found)
    return found


def project_rows(stack, weights, frames_local, query_blocks, boundary=None):
    count = stack.shape[0]
    rows, width = count * frames_local, weights[1].shape[2]
    query_rows = query_blocks * frames_local
    places, every, fixed = boundary or ((), (), jnp.zeros((0, 2 * NMEL), jnp.bfloat16))
    counts = [block.shape[0] for block in every]
    last_count = fixed.shape[0]
    extra_rows = last_count + 2 * HALO if boundary else 0

    def boundary_stack(every_refs, fixed_ref, lasts, heads, tails):
        lasts[...] = last_rows(
            every_refs, counts, frames_local, fixed_ref[...], last_count
        ).astype(jnp.float32)
        slot = 0
        for ref, blocks in zip(every_refs, counts):
            for block in range(blocks):
                heads[slot] = ref[block, 0:HALO, :]
                tails[slot] = ref[block, frames_local - HALO : frames_local, :]
                slot += 1
        time_index, parts = lax.axis_index("tm"), lax.axis_size("mp")
        left = slot_of(places, time_index - 1, parts - 1)
        right = slot_of(places, time_index + 1, 0)
        tail = tails[left].astype(jnp.float32)
        final = lax.broadcasted_iota(jnp.int32, tail.shape, 0) == HALO - 1
        tail = jnp.where(final, lasts[pl.ds(left, 1), :], tail).astype(jnp.bfloat16)
        return [lasts[...].astype(jnp.bfloat16), tail, heads[right]]

    def kernel(stack_ref, w_sub, w_att, sums, *refs):
        stack_rows = [stack_ref[block, 0:frames_local, :] for block in range(count)]
        if boundary:
            every_refs, refs = refs[: len(every)], refs[len(every) :]
            fixed_ref, *refs = refs
            refs, scratch = refs[:-3], refs[-3:]
            stack_rows += boundary_stack(every_refs, fixed_ref, *scratch)
        features = dot32(jnp.concatenate(stack_rows, axis=0), w_sub[...]).astype(jnp.bfloat16)
        wide = features.astype(jnp.float32)
        center = jnp.mean(wide, axis=-1, keepdims=True)
        spread = jnp.mean(jnp.square(wide - center), axis=-1, keepdims=True)
        scale = lax.rsqrt(spread + 1e-05)

        def projected(part, begin, end):
            product = dot32(features[begin:end], w_att[part])
            shifted = product - center[begin:end] * sums[part : part + 1, :]
            return (shifted * scale[begin:end]).astype(jnp.bfloat16)

        refs = list(refs)
        if query_rows:
            refs.pop(0)[...] = projected(0, 0, query_rows)
        if extra_rows:
            refs.pop(0)[...] = projected(0, rows, rows + extra_rows)
        for part in (1, 2):
            both = projected(part, 0, rows + extra_rows)
            refs.pop(0)[...] = both[:rows]
            if extra_rows:
                refs.pop(0)[...] = both[rows:]

    def shape(size):
        return jax.ShapeDtypeStruct((size, width), jnp.bfloat16)

    shapes = [shape(query_rows)] * bool(query_rows) + [shape(extra_rows)] * bool(extra_rows)
    shapes += ([shape(rows)] + [shape(extra_rows)] * bool(extra_rows)) * 2
    depth = stack.shape[2]
    return call(
        kernel,
        shapes,
        (stack, *weights, *every) + ((fixed,) if boundary else ()),
        scratch=[
            pltpu.VMEM((last_count, depth), jnp.float32),
            pltpu.VMEM((len(places), HALO, depth), jnp.bfloat16),
            pltpu.VMEM((len(places), HALO, depth), jnp.bfloat16),
        ]
        if boundary
        else [],
        micros=0.5 + 0.006 * (rows + extra_rows),
    )


def gather_rows(places, query_slots, bounds, sources, extras, frames_local, outs):
    q_rows, k_all, v_all, q_all, first, last = outs
    parts = lax.axis_size("mp")
    frames_shard = frames_local * parts
    last_count = extras[0].shape[0] - 2 * HALO
    slots = range(len(places))
    for held, group, extra, held_slots in zip(
        (q_all, k_all, v_all), sources, extras, (query_slots, slots, slots)
    ):
        begin = 0
        for source in group:
            held[begin : begin + source.shape[0], :] = source[...]
            begin += source.shape[0]
        patch(held, extra[0:last_count, :], held_slots, frames_local)
    query_places = [places[slot] for slot in query_slots]
    q_rows[0:HALO, :] = extras[0][last_count : last_count + HALO, :]
    for part in range(parts):
        begin = HALO + part * frames_local
        slot = slot_of(query_places, lax.axis_index("tm"), part)
        start = pl.multiple_of(slot * frames_local, HALO)
        q_rows[begin : begin + frames_local, :] = q_all[pl.ds(start, frames_local), :]
    q_rows[HALO + frames_shard :, :] = extras[0][last_count + HALO :, :]
    for line, ref in enumerate((first, last)):
        row = bounds[line : line + 1, :]
        ref[...] = jnp.transpose(jnp.broadcast_to(row, (LANES, row.shape[1])))


def attend_rows(places, begin, q_rows, k_all, v_all, first, last, frames_local, result, bias):
    count, width = result.shape
    rows = k_all.shape[0]
    time_index, model_index = lax.axis_index("tm"), lax.axis_index("mp")
    frames_shard = frames_local * lax.axis_size("mp")
    lows, highs = first[pl.ds(begin, count), :], last[pl.ds(begin, count), :]
    lanes = lax.broadcasted_iota(jnp.int32, (1, LANES), 1)
    for lane in range(0, rows, LANES):
        at = jnp.zeros((1, LANES), jnp.int32)
        for slot in range(lane // frames_local, -(-(lane + LANES) // frames_local)):
            if slot < len(places):
                slot_tm, slot_mp = places[slot]
                base = slot_tm(time_index) * frames_shard
                base += (model_index ^ slot_mp) * frames_local - slot * frames_local + lane
                at = jnp.where(lanes >= slot * frames_local - lane, lanes + base, at)
        at = at.astype(jnp.float32)
        bias[:, lane : lane + LANES] = jnp.where((at >= lows) & (at < highs), 0.0, -1e30)
    for lane in range(0, width, LANES):
        span = min(LANES, width - lane)
        q_pair = q_rows[pl.ds(begin, count), lane : lane + span]
        k_pair = k_all[:, lane : lane + span]
        v_pair = v_all[:, lane : lane + span]
        heads = span // HD
        head_of = lax.broadcasted_iota(jnp.int32, (count, span), 1) // HD
        scaled = q_pair * jnp.bfloat16(1.0 / math.sqrt(HD))
        stacked = jnp.concatenate(
            [jnp.where(head_of == head, scaled, jnp.zeros_like(scaled)) for head in range(heads)],
            axis=0,
        )
        scores = lax.dot_general(
            stacked, k_pair, (((1,), (1,)), ((), ())), preferred_element_type=jnp.float32
        )
        scores = scores + jnp.concatenate([bias[...]] * heads, axis=0)
        weights = jnp.exp(scores - jnp.max(scores, axis=1, keepdims=True))
        total = jnp.sum(weights, axis=1, keepdims=True)
        ratio = dot32(weights.astype(jnp.bfloat16), v_pair) / total
        merged = ratio[0:count]
        for head in range(1, heads):
            merged = jnp.where(head_of == head, ratio[head * count : (head + 1) * count], merged)
        result[:, lane : lane + span] = merged.astype(jnp.bfloat16)


def split_pair(model_index, result, mine, other, frames_local):
    window = mine.shape[0]
    place = lax.rem(model_index, 2) * frames_local
    mine[...] = result[pl.ds(pl.multiple_of(place, HALO), window), :]
    place = frames_local - place
    other[...] = result[pl.ds(pl.multiple_of(place, HALO), window), :]


def attend_far(places, query_slots, far, bounds, sources, extras, frames_local):
    width = sources[0][0].shape[1]
    query_count, rows = (sum(group.shape[0] for group in groups) for groups in sources[:2])
    sizes = [len(groups) for groups in sources]
    extended = frames_local * lax.axis_size("mp") + 2 * HALO
    window = frames_local + 2 * HALO
    pair = 2 * frames_local + 2 * HALO

    def kernel(bound_ref, *refs):
        groups = []
        for size in sizes:
            groups.append(refs[:size])
            refs = refs[size:]
        extra_refs, refs = refs[:3], refs[3:]
        windows, refs = refs[: 2 * len(far)], refs[2 * len(far) :]
        q_rows, k_all, v_all, first, last, q_all, result, bias = refs
        gather_rows(
            places,
            query_slots,
            bound_ref,
            groups,
            extra_refs,
            frames_local,
            (q_rows, k_all, v_all, q_all, first, last),
        )
        model_index = lax.axis_index("mp")
        for number, bit in enumerate(far):
            begin = pl.multiple_of((model_index ^ bit) // 2 * (2 * frames_local), HALO)
            attend_rows(
                places, begin, q_rows, k_all, v_all, first, last, frames_local, result, bias
            )
            split_pair(
                model_index, result, windows[2 * number], windows[2 * number + 1], frames_local
            )

    def shape(count, wide=width, dtype=jnp.bfloat16):
        return jax.ShapeDtypeStruct((count, wide), dtype)

    return call(
        kernel,
        [shape(window)] * (2 * len(far))
        + [shape(extended), shape(rows), shape(rows)]
        + [shape(extended, LANES, jnp.float32)] * 2,
        (bounds, *(array for groups in sources for array in groups), *extras),
        scratch=[
            pltpu.VMEM((query_count, width), jnp.bfloat16),
            pltpu.VMEM((pair, width), jnp.bfloat16),
            pltpu.VMEM((pair, rows), jnp.float32),
        ],
        micros=2.5 * len(far),
        vmem=16 + pair * rows * 20 // 1024 // 1024,
    )


def attend_near(places, after, q_rows, k_all, v_all, first, last, frames_local):
    rows, width = k_all.shape
    window = frames_local + 2 * HALO
    pair = 2 * frames_local + 2 * HALO

    def kernel(_, q_ref, k_ref, v_ref, first_ref, last_ref, mine, other, result, bias):
        model_index = lax.axis_index("mp")
        begin = pl.multiple_of(model_index // 2 * (2 * frames_local), HALO)
        attend_rows(
            places, begin, q_ref, k_ref, v_ref, first_ref, last_ref, frames_local, result, bias
        )
        split_pair(model_index, result, mine, other, frames_local)

    return call(
        kernel,
        [jax.ShapeDtypeStruct((window, width), jnp.bfloat16)] * 2,
        (after, q_rows, k_all, v_all, first, last),
        scratch=[
            pltpu.VMEM((pair, width), jnp.bfloat16),
            pltpu.VMEM((pair, rows), jnp.float32),
        ],
        micros=1.0,
        vmem=16 + pair * rows * 20 // 1024 // 1024,
    )


def far_branch(windows, w_rows):
    count = len(windows) // 2

    def kernel(*refs):
        windows, (w_own, w_near), outs = refs[: 2 * count], refs[2 * count :][:2], refs[-count:]
        for number in range(count):
            own, near = windows[2 * number : 2 * number + 2]
            share = dot32(own[...], w_own[...]) + dot32(near[...], w_near[...])
            outs[number][...] = share.astype(jnp.bfloat16)

    shape = jax.ShapeDtypeStruct((windows[0].shape[0], w_rows[0].shape[1]), jnp.bfloat16)
    return call(kernel, [shape] * count, (*windows, *w_rows), micros=0.9 * count)


def near_branch(places, windows, w_rows, stacks, fixed, w_subsample, frames_local):
    counts = [stack.shape[0] for stack in stacks]
    depth, model = w_subsample.shape
    window = frames_local + 2 * HALO
    slots = len(places)

    def kernel(own, near, w_own, w_near, *refs):
        stack_refs, (fixed_ref, w_sub, out, held, taken) = refs[: len(counts)], refs[len(counts) :]
        begin = 0
        for stack_ref, count in zip(stack_refs, counts):
            for block in range(count):
                held[begin : begin + frames_local, :] = stack_ref[block, 0:frames_local, :]
                begin += frames_local
        rows = last_rows(stack_refs, counts, frames_local, fixed_ref[...], fixed.shape[0])
        patch(held, rows, range(slots), frames_local)
        parts = lax.axis_size("mp")
        block = lax.axis_index("tm") * parts + lax.axis_index("mp") + parts

        def source(number, offset, count):
            slot = slot_of(places, number // parts - 1, lax.rem(number, parts))
            start = pl.multiple_of(slot * frames_local + offset, HALO)
            return held[pl.ds(start, count), :]

        taken[0:HALO, :] = source(block - 1, frames_local - HALO, HALO)
        taken[HALO : HALO + frames_local, :] = source(block, 0, frames_local)
        taken[HALO + frames_local : window, :] = source(block + 1, 0, HALO)
        features = dot32(taken[...], w_sub[...]).astype(jnp.bfloat16).astype(jnp.float32)
        share = dot32(own[...], w_own[...]) + dot32(near[...], w_near[...])
        out[...] = features + share

    return call(
        kernel,
        jax.ShapeDtypeStruct((window, model), jnp.float32),
        (*windows, *w_rows, *stacks, fixed, w_subsample),
        scratch=[
            pltpu.VMEM((slots * frames_local, depth), jnp.bfloat16),
            pltpu.VMEM((window, depth), jnp.bfloat16),
        ],
        micros=0.6,
    )


def finish_rows(base, shares, gain, taps, frames_local):
    count = len(shares)
    parts = lax.axis_size("mp")
    window, model = base.shape
    chunk = 2 * LANES
    offset = HALO - KERNEL // 2

    def kernel(base_ref, *refs):
        share_refs, (gain_ref, tap_ref, out, held, mixed_rows) = refs[:count], refs[count:]
        mixed = base_ref[...]
        for share_ref in share_refs:
            mixed += share_ref[...].astype(jnp.float32)
        mixed = mixed.astype(jnp.bfloat16).astype(jnp.float32)
        mixed_rows[...] = mixed[HALO : HALO + frames_local]
        conv_in = (normalize(mixed) * gain_ref[...]).astype(jnp.bfloat16).astype(jnp.float32)
        held[HALO : HALO + frames_local, :] = conv_in[HALO : HALO + frames_local]
        block = lax.axis_index("tm") * parts + lax.axis_index("mp")
        before = block > 0
        held[0:HALO, :] = jnp.where(before, conv_in[0:HALO], 0.0)
        after = block < lax.axis_size("tm") * parts - 1
        held[HALO + frames_local : window, :] = jnp.where(after, conv_in[HALO + frames_local :], 0.0)
        for lane in range(0, model, chunk):
            here = slice(lane, lane + chunk)
            total = jnp.zeros((frames_local, chunk), jnp.float32)
            tap_rows = tap_ref[:, here].astype(jnp.float32)
            rows = held[:, here]
            reach = frames_local + 8
            for phase in range(8):
                share = jnp.zeros((reach, chunk), jnp.float32)
                for tap in range(KERNEL):
                    if (tap + offset) % 8 == phase:
                        begin = (tap + offset) // 8 * 8
                        share += rows[begin : begin + reach] * tap_rows[tap : tap + 1]
                moved = pltpu.roll(share, reach - phase, axis=0) if phase else share
                total += moved[0:frames_local]
            silu = total / (1.0 + jnp.exp(-total))
            out[:, here] = (mixed_rows[:, here] + silu).astype(jnp.bfloat16)

    return call(
        kernel,
        jax.ShapeDtypeStruct((frames_local, model), jnp.bfloat16),
        (base, *shares, gain, taps),
        scratch=[
            pltpu.VMEM((window, model), jnp.float32),
            pltpu.VMEM((frames_local, model), jnp.float32),
        ],
        micros=2.8,
    )


def exchange(block, axis, bit):
    return lax.ppermute(block, axis, [(i, i ^ bit) for i in range(lax.axis_size(axis))])


def shifted(block, axis, distance):
    count = lax.axis_size(axis)
    route = [(i - distance, i) for i in range(count) if 0 <= i - distance < count]
    return lax.ppermute(block, axis, route)


def shards(
    waveform,
    segment_start,
    segment_end,
    w_subsample,
    w_attention,
    w_output,
    gain_convolution,
    w_depthwise,
):
    frames_local = waveform.shape[0] // (SUB * HOP)
    frames_shard = segment_start.shape[0]
    parts, shards_total = lax.axis_size("mp"), lax.axis_size("tm")
    bits = [1 << b for b in reversed(range((parts - 1).bit_length()))]

    samples = waveform.reshape(-1, LANES)
    starts, ends = segment_start[None, :], segment_end[None, :]
    tables = jnp.asarray(front_tables())
    stacked = log_mel_rows(starts, ends, samples, tables, frames_local)
    *weights, kept = fetch(stacked, w_subsample, w_attention)

    w_near = exchange(w_output, "mp", bits[-1])

    reach = min((SEG_MAX + HALO - 2) // frames_shard + 1, shards_total - 1)
    whole = reach == shards_total - 1 and shards_total & (shards_total - 1) == 0
    if whole:
        moves = [lambda tm, bit=bit: tm ^ bit for bit in range(1, shards_total)]
        column = [exchange(stacked, "tm", bit) for bit in range(1, shards_total)]
    else:
        steps = [sign * d for d in range(1, reach + 1) for sign in (1, -1)]
        moves = [lambda tm, step=step: tm - step for step in steps]
        column = [shifted(stacked, "tm", step) for step in steps]
    early = [(kept, [(lambda tm: tm, 0)])]
    late = [(assemble(column, weights[-1:]), [(move, 0) for move in moves])]

    def across(blocks, bit):
        return [
            (exchange(block, "mp", bit), [(move, mp ^ bit) for move, mp in held])
            for block, held in blocks
        ]

    for bit in bits[:-1]:
        early, late = early + across(early, bit), late + across(late, bit)
    ready = early + late[:1]
    joined = (assemble([block for block, _ in ready]), sum([held for _, held in ready], []))
    groups = [joined] + across([joined], bits[-1])
    projected = [
        project_rows(block, weights, frames_local, len(early)) for block, _ in groups
    ]
    done = [group[-1] for group in projected]
    late = [(assemble([block], done), held) for block, held in late[1:]]
    groups += late + across(late, bits[-1])
    stacks, held = zip(*groups)
    places = sum(held, [])
    joined_slots = range(len(joined[1]), 2 * len(joined[1]))
    query_slots = [*range(len(early)), *joined_slots[: len(early)]]
    fixed, bounds = boundary_rows(places, starts, ends, stacks, tables, frames_local)
    projected += [project_rows(block, weights, frames_local, 0) for block in stacks[2:-1]]
    outs = project_rows(stacks[-1], weights, frames_local, 0, (places, stacks, fixed))
    extras = (outs[0], outs[2], outs[4])
    queries = [group[0] for group in projected[:2]]
    keys = [*(group[-2] for group in projected), outs[1]]
    values = [*(group[-1] for group in projected), outs[3]]

    far = list(range(2, parts, 2))
    outs = attend_far(
        places, query_slots, far, bounds, (queries, keys, values), extras, frames_local
    )
    windows, shared = outs[: 2 * len(far)], outs[2 * len(far) :]
    windows = [
        exchange(block, "mp", 1) if number % 2 else block for number, block in enumerate(windows)
    ]
    w_rows = (w_output, w_near)
    shares = far_branch(windows, w_rows)
    mine, other = attend_near(places, shares[0], *shared, frames_local)
    shares = [exchange(share, "mp", bit) for share, bit in zip(shares, far)]
    base = near_branch(
        places, (mine, exchange(other, "mp", 1)), w_rows, stacks, fixed, weights[0], frames_local
    )
    return finish_rows(base, shares, gain_convolution[None, :], w_depthwise, frames_local)


def solution(mesh):
    placed = (
        P(("groups", "tm", "mp")),
        P(("groups", "tm")),
        P(("groups", "tm")),
        P(),
        P(None, None, "mp"),
        P("mp", None),
        P(),
        P(),
    )
    return jax.shard_map(
        shards,
        mesh=mesh,
        in_specs=placed,
        out_specs=P(("groups", "tm", "mp"), None),
        check_vma=False,
    )
```

```python
import math

import jax
import jax.numpy as jnp
import ml_dtypes
import numpy as np
from jax import lax
from jax.experimental import pallas as pl
from jax.experimental.pallas import tpu as pltpu
from jax.sharding import PartitionSpec as P

HD = 64
NMEL = 128
NFFT = 400
HOP = 160
BINS = 256
SUB = 4
KERNEL = 31
SEG_MAX = 750
LANES = 128
HALO = 16
EXTRA = 8
FLOPS_PER_MICRO = 2000000000
TAIL_LINES = 3
HEAD_LINES = 2
DIGIT = 128
FRAME_ROWS = SUB * HOP // LANES
WIDE = -(-NFFT // LANES) * LANES


def split_high_low(table):
    high = table.astype(ml_dtypes.bfloat16)
    low = (table - high.astype(np.float32)).astype(ml_dtypes.bfloat16)
    return high, low


def fourier_table():
    sample_index = np.arange(NFFT)[:, None]
    bin_index = np.arange(BINS)[None, :]
    angle = (sample_index * bin_index % NFFT) * (2.0 * math.pi / NFFT)
    window = 0.5 - 0.5 * np.cos(np.arange(NFFT) * (2.0 * math.pi / NFFT))
    kept = bin_index <= NFFT // 2
    cosine = np.where(kept, np.cos(angle), 0.0) * window[:, None]
    sine = np.where(kept, -np.sin(angle), 0.0) * window[:, None]
    table = np.concatenate([cosine, sine], axis=1).astype(np.float32)
    return np.pad(table, ((0, WIDE - NFFT), (0, 0)))


def mel_bank():
    mel_top = 2595.0 * math.log10(1.0 + 8000.0 / 700.0)
    mel_points = np.arange(NMEL + 2) * (mel_top / (NMEL + 1))
    edges = 700.0 * (np.power(10.0, mel_points / 2595.0) - 1.0) * (NFFT / 16000.0)
    widths = np.maximum(edges[2:] - edges[1:-1], 1.0)
    bin_value = np.arange(BINS)[:, None]
    triangle = np.maximum(0.0, 1.0 - np.abs(bin_value - edges[None, 1:-1]) / widths[None, :])
    return np.where(bin_value <= NFFT // 2, triangle, 0.0).astype(np.float32)


def front_tables():
    high, low = split_high_low(fourier_table())
    bank = np.concatenate(split_high_low(mel_bank()), axis=0)
    return np.concatenate([high, low, bank], axis=1)


def dot32(left, right):
    return jnp.dot(left, right, preferred_element_type=jnp.float32)


def dot_split(values, table_high, table_low):
    high = values.astype(jnp.bfloat16)
    low = (values - high.astype(jnp.float32)).astype(jnp.bfloat16)
    table = table_high()
    large, small = dot32(high, table), dot32(low, table)
    return large + (small + dot32(high, table_low()))


def normalize(values):
    center = jnp.mean(values, axis=-1, keepdims=True)
    shifted = values - center
    spread = jnp.mean(jnp.square(shifted), axis=-1, keepdims=True)
    return shifted * lax.rsqrt(spread + 1e-05)


def call(
    kernel, out_shape, operands, scratch=(), micros=1.0, remote=0, vmem=16, result=pltpu.VMEM
):
    specs = [pl.BlockSpec(memory_space=pltpu.VMEM)] * (len(operands) - remote)
    specs += [pl.BlockSpec(memory_space=pltpu.HBM)] * remote
    return pl.pallas_call(
        kernel,
        out_shape=out_shape,
        in_specs=specs,
        out_specs=jax.tree.map(lambda _: pl.BlockSpec(memory_space=result), out_shape),
        scratch_shapes=list(scratch),
        compiler_params=pltpu.CompilerParams(vmem_limit_bytes=vmem * 1024 * 1024),
        cost_estimate=pl.CostEstimate(
            flops=int(micros * FLOPS_PER_MICRO), bytes_accessed=1000000, transcendentals=0
        ),
    )(*operands)


def fetch(stacked, w_subsample, w_attention):
    parts, _, width = w_attention.shape

    def kernel(stack_ref, w_sub, w_att, out_sub, out_att, sums, out_stack, sems):
        out_stack[...] = stack_ref[...]
        copies = [
            pltpu.make_async_copy(w_att, out_att, sems.at[0]),
            pltpu.make_async_copy(w_sub, out_sub, sems.at[1]),
        ]
        for copy in copies:
            copy.start()
        for copy in copies:
            copy.wait()
        sums[...] = jnp.zeros_like(sums)
        for part in range(parts):
            columns = out_att[part].astype(jnp.float32)
            sums[part : part + 1, :] = jnp.sum(columns, axis=0, keepdims=True)

    return call(
        kernel,
        [jax.ShapeDtypeStruct(array.shape, array.dtype) for array in (w_subsample, w_attention)]
        + [
            jax.ShapeDtypeStruct((8, width), jnp.float32),
            jax.ShapeDtypeStruct(stacked.shape, stacked.dtype),
        ],
        (stacked, w_subsample, w_attention),
        scratch=[pltpu.SemaphoreType.DMA((2,))],
        remote=2,
    )


def padded_row(row):
    return jnp.concatenate([row, jnp.zeros((1, SUB * NMEL - row.shape[1]), row.dtype)], axis=1)


def log_mel(windows, tables, copies=()):
    wide, bank = 2 * BINS, slice(4 * BINS, 4 * BINS + NMEL)

    def fetched(number, rows, columns):
        def load():
            if copies:
                copies[number].wait()
            return tables[rows, columns]

        return load

    every = slice(None)
    spectrum = dot_split(
        windows, fetched(0, every, slice(0, wide)), fetched(1, every, slice(wide, 2 * wide))
    )
    power = jnp.square(spectrum[:, :BINS]) + jnp.square(spectrum[:, BINS:])
    bank_high = fetched(2, slice(0, BINS), bank)
    return jnp.log(dot_split(power, bank_high, lambda: tables[BINS:, bank]) + 1e-06)


def log_mel_rows(starts, ends, samples, tables, frames_local):
    rows = frames_local * FRAME_ROWS
    frames_shard = starts.shape[1]

    wide = 2 * BINS
    spans = (slice(0, wide), slice(wide, 2 * wide), slice(2 * wide, tables.shape[1]))

    def kernel(start, end, wave, table, out, held, start_ref, end_ref, tables_ref, sems):
        pairs = (
            (wave, held.at[pl.ds(0, rows)]),
            (start, start_ref),
            (end, end_ref),
        ) + tuple((table.at[:, span], tables_ref.at[:, span]) for span in spans)
        copies = [
            pltpu.make_async_copy(source, target, sems.at[slot])
            for slot, (source, target) in enumerate(pairs)
        ]
        for copy in copies:
            copy.start()
        held[rows : rows + 8, :] = jnp.zeros((8, LANES), jnp.float32)
        for copy in copies[:3]:
            copy.wait()
        lines = [held[pl.ds(j, frames_local, stride=FRAME_ROWS), :] for j in range(FRAME_ROWS + 2)]
        windows = []
        for sub in range(SUB):
            line, lane = divmod(sub * HOP, LANES)
            taken = jnp.concatenate(lines[line : line + WIDE // LANES], axis=1)
            windows.append(pltpu.roll(taken, WIDE - lane, axis=1) if lane else taken)
        extras = []
        for taken in (range(rows - TAIL_LINES, rows), range(HEAD_LINES)):
            line = jnp.concatenate([held[row : row + 1, :] for row in taken], axis=1)
            high = line.astype(jnp.bfloat16).astype(jnp.float32)
            extras += [padded_row(high), padded_row(line - high)]
        for ref in (start_ref, end_ref):
            edge = jnp.concatenate([ref[:, :HALO], ref[:, frames_shard - HALO :]], axis=1)
            high = edge // DIGIT
            low = edge - high * DIGIT
            extras += [padded_row(digit.astype(jnp.float32)) for digit in (high, low)]
        out[0, frames_local:, :] = jnp.concatenate(extras, axis=0).astype(jnp.bfloat16)
        mel = log_mel(jnp.concatenate(windows, axis=0), tables_ref, copies[3:])
        for sub in range(SUB):
            out[0, 0:frames_local, sub * NMEL : (sub + 1) * NMEL] = mel[
                sub * frames_local : (sub + 1) * frames_local
            ].astype(jnp.bfloat16)

    return call(
        kernel,
        jax.ShapeDtypeStruct((1, frames_local + EXTRA, SUB * NMEL), jnp.bfloat16),
        (starts, ends, samples, tables),
        scratch=[
            pltpu.VMEM((rows + 8, LANES), jnp.float32),
            pltpu.VMEM(starts.shape, starts.dtype),
            pltpu.VMEM(ends.shape, ends.dtype),
            pltpu.VMEM(tables.shape, tables.dtype),
            pltpu.SemaphoreType.DMA((6,)),
        ],
        remote=4,
        vmem=54,
        micros=1.0,
    )


def boundary_rows(places, starts, ends, stacks, tables, frames_local):
    counts = [stack.shape[0] for stack in stacks]
    slots = len(places)
    rows = -(-slots // HALO) * HALO
    frames_shard = starts.shape[1]
    parts = lax.axis_size("mp")
    final = lax.axis_size("tm") * parts - 1
    shift = final + 1

    def kernel(start_ref, end_ref, *refs):
        stack_refs, refs = refs[: len(counts)], refs[len(counts) :]
        tables_ref, out, bounds, tails, heads, nexts, edges, order = refs
        time_index, model_index = lax.axis_index("tm"), lax.axis_index("mp")
        tails[...] = jnp.zeros_like(tails)
        nexts[...] = jnp.zeros_like(nexts)
        slot = 0
        for stack_ref, count in zip(stack_refs, counts):
            for block in range(count):
                kept = stack_ref[block, frames_local:, :].astype(jnp.float32)
                here = slice(slot, slot + 1)
                tails[here, :] = (kept[0:1] + kept[1:2])[:, : TAIL_LINES * LANES]
                heads[here, :] = (kept[2:3] + kept[3:4])[:, : HEAD_LINES * LANES]
                for line in range(2):
                    edge = kept[4 + 2 * line : 5 + 2 * line] * DIGIT + kept[5 + 2 * line : 6 + 2 * line]
                    edges[line, here, :] = edge[:, :LANES]
                slot += 1
        numbers = [
            slot_tm(time_index) * parts + (model_index ^ slot_mp) for slot_tm, slot_mp in places
        ]
        for number in numbers:
            order[number + 1 + shift] = jnp.int32(0)
        for slot, number in enumerate(numbers):
            order[number + shift] = jnp.int32(slot)
        for slot, number in enumerate(numbers):
            taken = heads[pl.ds(order[number + 1 + shift], 1), :]
            nexts[slot : slot + 1, :] = jnp.where(number == final, 0.0, taken)
        line = jnp.concatenate([tails[...], nexts[...]], axis=1)
        windows = []
        for sub in range(SUB - 2, SUB):
            skip, lane = divmod(sub * HOP - (FRAME_ROWS - TAIL_LINES) * LANES, LANES)
            windows.append(
                pltpu.roll(line[:, skip * LANES : skip * LANES + WIDE], WIDE - lane, axis=1)
            )
        mel = log_mel(jnp.concatenate(windows, axis=0), tables_ref).astype(jnp.bfloat16)
        for number in range(2):
            lane = number * NMEL
            out[:, lane : lane + NMEL] = mel[number * rows : (number + 1) * rows]
        left = slot_of(places, time_index - 1, model_index)
        right = slot_of(places, time_index + 1, model_index)
        for number, ref in enumerate((start_ref, end_ref)):
            bounds[number : number + 1, :] = jnp.concatenate(
                [
                    edges[number, pl.ds(left, 1), :][:, HALO : 2 * HALO],
                    ref[...].astype(jnp.float32),
                    edges[number, pl.ds(right, 1), :][:, 0:HALO],
                ],
                axis=1,
            )

    return call(
        kernel,
        (
            jax.ShapeDtypeStruct((rows, 2 * NMEL), jnp.bfloat16),
            jax.ShapeDtypeStruct((2, frames_shard + 2 * HALO), jnp.float32),
        ),
        (starts, ends, *stacks, tables),
        scratch=[
            pltpu.VMEM((rows, TAIL_LINES * LANES), jnp.float32),
            pltpu.VMEM((rows, HEAD_LINES * LANES), jnp.float32),
            pltpu.VMEM((rows, HEAD_LINES * LANES), jnp.float32),
            pltpu.VMEM((2, rows, LANES), jnp.float32),
            pltpu.SMEM((3 * shift,), jnp.int32),
        ],
        micros=0.9,
    )


def last_rows(stack_refs, counts, frames_local, fixed, rows):
    lasts = []
    for stack_ref, count in zip(stack_refs, counts):
        for block in range(count):
            kept = stack_ref[block, frames_local - HALO : frames_local, 0 : 2 * NMEL]
            lasts.append(kept.astype(jnp.float32)[HALO - 1 : HALO])
    if len(lasts) < rows:
        lasts.append(jnp.zeros((rows - len(lasts), 2 * NMEL), jnp.float32))
    return jnp.concatenate([jnp.concatenate(lasts, axis=0).astype(jnp.bfloat16), fixed], axis=1)


def patch(held, fixed, slots, frames_local):
    fixed = fixed.astype(jnp.float32)
    for number, slot in enumerate(slots):
        here = slice((number + 1) * frames_local - HALO, (number + 1) * frames_local)
        kept = held[here, :].astype(jnp.float32)
        last = lax.broadcasted_iota(jnp.int32, kept.shape, 0) == HALO - 1
        held[here, :] = jnp.where(last, fixed[slot : slot + 1, :], kept).astype(held.dtype)


def assemble(parts, after=()):
    counts = [part.shape[0] for part in parts]

    def kernel(*refs):
        begin = 0
        for ref, count in zip(refs, counts):
            refs[-1][begin : begin + count] = ref[...]
            begin += count

    shape = jax.ShapeDtypeStruct((sum(counts), *parts[0].shape[1:]), parts[0].dtype)
    return call(kernel, shape, (*parts, *after))


def slot_of(places, tm, mp):
    found = jnp.int32(0)
    for slot, (slot_tm, slot_mp) in enumerate(places):
        here = (slot_tm(lax.axis_index("tm")) == tm) & (lax.axis_index("mp") ^ slot_mp == mp)
        found = jnp.where(here, slot, found)
    return found


def project_rows(stack, weights, frames_local, query_blocks, boundary=None):
    count = stack.shape[0]
    rows, width = count * frames_local, weights[1].shape[2]
    query_rows = query_blocks * frames_local
    places, every, fixed = boundary or ((), (), jnp.zeros((0, 2 * NMEL), jnp.bfloat16))
    counts = [block.shape[0] for block in every]
    last_count = fixed.shape[0]
    extra_rows = last_count + 2 * HALO if boundary else 0

    def boundary_stack(every_refs, fixed_ref, lasts, heads, tails):
        lasts[...] = last_rows(
            every_refs, counts, frames_local, fixed_ref[...], last_count
        ).astype(jnp.float32)
        slot = 0
        for ref, blocks in zip(every_refs, counts):
            for block in range(blocks):
                heads[slot] = ref[block, 0:HALO, :]
                tails[slot] = ref[block, frames_local - HALO : frames_local, :]
                slot += 1
        time_index, parts = lax.axis_index("tm"), lax.axis_size("mp")
        left = slot_of(places, time_index - 1, parts - 1)
        right = slot_of(places, time_index + 1, 0)
        tail = tails[left].astype(jnp.float32)
        final = lax.broadcasted_iota(jnp.int32, tail.shape, 0) == HALO - 1
        tail = jnp.where(final, lasts[pl.ds(left, 1), :], tail).astype(jnp.bfloat16)
        return [lasts[...].astype(jnp.bfloat16), tail, heads[right]]

    def kernel(stack_ref, w_sub, w_att, sums, *refs):
        stack_rows = [stack_ref[block, 0:frames_local, :] for block in range(count)]
        if boundary:
            every_refs, refs = refs[: len(every)], refs[len(every) :]
            fixed_ref, *refs = refs
            refs, scratch = refs[:-3], refs[-3:]
            stack_rows += boundary_stack(every_refs, fixed_ref, *scratch)
        features = dot32(jnp.concatenate(stack_rows, axis=0), w_sub[...]).astype(jnp.bfloat16)
        wide = features.astype(jnp.float32)
        center = jnp.mean(wide, axis=-1, keepdims=True)
        spread = jnp.mean(jnp.square(wide - center), axis=-1, keepdims=True)
        scale = lax.rsqrt(spread + 1e-05)

        def projected(part, begin, end):
            product = dot32(features[begin:end], w_att[part])
            shifted = product - center[begin:end] * sums[part : part + 1, :]
            return (shifted * scale[begin:end]).astype(jnp.bfloat16)

        refs = list(refs)
        if query_rows:
            refs.pop(0)[...] = projected(0, 0, query_rows)
        if extra_rows:
            refs.pop(0)[...] = projected(0, rows, rows + extra_rows)
        for part in (1, 2):
            both = projected(part, 0, rows + extra_rows)
            refs.pop(0)[...] = both[:rows]
            if extra_rows:
                refs.pop(0)[...] = both[rows:]

    def shape(size):
        return jax.ShapeDtypeStruct((size, width), jnp.bfloat16)

    shapes = [shape(query_rows)] * bool(query_rows) + [shape(extra_rows)] * bool(extra_rows)
    shapes += ([shape(rows)] + [shape(extra_rows)] * bool(extra_rows)) * 2
    depth = stack.shape[2]
    return call(
        kernel,
        shapes,
        (stack, *weights, *every) + ((fixed,) if boundary else ()),
        scratch=[
            pltpu.VMEM((last_count, depth), jnp.float32),
            pltpu.VMEM((len(places), HALO, depth), jnp.bfloat16),
            pltpu.VMEM((len(places), HALO, depth), jnp.bfloat16),
        ]
        if boundary
        else [],
        micros=0.5 + 0.006 * (rows + extra_rows),
    )


def gather_rows(places, query_slots, bounds, sources, extras, frames_local, outs):
    q_rows, k_all, v_all, q_all, first, last = outs
    parts = lax.axis_size("mp")
    frames_shard = frames_local * parts
    last_count = extras[0].shape[0] - 2 * HALO
    slots = range(len(places))
    for held, group, extra, held_slots in zip(
        (q_all, k_all, v_all), sources, extras, (query_slots, slots, slots)
    ):
        begin = 0
        for source in group:
            held[begin : begin + source.shape[0], :] = source[...]
            begin += source.shape[0]
        patch(held, extra[0:last_count, :], held_slots, frames_local)
    query_places = [places[slot] for slot in query_slots]
    q_rows[0:HALO, :] = extras[0][last_count : last_count + HALO, :]
    for part in range(parts):
        begin = HALO + part * frames_local
        slot = slot_of(query_places, lax.axis_index("tm"), part)
        start = pl.multiple_of(slot * frames_local, HALO)
        q_rows[begin : begin + frames_local, :] = q_all[pl.ds(start, frames_local), :]
    q_rows[HALO + frames_shard :, :] = extras[0][last_count + HALO :, :]
    for line, ref in enumerate((first, last)):
        row = bounds[line : line + 1, :]
        ref[...] = jnp.transpose(jnp.broadcast_to(row, (LANES, row.shape[1])))


def attend_rows(places, begin, q_rows, k_all, v_all, first, last, frames_local, result, bias):
    count, width = result.shape
    rows = k_all.shape[0]
    time_index, model_index = lax.axis_index("tm"), lax.axis_index("mp")
    frames_shard = frames_local * lax.axis_size("mp")
    lows, highs = first[pl.ds(begin, count), :], last[pl.ds(begin, count), :]
    lanes = lax.broadcasted_iota(jnp.int32, (1, LANES), 1)
    for lane in range(0, rows, LANES):
        at = jnp.zeros((1, LANES), jnp.int32)
        for slot in range(lane // frames_local, -(-(lane + LANES) // frames_local)):
            if slot < len(places):
                slot_tm, slot_mp = places[slot]
                base = slot_tm(time_index) * frames_shard
                base += (model_index ^ slot_mp) * frames_local - slot * frames_local + lane
                at = jnp.where(lanes >= slot * frames_local - lane, lanes + base, at)
        at = at.astype(jnp.float32)
        bias[:, lane : lane + LANES] = jnp.where((at >= lows) & (at < highs), 0.0, -1e30)
    for lane in range(0, width, LANES):
        span = min(LANES, width - lane)
        q_pair = q_rows[pl.ds(begin, count), lane : lane + span]
        k_pair = k_all[:, lane : lane + span]
        v_pair = v_all[:, lane : lane + span]
        heads = span // HD
        head_of = lax.broadcasted_iota(jnp.int32, (count, span), 1) // HD
        scaled = q_pair * jnp.bfloat16(1.0 / math.sqrt(HD))
        stacked = jnp.concatenate(
            [jnp.where(head_of == head, scaled, jnp.zeros_like(scaled)) for head in range(heads)],
            axis=0,
        )
        scores = lax.dot_general(
            stacked, k_pair, (((1,), (1,)), ((), ())), preferred_element_type=jnp.float32
        )
        scores = scores + jnp.concatenate([bias[...]] * heads, axis=0)
        weights = jnp.exp(scores - jnp.max(scores, axis=1, keepdims=True))
        total = jnp.sum(weights, axis=1, keepdims=True)
        ratio = dot32(weights.astype(jnp.bfloat16), v_pair) / total
        merged = ratio[0:count]
        for head in range(1, heads):
            merged = jnp.where(head_of == head, ratio[head * count : (head + 1) * count], merged)
        result[:, lane : lane + span] = merged.astype(jnp.bfloat16)


def split_pair(model_index, result, mine, other, frames_local):
    window = mine.shape[0]
    place = lax.rem(model_index, 2) * frames_local
    mine[...] = result[pl.ds(pl.multiple_of(place, HALO), window), :]
    place = frames_local - place
    other[...] = result[pl.ds(pl.multiple_of(place, HALO), window), :]


def attend_far(places, query_slots, far, bounds, sources, extras, frames_local):
    width = sources[0][0].shape[1]
    query_count, rows = (sum(group.shape[0] for group in groups) for groups in sources[:2])
    sizes = [len(groups) for groups in sources]
    extended = frames_local * lax.axis_size("mp") + 2 * HALO
    window = frames_local + 2 * HALO
    pair = 2 * frames_local + 2 * HALO

    def kernel(bound_ref, *refs):
        groups = []
        for size in sizes:
            groups.append(refs[:size])
            refs = refs[size:]
        extra_refs, refs = refs[:3], refs[3:]
        windows, refs = refs[: 2 * len(far)], refs[2 * len(far) :]
        q_rows, k_all, v_all, first, last, q_all, result, bias = refs
        gather_rows(
            places,
            query_slots,
            bound_ref,
            groups,
            extra_refs,
            frames_local,
            (q_rows, k_all, v_all, q_all, first, last),
        )
        model_index = lax.axis_index("mp")
        for number, bit in enumerate(far):
            begin = pl.multiple_of((model_index ^ bit) // 2 * (2 * frames_local), HALO)
            attend_rows(
                places, begin, q_rows, k_all, v_all, first, last, frames_local, result, bias
            )
            split_pair(
                model_index, result, windows[2 * number], windows[2 * number + 1], frames_local
            )

    def shape(count, wide=width, dtype=jnp.bfloat16):
        return jax.ShapeDtypeStruct((count, wide), dtype)

    return call(
        kernel,
        [shape(window)] * (2 * len(far))
        + [shape(extended), shape(rows), shape(rows)]
        + [shape(extended, LANES, jnp.float32)] * 2,
        (bounds, *(array for groups in sources for array in groups), *extras),
        scratch=[
            pltpu.VMEM((query_count, width), jnp.bfloat16),
            pltpu.VMEM((pair, width), jnp.bfloat16),
            pltpu.VMEM((pair, rows), jnp.float32),
        ],
        micros=2.5 * len(far),
        vmem=16 + pair * rows * 20 // 1024 // 1024,
    )


def attend_near(places, after, q_rows, k_all, v_all, first, last, frames_local):
    rows, width = k_all.shape
    window = frames_local + 2 * HALO
    pair = 2 * frames_local + 2 * HALO

    def kernel(_, q_ref, k_ref, v_ref, first_ref, last_ref, mine, other, result, bias):
        model_index = lax.axis_index("mp")
        begin = pl.multiple_of(model_index // 2 * (2 * frames_local), HALO)
        attend_rows(
            places, begin, q_ref, k_ref, v_ref, first_ref, last_ref, frames_local, result, bias
        )
        split_pair(model_index, result, mine, other, frames_local)

    return call(
        kernel,
        [jax.ShapeDtypeStruct((window, width), jnp.bfloat16)] * 2,
        (after, q_rows, k_all, v_all, first, last),
        scratch=[
            pltpu.VMEM((pair, width), jnp.bfloat16),
            pltpu.VMEM((pair, rows), jnp.float32),
        ],
        micros=1.0,
        vmem=16 + pair * rows * 20 // 1024 // 1024,
    )


def far_branch_own(windows, w_own):
    count = len(windows)

    def kernel(*refs):
        for window, out in zip(refs[:count], refs[count + 1 :]):
            out[...] = dot32(window[...], refs[count][...])

    shape = jax.ShapeDtypeStruct((windows[0].shape[0], w_own.shape[1]), jnp.float32)
    return call(kernel, [shape] * count, (*windows, w_own), micros=0.4 * count)


def far_branch(shares, windows, w_near, cut):
    count = len(windows)

    def kernel(*refs):
        share_refs, window_refs, near, outs = (
            refs[:count],
            refs[count : 2 * count],
            refs[2 * count],
            refs[2 * count + 1 :],
        )
        for number, (share, window) in enumerate(zip(share_refs, window_refs)):
            total = (share[...] + dot32(window[...], near[...])).astype(jnp.bfloat16)
            outs[2 * number][...] = total[:cut]
            outs[2 * number + 1][...] = total[cut:]

    sizes = [cut, windows[0].shape[0] - cut] * count
    shapes = [jax.ShapeDtypeStruct((size, w_near.shape[1]), jnp.bfloat16) for size in sizes]
    return call(kernel, shapes, (*shares, *windows, w_near), micros=0.5 * count)


def near_branch(places, windows, w_rows, stacks, fixed, w_subsample, frames_local):
    counts = [stack.shape[0] for stack in stacks]
    depth, model = w_subsample.shape
    window = frames_local + 2 * HALO
    slots = len(places)

    def kernel(own, near, w_own, w_near, *refs):
        stack_refs, (fixed_ref, w_sub, out, held, taken) = refs[: len(counts)], refs[len(counts) :]
        begin = 0
        for stack_ref, count in zip(stack_refs, counts):
            for block in range(count):
                held[begin : begin + frames_local, :] = stack_ref[block, 0:frames_local, :]
                begin += frames_local
        rows = last_rows(stack_refs, counts, frames_local, fixed_ref[...], fixed.shape[0])
        patch(held, rows, range(slots), frames_local)
        parts = lax.axis_size("mp")
        block = lax.axis_index("tm") * parts + lax.axis_index("mp") + parts

        def source(number, offset, count):
            slot = slot_of(places, number // parts - 1, lax.rem(number, parts))
            start = pl.multiple_of(slot * frames_local + offset, HALO)
            return held[pl.ds(start, count), :]

        taken[0:HALO, :] = source(block - 1, frames_local - HALO, HALO)
        taken[HALO : HALO + frames_local, :] = source(block, 0, frames_local)
        taken[HALO + frames_local : window, :] = source(block + 1, 0, HALO)
        features = dot32(taken[...], w_sub[...]).astype(jnp.bfloat16).astype(jnp.float32)
        share = dot32(own[...], w_own[...]) + dot32(near[...], w_near[...])
        out[...] = features + share

    return call(
        kernel,
        jax.ShapeDtypeStruct((window, model), jnp.float32),
        (*windows, *w_rows, *stacks, fixed, w_subsample),
        scratch=[
            pltpu.VMEM((slots * frames_local, depth), jnp.bfloat16),
            pltpu.VMEM((window, depth), jnp.bfloat16),
        ],
        micros=0.6,
    )


def convolve(held, taps, begin, count, here):
    offset = HALO - KERNEL // 2
    reach = count + 8
    rows = held[begin : begin + count + 2 * HALO, here]
    tap_rows = taps[:, here].astype(jnp.float32)
    total = jnp.zeros((count, rows.shape[1]), jnp.float32)
    for phase in range(8):
        share = jnp.zeros((reach, rows.shape[1]), jnp.float32)
        for tap in range(KERNEL):
            if (tap + offset) % 8 == phase:
                first = (tap + offset) // 8 * 8
                share += rows[first : first + reach] * tap_rows[tap : tap + 1]
        moved = pltpu.roll(share, reach - phase, axis=0) if phase else share
        total += moved[0:count]
    return total


def mix(base, shares, gain):
    mixed = base
    for share in shares:
        mixed += share[...].astype(jnp.float32)
    mixed = mixed.astype(jnp.bfloat16).astype(jnp.float32)
    return mixed, (normalize(mixed) * gain[...]).astype(jnp.bfloat16).astype(jnp.float32)


def silu(values):
    return values / (1.0 + jnp.exp(-values))


def finish_first(base, shares, gain, taps):
    count = len(shares)
    cut, model = shares[0].shape
    done = cut - 2 * HALO
    chunk = 2 * LANES

    def kernel(base_ref, *refs):
        share_refs, (gain_ref, tap_ref, out, held, mixed_rows) = refs[:count], refs[count:]
        mixed, conv_in = mix(base_ref[0:cut, :], share_refs, gain_ref)
        mixed_rows[...] = mixed
        held[...] = conv_in
        before = lax.axis_index("tm") * lax.axis_size("mp") + lax.axis_index("mp") > 0
        held[0:HALO, :] = jnp.where(before, conv_in[0:HALO], 0.0)
        for lane in range(0, model, chunk):
            here = slice(lane, lane + chunk)
            total = convolve(held, tap_ref, 0, done, here)
            out[:, here] = (mixed_rows[HALO : HALO + done, here] + silu(total)).astype(jnp.bfloat16)

    rows = jax.ShapeDtypeStruct((cut, model), jnp.float32)
    return call(
        kernel,
        (jax.ShapeDtypeStruct((done, model), jnp.bfloat16), rows, rows),
        (base, *shares, gain, taps),
        micros=0.5,
    )


def finish_last(base, shares, first, gain, taps, frames_local):
    count = len(shares)
    window, model = base.shape
    cut, done = first[1].shape[0], first[0].shape[0]
    left = frames_local - done
    chunk = 2 * LANES
    chunks = model // chunk

    def kernel(base_ref, *refs):
        share_refs, refs = refs[:count], refs[count:]
        out_ref, held_ref, mixed_ref, gain_ref, tap_ref, result, held, mixed_rows, staged, sems = refs
        copies = [pltpu.make_async_copy(out_ref, result.at[pl.ds(0, done)], sems.at[chunks])]
        copies[0].start()
        mixed, conv_in = mix(base_ref[cut:window, :], share_refs, gain_ref)
        mixed_rows[0:cut, :] = mixed_ref[...]
        mixed_rows[cut:window, :] = mixed
        held[0:cut, :] = held_ref[...]
        held[cut:window, :] = conv_in
        parts = lax.axis_size("mp")
        block = lax.axis_index("tm") * parts + lax.axis_index("mp")
        after = block < lax.axis_size("tm") * parts - 1
        held[window - HALO : window, :] = jnp.where(after, conv_in[window - HALO - cut :], 0.0)
        for number in range(chunks):
            here = slice(number * chunk, (number + 1) * chunk)
            total = convolve(held, tap_ref, done, left, here)
            kept = mixed_rows[HALO + done : HALO + frames_local, here]
            staged[:, here] = (kept + silu(total)).astype(jnp.bfloat16)
            copies.append(
                pltpu.make_async_copy(
                    staged.at[:, here], result.at[pl.ds(done, left), here], sems.at[number]
                )
            )
            copies[-1].start()
        for copy in copies:
            copy.wait()

    return call(
        kernel,
        jax.ShapeDtypeStruct((frames_local, model), jnp.bfloat16),
        (base, *shares, *first, gain, taps),
        scratch=[
            pltpu.VMEM((window, model), jnp.float32),
            pltpu.VMEM((window, model), jnp.float32),
            pltpu.VMEM((left, model), jnp.bfloat16),
            pltpu.SemaphoreType.DMA((chunks + 1,)),
        ],
        micros=1.5,
        result=pltpu.HBM,
    )


def exchange(block, axis, bit):
    return lax.ppermute(block, axis, [(i, i ^ bit) for i in range(lax.axis_size(axis))])


def shifted(block, axis, distance):
    count = lax.axis_size(axis)
    route = [(i - distance, i) for i in range(count) if 0 <= i - distance < count]
    return lax.ppermute(block, axis, route)


def shards(
    waveform,
    segment_start,
    segment_end,
    w_subsample,
    w_attention,
    w_output,
    gain_convolution,
    w_depthwise,
):
    frames_local = waveform.shape[0] // (SUB * HOP)
    frames_shard = segment_start.shape[0]
    parts, shards_total = lax.axis_size("mp"), lax.axis_size("tm")
    bits = [1 << b for b in reversed(range((parts - 1).bit_length()))]

    samples = waveform.reshape(-1, LANES)
    starts, ends = segment_start[None, :], segment_end[None, :]
    tables = jnp.asarray(front_tables())
    stacked = log_mel_rows(starts, ends, samples, tables, frames_local)
    *weights, kept = fetch(stacked, w_subsample, w_attention)

    w_near = exchange(w_output, "mp", bits[-1])

    reach = min((SEG_MAX + HALO - 2) // frames_shard + 1, shards_total - 1)
    whole = reach == shards_total - 1 and shards_total & (shards_total - 1) == 0
    if whole:
        moves = [lambda tm, bit=bit: tm ^ bit for bit in range(1, shards_total)]
        column = [exchange(stacked, "tm", bit) for bit in range(1, shards_total)]
    else:
        steps = [sign * d for d in range(1, reach + 1) for sign in (1, -1)]
        moves = [lambda tm, step=step: tm - step for step in steps]
        column = [shifted(stacked, "tm", step) for step in steps]
    early = [(kept, [(lambda tm: tm, 0)])]
    late = [(assemble(column, weights[-1:]), [(move, 0) for move in moves])]

    def across(blocks, bit):
        return [
            (exchange(block, "mp", bit), [(move, mp ^ bit) for move, mp in held])
            for block, held in blocks
        ]

    for bit in bits[:-1]:
        early, late = early + across(early, bit), late + across(late, bit)
    ready = early + late[:1]
    joined = (assemble([block for block, _ in ready]), sum([held for _, held in ready], []))
    groups = [joined] + across([joined], bits[-1])
    projected = [
        project_rows(block, weights, frames_local, len(early)) for block, _ in groups
    ]
    done = [group[-1] for group in projected]
    late = [(assemble([block], done), held) for block, held in late[1:]]
    groups += late + across(late, bits[-1])
    stacks, held = zip(*groups)
    places = sum(held, [])
    joined_slots = range(len(joined[1]), 2 * len(joined[1]))
    query_slots = [*range(len(early)), *joined_slots[: len(early)]]
    fixed, bounds = boundary_rows(places, starts, ends, stacks, tables, frames_local)
    projected += [project_rows(block, weights, frames_local, 0) for block in stacks[2:-1]]
    outs = project_rows(stacks[-1], weights, frames_local, 0, (places, stacks, fixed))
    extras = (outs[0], outs[2], outs[4])
    queries = [group[0] for group in projected[:2]]
    keys = [*(group[-2] for group in projected), outs[1]]
    values = [*(group[-1] for group in projected), outs[3]]

    far = list(range(2, parts, 2))
    outs = attend_far(
        places, query_slots, far, bounds, (queries, keys, values), extras, frames_local
    )
    windows, shared = outs[: 2 * len(far)], outs[2 * len(far) :]
    arrived = [exchange(window, "mp", 1) for window in windows[1::2]]
    w_rows = (w_output, w_near)
    shares = far_branch_own(windows[0::2], w_output)
    shares = far_branch(shares, arrived, w_near, frames_local + HALO)
    mine, other = attend_near(places, shares[0], *shared, frames_local)
    shares = [exchange(share, "mp", far[number // 2]) for number, share in enumerate(shares)]
    base = near_branch(
        places, (mine, exchange(other, "mp", 1)), w_rows, stacks, fixed, weights[0], frames_local
    )
    gain = gain_convolution[None, :]
    first = finish_first(base, shares[0::2], gain, w_depthwise)
    return finish_last(base, shares[1::2], first, gain, w_depthwise, frames_local)


def solution(mesh):
    placed = (
        P(("groups", "tm", "mp")),
        P(("groups", "tm")),
        P(("groups", "tm")),
        P(),
        P(None, None, "mp"),
        P("mp", None),
        P(),
        P(),
    )
    return jax.shard_map(
        shards,
        mesh=mesh,
        in_specs=placed,
        out_specs=P(("groups", "tm", "mp"), None),
        check_vma=False,
    )
```

```python
import math

import jax
import jax.numpy as jnp
import ml_dtypes
import numpy as np
from jax import lax
from jax.experimental import pallas as pl
from jax.experimental.pallas import tpu as pltpu
from jax.sharding import PartitionSpec as P

HD = 64
NMEL = 128
NFFT = 400
HOP = 160
BINS = 256
SUB = 4
KERNEL = 31
SEG_MAX = 750
LANES = 128
HALO = 16
EXTRA = 8
FLOPS_PER_MICRO = 2000000000
TAIL_LINES = 3
HEAD_LINES = 2
DIGIT = 128
FRAME_ROWS = SUB * HOP // LANES
WIDE = -(-NFFT // LANES) * LANES


def split_high_low(table):
    high = table.astype(ml_dtypes.bfloat16)
    low = (table - high.astype(np.float32)).astype(ml_dtypes.bfloat16)
    return high, low


def fourier_table():
    sample_index = np.arange(NFFT)[:, None]
    bin_index = np.arange(BINS)[None, :]
    angle = (sample_index * bin_index % NFFT) * (2.0 * math.pi / NFFT)
    window = 0.5 - 0.5 * np.cos(np.arange(NFFT) * (2.0 * math.pi / NFFT))
    kept = bin_index <= NFFT // 2
    cosine = np.where(kept, np.cos(angle), 0.0) * window[:, None]
    sine = np.where(kept, -np.sin(angle), 0.0) * window[:, None]
    table = np.concatenate([cosine, sine], axis=1).astype(np.float32)
    return np.pad(table, ((0, WIDE - NFFT), (0, 0)))


def mel_bank():
    mel_top = 2595.0 * math.log10(1.0 + 8000.0 / 700.0)
    mel_points = np.arange(NMEL + 2) * (mel_top / (NMEL + 1))
    edges = 700.0 * (np.power(10.0, mel_points / 2595.0) - 1.0) * (NFFT / 16000.0)
    widths = np.maximum(edges[2:] - edges[1:-1], 1.0)
    bin_value = np.arange(BINS)[:, None]
    triangle = np.maximum(0.0, 1.0 - np.abs(bin_value - edges[None, 1:-1]) / widths[None, :])
    return np.where(bin_value <= NFFT // 2, triangle, 0.0).astype(np.float32)


def front_tables():
    high, low = split_high_low(fourier_table())
    bank = np.concatenate(split_high_low(mel_bank()), axis=0)
    return np.concatenate([high, low, bank], axis=1)


def dot32(left, right):
    return jnp.dot(left, right, preferred_element_type=jnp.float32)


def dot_split(values, table_high, table_low):
    high = values.astype(jnp.bfloat16)
    low = (values - high.astype(jnp.float32)).astype(jnp.bfloat16)
    table = table_high()
    large, small = dot32(high, table), dot32(low, table)
    return large + (small + dot32(high, table_low()))


def normalize(values):
    center = jnp.mean(values, axis=-1, keepdims=True)
    shifted = values - center
    spread = jnp.mean(jnp.square(shifted), axis=-1, keepdims=True)
    return shifted * lax.rsqrt(spread + 1e-05)


def call(
    kernel, out_shape, operands, scratch=(), micros=1.0, remote=0, vmem=16, result=pltpu.VMEM
):
    specs = [pl.BlockSpec(memory_space=pltpu.VMEM)] * (len(operands) - remote)
    specs += [pl.BlockSpec(memory_space=pltpu.HBM)] * remote
    return pl.pallas_call(
        kernel,
        out_shape=out_shape,
        in_specs=specs,
        out_specs=jax.tree.map(lambda _: pl.BlockSpec(memory_space=result), out_shape),
        scratch_shapes=list(scratch),
        compiler_params=pltpu.CompilerParams(vmem_limit_bytes=vmem * 1024 * 1024),
        cost_estimate=pl.CostEstimate(
            flops=int(micros * FLOPS_PER_MICRO), bytes_accessed=1000000, transcendentals=0
        ),
    )(*operands)


def fetch(stacked, w_subsample, w_attention):
    parts, _, width = w_attention.shape

    def kernel(stack_ref, w_sub, w_att, out_sub, out_att, sums, out_stack, sems):
        out_stack[...] = stack_ref[...]
        copies = [
            pltpu.make_async_copy(w_att, out_att, sems.at[0]),
            pltpu.make_async_copy(w_sub, out_sub, sems.at[1]),
        ]
        for copy in copies:
            copy.start()
        for copy in copies:
            copy.wait()
        sums[...] = jnp.zeros_like(sums)
        for part in range(parts):
            columns = out_att[part].astype(jnp.float32)
            sums[part : part + 1, :] = jnp.sum(columns, axis=0, keepdims=True)

    return call(
        kernel,
        [jax.ShapeDtypeStruct(array.shape, array.dtype) for array in (w_subsample, w_attention)]
        + [
            jax.ShapeDtypeStruct((8, width), jnp.float32),
            jax.ShapeDtypeStruct(stacked.shape, stacked.dtype),
        ],
        (stacked, w_subsample, w_attention),
        scratch=[pltpu.SemaphoreType.DMA((2,))],
        remote=2,
    )


def padded_row(row):
    return jnp.concatenate([row, jnp.zeros((1, SUB * NMEL - row.shape[1]), row.dtype)], axis=1)


def log_mel(windows, tables, copies=()):
    wide, bank = 2 * BINS, slice(4 * BINS, 4 * BINS + NMEL)

    def fetched(number, rows, columns):
        def load():
            if copies:
                copies[number].wait()
            return tables[rows, columns]

        return load

    every = slice(None)
    spectrum = dot_split(
        windows, fetched(0, every, slice(0, wide)), fetched(1, every, slice(wide, 2 * wide))
    )
    power = jnp.square(spectrum[:, :BINS]) + jnp.square(spectrum[:, BINS:])
    bank_high = fetched(2, slice(0, BINS), bank)
    return jnp.log(dot_split(power, bank_high, lambda: tables[BINS:, bank]) + 1e-06)


def log_mel_rows(starts, ends, samples, tables, frames_local):
    rows = frames_local * FRAME_ROWS
    frames_shard = starts.shape[1]

    wide = 2 * BINS
    spans = (slice(0, wide), slice(wide, 2 * wide), slice(2 * wide, tables.shape[1]))

    def kernel(start, end, wave, table, out, held, start_ref, end_ref, tables_ref, sems):
        pairs = (
            (wave, held.at[pl.ds(0, rows)]),
            (start, start_ref),
            (end, end_ref),
        ) + tuple((table.at[:, span], tables_ref.at[:, span]) for span in spans)
        copies = [
            pltpu.make_async_copy(source, target, sems.at[slot])
            for slot, (source, target) in enumerate(pairs)
        ]
        for copy in copies:
            copy.start()
        held[rows : rows + 8, :] = jnp.zeros((8, LANES), jnp.float32)
        for copy in copies[:3]:
            copy.wait()
        lines = [held[pl.ds(j, frames_local, stride=FRAME_ROWS), :] for j in range(FRAME_ROWS + 2)]
        windows = []
        for sub in range(SUB):
            line, lane = divmod(sub * HOP, LANES)
            taken = jnp.concatenate(lines[line : line + WIDE // LANES], axis=1)
            windows.append(pltpu.roll(taken, WIDE - lane, axis=1) if lane else taken)
        extras = []
        for taken in (range(rows - TAIL_LINES, rows), range(HEAD_LINES)):
            line = jnp.concatenate([held[row : row + 1, :] for row in taken], axis=1)
            high = line.astype(jnp.bfloat16).astype(jnp.float32)
            extras += [padded_row(high), padded_row(line - high)]
        for ref in (start_ref, end_ref):
            edge = jnp.concatenate([ref[:, :HALO], ref[:, frames_shard - HALO :]], axis=1)
            high = edge // DIGIT
            low = edge - high * DIGIT
            extras += [padded_row(digit.astype(jnp.float32)) for digit in (high, low)]
        out[0, frames_local:, :] = jnp.concatenate(extras, axis=0).astype(jnp.bfloat16)
        mel = log_mel(jnp.concatenate(windows, axis=0), tables_ref, copies[3:])
        for sub in range(SUB):
            out[0, 0:frames_local, sub * NMEL : (sub + 1) * NMEL] = mel[
                sub * frames_local : (sub + 1) * frames_local
            ].astype(jnp.bfloat16)

    return call(
        kernel,
        jax.ShapeDtypeStruct((1, frames_local + EXTRA, SUB * NMEL), jnp.bfloat16),
        (starts, ends, samples, tables),
        scratch=[
            pltpu.VMEM((rows + 8, LANES), jnp.float32),
            pltpu.VMEM(starts.shape, starts.dtype),
            pltpu.VMEM(ends.shape, ends.dtype),
            pltpu.VMEM(tables.shape, tables.dtype),
            pltpu.SemaphoreType.DMA((6,)),
        ],
        remote=4,
        vmem=54,
        micros=1.0,
    )


def boundary_rows(places, starts, ends, stacks, tables, frames_local):
    counts = [stack.shape[0] for stack in stacks]
    slots = len(places)
    rows = -(-slots // HALO) * HALO
    frames_shard = starts.shape[1]
    parts = lax.axis_size("mp")
    final = lax.axis_size("tm") * parts - 1
    shift = final + 1

    def kernel(start_ref, end_ref, *refs):
        stack_refs, refs = refs[: len(counts)], refs[len(counts) :]
        tables_ref, out, bounds, tails, heads, nexts, edges, order = refs
        time_index, model_index = lax.axis_index("tm"), lax.axis_index("mp")
        tails[...] = jnp.zeros_like(tails)
        nexts[...] = jnp.zeros_like(nexts)
        slot = 0
        for stack_ref, count in zip(stack_refs, counts):
            for block in range(count):
                kept = stack_ref[block, frames_local:, :].astype(jnp.float32)
                here = slice(slot, slot + 1)
                tails[here, :] = (kept[0:1] + kept[1:2])[:, : TAIL_LINES * LANES]
                heads[here, :] = (kept[2:3] + kept[3:4])[:, : HEAD_LINES * LANES]
                for line in range(2):
                    edge = kept[4 + 2 * line : 5 + 2 * line] * DIGIT + kept[5 + 2 * line : 6 + 2 * line]
                    edges[line, here, :] = edge[:, :LANES]
                slot += 1
        numbers = [
            slot_tm(time_index) * parts + (model_index ^ slot_mp) for slot_tm, slot_mp in places
        ]
        for number in numbers:
            order[number + 1 + shift] = jnp.int32(0)
        for slot, number in enumerate(numbers):
            order[number + shift] = jnp.int32(slot)
        for slot, number in enumerate(numbers):
            taken = heads[pl.ds(order[number + 1 + shift], 1), :]
            nexts[slot : slot + 1, :] = jnp.where(number == final, 0.0, taken)
        line = jnp.concatenate([tails[...], nexts[...]], axis=1)
        windows = []
        for sub in range(SUB - 2, SUB):
            skip, lane = divmod(sub * HOP - (FRAME_ROWS - TAIL_LINES) * LANES, LANES)
            windows.append(
                pltpu.roll(line[:, skip * LANES : skip * LANES + WIDE], WIDE - lane, axis=1)
            )
        mel = log_mel(jnp.concatenate(windows, axis=0), tables_ref).astype(jnp.bfloat16)
        for number in range(2):
            lane = number * NMEL
            out[:, lane : lane + NMEL] = mel[number * rows : (number + 1) * rows]
        left = slot_of(places, time_index - 1, model_index)
        right = slot_of(places, time_index + 1, model_index)
        for number, ref in enumerate((start_ref, end_ref)):
            bounds[number : number + 1, :] = jnp.concatenate(
                [
                    edges[number, pl.ds(left, 1), :][:, HALO : 2 * HALO],
                    ref[...].astype(jnp.float32),
                    edges[number, pl.ds(right, 1), :][:, 0:HALO],
                ],
                axis=1,
            )

    return call(
        kernel,
        (
            jax.ShapeDtypeStruct((rows, 2 * NMEL), jnp.bfloat16),
            jax.ShapeDtypeStruct((2, frames_shard + 2 * HALO), jnp.float32),
        ),
        (starts, ends, *stacks, tables),
        scratch=[
            pltpu.VMEM((rows, TAIL_LINES * LANES), jnp.float32),
            pltpu.VMEM((rows, HEAD_LINES * LANES), jnp.float32),
            pltpu.VMEM((rows, HEAD_LINES * LANES), jnp.float32),
            pltpu.VMEM((2, rows, LANES), jnp.float32),
            pltpu.SMEM((3 * shift,), jnp.int32),
        ],
        micros=0.9,
    )


def last_rows(stack_refs, counts, frames_local, fixed, rows):
    lasts = []
    for stack_ref, count in zip(stack_refs, counts):
        for block in range(count):
            kept = stack_ref[block, frames_local - HALO : frames_local, 0 : 2 * NMEL]
            lasts.append(kept.astype(jnp.float32)[HALO - 1 : HALO])
    if len(lasts) < rows:
        lasts.append(jnp.zeros((rows - len(lasts), 2 * NMEL), jnp.float32))
    return jnp.concatenate([jnp.concatenate(lasts, axis=0).astype(jnp.bfloat16), fixed], axis=1)


def patch(held, fixed, slots, frames_local):
    fixed = fixed.astype(jnp.float32)
    for number, slot in enumerate(slots):
        here = slice((number + 1) * frames_local - HALO, (number + 1) * frames_local)
        kept = held[here, :].astype(jnp.float32)
        last = lax.broadcasted_iota(jnp.int32, kept.shape, 0) == HALO - 1
        held[here, :] = jnp.where(last, fixed[slot : slot + 1, :], kept).astype(held.dtype)


def assemble(parts, after=()):
    counts = [part.shape[0] for part in parts]

    def kernel(*refs):
        begin = 0
        for ref, count in zip(refs, counts):
            refs[-1][begin : begin + count] = ref[...]
            begin += count

    shape = jax.ShapeDtypeStruct((sum(counts), *parts[0].shape[1:]), parts[0].dtype)
    return call(kernel, shape, (*parts, *after))


def slot_of(places, tm, mp):
    found = jnp.int32(0)
    for slot, (slot_tm, slot_mp) in enumerate(places):
        here = (slot_tm(lax.axis_index("tm")) == tm) & (lax.axis_index("mp") ^ slot_mp == mp)
        found = jnp.where(here, slot, found)
    return found


def project_rows(stack, weights, frames_local, query_blocks, boundary=None):
    count = stack.shape[0]
    rows, width = count * frames_local, weights[1].shape[2]
    query_rows = query_blocks * frames_local
    places, every, fixed = boundary or ((), (), jnp.zeros((0, 2 * NMEL), jnp.bfloat16))
    counts = [block.shape[0] for block in every]
    last_count = fixed.shape[0]
    extra_rows = last_count + 2 * HALO if boundary else 0

    def boundary_stack(every_refs, fixed_ref, lasts, heads, tails):
        lasts[...] = last_rows(
            every_refs, counts, frames_local, fixed_ref[...], last_count
        ).astype(jnp.float32)
        slot = 0
        for ref, blocks in zip(every_refs, counts):
            for block in range(blocks):
                heads[slot] = ref[block, 0:HALO, :]
                tails[slot] = ref[block, frames_local - HALO : frames_local, :]
                slot += 1
        time_index, parts = lax.axis_index("tm"), lax.axis_size("mp")
        left = slot_of(places, time_index - 1, parts - 1)
        right = slot_of(places, time_index + 1, 0)
        tail = tails[left].astype(jnp.float32)
        final = lax.broadcasted_iota(jnp.int32, tail.shape, 0) == HALO - 1
        tail = jnp.where(final, lasts[pl.ds(left, 1), :], tail).astype(jnp.bfloat16)
        return [lasts[...].astype(jnp.bfloat16), tail, heads[right]]

    def kernel(stack_ref, w_sub, w_att, sums, *refs):
        stack_rows = [stack_ref[block, 0:frames_local, :] for block in range(count)]
        if boundary:
            every_refs, refs = refs[: len(every)], refs[len(every) :]
            fixed_ref, *refs = refs
            refs, scratch = refs[:-3], refs[-3:]
            stack_rows += boundary_stack(every_refs, fixed_ref, *scratch)
        features = dot32(jnp.concatenate(stack_rows, axis=0), w_sub[...]).astype(jnp.bfloat16)
        wide = features.astype(jnp.float32)
        center = jnp.mean(wide, axis=-1, keepdims=True)
        spread = jnp.mean(jnp.square(wide - center), axis=-1, keepdims=True)
        scale = lax.rsqrt(spread + 1e-05)

        def projected(part, begin, end):
            product = dot32(features[begin:end], w_att[part])
            shifted = product - center[begin:end] * sums[part : part + 1, :]
            return (shifted * scale[begin:end]).astype(jnp.bfloat16)

        refs = list(refs)
        if query_rows:
            refs.pop(0)[...] = projected(0, 0, query_rows)
        if extra_rows:
            refs.pop(0)[...] = projected(0, rows, rows + extra_rows)
        for part in (1, 2):
            both = projected(part, 0, rows + extra_rows)
            refs.pop(0)[...] = both[:rows]
            if extra_rows:
                refs.pop(0)[...] = both[rows:]

    def shape(size):
        return jax.ShapeDtypeStruct((size, width), jnp.bfloat16)

    shapes = [shape(query_rows)] * bool(query_rows) + [shape(extra_rows)] * bool(extra_rows)
    shapes += ([shape(rows)] + [shape(extra_rows)] * bool(extra_rows)) * 2
    depth = stack.shape[2]
    return call(
        kernel,
        shapes,
        (stack, *weights, *every) + ((fixed,) if boundary else ()),
        scratch=[
            pltpu.VMEM((last_count, depth), jnp.float32),
            pltpu.VMEM((len(places), HALO, depth), jnp.bfloat16),
            pltpu.VMEM((len(places), HALO, depth), jnp.bfloat16),
        ]
        if boundary
        else [],
        micros=0.5 + 0.006 * (rows + extra_rows),
    )


def gather_rows(places, query_slots, bounds, sources, extras, frames_local, outs):
    q_rows, k_all, v_all, q_all, first, last = outs
    parts = lax.axis_size("mp")
    frames_shard = frames_local * parts
    last_count = extras[0].shape[0] - 2 * HALO
    slots = range(len(places))
    for held, group, extra, held_slots in zip(
        (q_all, k_all, v_all), sources, extras, (query_slots, slots, slots)
    ):
        begin = 0
        for source in group:
            held[begin : begin + source.shape[0], :] = source[...]
            begin += source.shape[0]
        patch(held, extra[0:last_count, :], held_slots, frames_local)
    query_places = [places[slot] for slot in query_slots]
    q_rows[0:HALO, :] = extras[0][last_count : last_count + HALO, :]
    for part in range(parts):
        begin = HALO + part * frames_local
        slot = slot_of(query_places, lax.axis_index("tm"), part)
        start = pl.multiple_of(slot * frames_local, HALO)
        q_rows[begin : begin + frames_local, :] = q_all[pl.ds(start, frames_local), :]
    q_rows[HALO + frames_shard :, :] = extras[0][last_count + HALO :, :]
    for line, ref in enumerate((first, last)):
        row = bounds[line : line + 1, :]
        ref[...] = jnp.transpose(jnp.broadcast_to(row, (LANES, row.shape[1])))


def attend_rows(places, begin, q_rows, k_all, v_all, first, last, frames_local, result, bias):
    count, width = result.shape
    rows = k_all.shape[0]
    time_index, model_index = lax.axis_index("tm"), lax.axis_index("mp")
    frames_shard = frames_local * lax.axis_size("mp")
    lows, highs = first[pl.ds(begin, count), :], last[pl.ds(begin, count), :]
    lanes = lax.broadcasted_iota(jnp.int32, (1, LANES), 1)
    for lane in range(0, rows, LANES):
        at = jnp.zeros((1, LANES), jnp.int32)
        for slot in range(lane // frames_local, -(-(lane + LANES) // frames_local)):
            if slot < len(places):
                slot_tm, slot_mp = places[slot]
                base = slot_tm(time_index) * frames_shard
                base += (model_index ^ slot_mp) * frames_local - slot * frames_local + lane
                at = jnp.where(lanes >= slot * frames_local - lane, lanes + base, at)
        at = at.astype(jnp.float32)
        bias[:, lane : lane + LANES] = jnp.where((at >= lows) & (at < highs), 0.0, -1e30)
    for lane in range(0, width, LANES):
        span = min(LANES, width - lane)
        q_pair = q_rows[pl.ds(begin, count), lane : lane + span]
        k_pair = k_all[:, lane : lane + span]
        v_pair = v_all[:, lane : lane + span]
        heads = span // HD
        head_of = lax.broadcasted_iota(jnp.int32, (count, span), 1) // HD
        scaled = q_pair * jnp.bfloat16(1.0 / math.sqrt(HD))
        stacked = jnp.concatenate(
            [jnp.where(head_of == head, scaled, jnp.zeros_like(scaled)) for head in range(heads)],
            axis=0,
        )
        scores = lax.dot_general(
            stacked, k_pair, (((1,), (1,)), ((), ())), preferred_element_type=jnp.float32
        )
        scores = scores + jnp.concatenate([bias[...]] * heads, axis=0)
        weights = jnp.exp(scores - jnp.max(scores, axis=1, keepdims=True))
        total = jnp.sum(weights, axis=1, keepdims=True)
        ratio = dot32(weights.astype(jnp.bfloat16), v_pair) / total
        merged = ratio[0:count]
        for head in range(1, heads):
            merged = jnp.where(head_of == head, ratio[head * count : (head + 1) * count], merged)
        result[:, lane : lane + span] = merged.astype(jnp.bfloat16)


def split_pair(model_index, result, mine, other, frames_local):
    window = mine.shape[0]
    place = lax.rem(model_index, 2) * frames_local
    mine[...] = result[pl.ds(pl.multiple_of(place, HALO), window), :]
    place = frames_local - place
    other[...] = result[pl.ds(pl.multiple_of(place, HALO), window), :]


def attend_far(places, query_slots, far, bounds, sources, extras, frames_local):
    width = sources[0][0].shape[1]
    query_count, rows = (sum(group.shape[0] for group in groups) for groups in sources[:2])
    sizes = [len(groups) for groups in sources]
    extended = frames_local * lax.axis_size("mp") + 2 * HALO
    window = frames_local + 2 * HALO
    pair = 2 * frames_local + 2 * HALO

    def kernel(bound_ref, *refs):
        groups = []
        for size in sizes:
            groups.append(refs[:size])
            refs = refs[size:]
        extra_refs, refs = refs[:3], refs[3:]
        windows, refs = refs[: 2 * len(far)], refs[2 * len(far) :]
        q_rows, k_all, v_all, first, last, q_all, result, bias = refs
        gather_rows(
            places,
            query_slots,
            bound_ref,
            groups,
            extra_refs,
            frames_local,
            (q_rows, k_all, v_all, q_all, first, last),
        )
        model_index = lax.axis_index("mp")
        for number, bit in enumerate(far):
            begin = pl.multiple_of((model_index ^ bit) // 2 * (2 * frames_local), HALO)
            attend_rows(
                places, begin, q_rows, k_all, v_all, first, last, frames_local, result, bias
            )
            split_pair(
                model_index, result, windows[2 * number], windows[2 * number + 1], frames_local
            )

    def shape(count, wide=width, dtype=jnp.bfloat16):
        return jax.ShapeDtypeStruct((count, wide), dtype)

    return call(
        kernel,
        [shape(window)] * (2 * len(far))
        + [shape(extended), shape(rows), shape(rows)]
        + [shape(extended, LANES, jnp.float32)] * 2,
        (bounds, *(array for groups in sources for array in groups), *extras),
        scratch=[
            pltpu.VMEM((query_count, width), jnp.bfloat16),
            pltpu.VMEM((pair, width), jnp.bfloat16),
            pltpu.VMEM((pair, rows), jnp.float32),
        ],
        micros=2.5 * len(far),
        vmem=16 + pair * rows * 20 // 1024 // 1024,
    )


def attend_near(places, after, q_rows, k_all, v_all, first, last, frames_local):
    rows, width = k_all.shape
    window = frames_local + 2 * HALO
    pair = 2 * frames_local + 2 * HALO

    def kernel(_, q_ref, k_ref, v_ref, first_ref, last_ref, mine, other, result, bias):
        model_index = lax.axis_index("mp")
        begin = pl.multiple_of(model_index // 2 * (2 * frames_local), HALO)
        attend_rows(
            places, begin, q_ref, k_ref, v_ref, first_ref, last_ref, frames_local, result, bias
        )
        split_pair(model_index, result, mine, other, frames_local)

    return call(
        kernel,
        [jax.ShapeDtypeStruct((window, width), jnp.bfloat16)] * 2,
        (after, q_rows, k_all, v_all, first, last),
        scratch=[
            pltpu.VMEM((pair, width), jnp.bfloat16),
            pltpu.VMEM((pair, rows), jnp.float32),
        ],
        micros=1.0,
        vmem=16 + pair * rows * 20 // 1024 // 1024,
    )


def far_branch_own(windows, w_own):
    count = len(windows)

    def kernel(*refs):
        for window, out in zip(refs[:count], refs[count + 1 :]):
            out[...] = dot32(window[...], refs[count][...])

    shape = jax.ShapeDtypeStruct((windows[0].shape[0], w_own.shape[1]), jnp.float32)
    return call(kernel, [shape] * count, (*windows, w_own), micros=0.4 * count)


def far_branch(shares, windows, w_near, cut):
    count = len(windows)

    def kernel(*refs):
        share_refs, window_refs, near, outs = (
            refs[:count],
            refs[count : 2 * count],
            refs[2 * count],
            refs[2 * count + 1 :],
        )
        for number, (share, window) in enumerate(zip(share_refs, window_refs)):
            total = (share[...] + dot32(window[...], near[...])).astype(jnp.bfloat16)
            outs[2 * number][...] = total[:cut]
            outs[2 * number + 1][...] = total[cut:]

    sizes = [cut, windows[0].shape[0] - cut] * count
    shapes = [jax.ShapeDtypeStruct((size, w_near.shape[1]), jnp.bfloat16) for size in sizes]
    return call(kernel, shapes, (*shares, *windows, w_near), micros=0.5 * count)


def near_branch(places, windows, w_rows, stacks, fixed, w_subsample, frames_local):
    counts = [stack.shape[0] for stack in stacks]
    depth, model = w_subsample.shape
    window = frames_local + 2 * HALO
    slots = len(places)

    def kernel(own, near, w_own, w_near, *refs):
        stack_refs, (fixed_ref, w_sub, out, held, taken) = refs[: len(counts)], refs[len(counts) :]
        begin = 0
        for stack_ref, count in zip(stack_refs, counts):
            for block in range(count):
                held[begin : begin + frames_local, :] = stack_ref[block, 0:frames_local, :]
                begin += frames_local
        rows = last_rows(stack_refs, counts, frames_local, fixed_ref[...], fixed.shape[0])
        patch(held, rows, range(slots), frames_local)
        parts = lax.axis_size("mp")
        block = lax.axis_index("tm") * parts + lax.axis_index("mp") + parts

        def source(number, offset, count):
            slot = slot_of(places, number // parts - 1, lax.rem(number, parts))
            start = pl.multiple_of(slot * frames_local + offset, HALO)
            return held[pl.ds(start, count), :]

        taken[0:HALO, :] = source(block - 1, frames_local - HALO, HALO)
        taken[HALO : HALO + frames_local, :] = source(block, 0, frames_local)
        taken[HALO + frames_local : window, :] = source(block + 1, 0, HALO)
        features = dot32(taken[...], w_sub[...]).astype(jnp.bfloat16).astype(jnp.float32)
        share = dot32(own[...], w_own[...]) + dot32(near[...], w_near[...])
        out[...] = features + share

    return call(
        kernel,
        jax.ShapeDtypeStruct((window, model), jnp.float32),
        (*windows, *w_rows, *stacks, fixed, w_subsample),
        scratch=[
            pltpu.VMEM((slots * frames_local, depth), jnp.bfloat16),
            pltpu.VMEM((window, depth), jnp.bfloat16),
        ],
        micros=0.6,
    )


def convolve(held, taps, begin, count, here):
    offset = HALO - KERNEL // 2
    reach = count + 8
    rows = held[begin : begin + count + 2 * HALO, here]
    tap_rows = taps[:, here].astype(jnp.float32)
    total = jnp.zeros((count, rows.shape[1]), jnp.float32)
    for phase in range(8):
        share = jnp.zeros((reach, rows.shape[1]), jnp.float32)
        for tap in range(KERNEL):
            if (tap + offset) % 8 == phase:
                first = (tap + offset) // 8 * 8
                share += rows[first : first + reach] * tap_rows[tap : tap + 1]
        moved = pltpu.roll(share, reach - phase, axis=0) if phase else share
        total += moved[0:count]
    return total


def mix(base, shares, gain):
    mixed = base
    for share in shares:
        mixed += share[...].astype(jnp.float32)
    mixed = mixed.astype(jnp.bfloat16).astype(jnp.float32)
    return mixed, (normalize(mixed) * gain[...]).astype(jnp.bfloat16).astype(jnp.float32)


def silu(values):
    return values / (1.0 + jnp.exp(-values))


def finish_first(base, shares, gain, taps):
    count = len(shares)
    cut, model = shares[0].shape
    done = cut - 2 * HALO
    chunk = 2 * LANES

    def kernel(base_ref, *refs):
        share_refs, (gain_ref, tap_ref, out, held, mixed_rows) = refs[:count], refs[count:]
        mixed, conv_in = mix(base_ref[0:cut, :], share_refs, gain_ref)
        mixed_rows[...] = mixed
        held[...] = conv_in
        before = lax.axis_index("tm") * lax.axis_size("mp") + lax.axis_index("mp") > 0
        held[0:HALO, :] = jnp.where(before, conv_in[0:HALO], 0.0)
        for lane in range(0, model, chunk):
            here = slice(lane, lane + chunk)
            total = convolve(held, tap_ref, 0, done, here)
            out[:, here] = (mixed_rows[HALO : HALO + done, here] + silu(total)).astype(jnp.bfloat16)

    rows = jax.ShapeDtypeStruct((cut, model), jnp.float32)
    return call(
        kernel,
        (jax.ShapeDtypeStruct((done, model), jnp.bfloat16), rows, rows),
        (base, *shares, gain, taps),
        micros=0.5,
    )


def finish_last(base, shares, first, gain, taps, frames_local):
    count = len(shares)
    window, model = base.shape
    cut, done = first[1].shape[0], first[0].shape[0]
    left = frames_local - done
    chunk = 2 * LANES
    chunks = model // chunk

    def kernel(base_ref, *refs):
        share_refs, refs = refs[:count], refs[count:]
        out_ref, held_ref, mixed_ref, gain_ref, tap_ref, result, held, mixed_rows, staged, sems = refs
        copies = [pltpu.make_async_copy(out_ref, result.at[pl.ds(0, done)], sems.at[chunks])]
        copies[0].start()
        mixed, conv_in = mix(base_ref[cut:window, :], share_refs, gain_ref)
        mixed_rows[0:cut, :] = mixed_ref[...]
        mixed_rows[cut:window, :] = mixed
        held[0:cut, :] = held_ref[...]
        held[cut:window, :] = conv_in
        parts = lax.axis_size("mp")
        block = lax.axis_index("tm") * parts + lax.axis_index("mp")
        after = block < lax.axis_size("tm") * parts - 1
        held[window - HALO : window, :] = jnp.where(after, conv_in[window - HALO - cut :], 0.0)
        for number in range(chunks):
            here = slice(number * chunk, (number + 1) * chunk)
            total = convolve(held, tap_ref, done, left, here)
            kept = mixed_rows[HALO + done : HALO + frames_local, here]
            staged[:, here] = (kept + silu(total)).astype(jnp.bfloat16)
            copies.append(
                pltpu.make_async_copy(
                    staged.at[:, here], result.at[pl.ds(done, left), here], sems.at[number]
                )
            )
            copies[-1].start()
        for copy in copies:
            copy.wait()

    return call(
        kernel,
        jax.ShapeDtypeStruct((frames_local, model), jnp.bfloat16),
        (base, *shares, *first, gain, taps),
        scratch=[
            pltpu.VMEM((window, model), jnp.float32),
            pltpu.VMEM((window, model), jnp.float32),
            pltpu.VMEM((left, model), jnp.bfloat16),
            pltpu.SemaphoreType.DMA((chunks + 1,)),
        ],
        micros=1.5,
        result=pltpu.HBM,
    )


def exchange(block, axis, bit):
    return lax.ppermute(block, axis, [(i, i ^ bit) for i in range(lax.axis_size(axis))])


def shifted(block, axis, distance):
    count = lax.axis_size(axis)
    route = [(i - distance, i) for i in range(count) if 0 <= i - distance < count]
    return lax.ppermute(block, axis, route)


def shards(
    waveform,
    segment_start,
    segment_end,
    w_subsample,
    w_attention,
    w_output,
    gain_convolution,
    w_depthwise,
):
    frames_local = waveform.shape[0] // (SUB * HOP)
    frames_shard = segment_start.shape[0]
    parts, shards_total = lax.axis_size("mp"), lax.axis_size("tm")
    bits = [1 << b for b in reversed(range((parts - 1).bit_length()))]

    samples = waveform.reshape(-1, LANES)
    starts, ends = segment_start[None, :], segment_end[None, :]
    tables = jnp.asarray(front_tables())
    stacked = log_mel_rows(starts, ends, samples, tables, frames_local)
    *weights, kept = fetch(stacked, w_subsample, w_attention)

    w_near = exchange(w_output, "mp", bits[-1])

    reach = min((SEG_MAX + HALO - 2) // frames_shard + 1, shards_total - 1)
    whole = reach == shards_total - 1 and shards_total & (shards_total - 1) == 0
    if whole:
        order = [shards_total - 1, *range(1, shards_total - 1)]
        moves = [lambda tm, bit=bit: tm ^ bit for bit in order]
        column = [exchange(stacked, "tm", bit) for bit in order]
    else:
        steps = [sign * d for d in range(1, reach + 1) for sign in (1, -1)]
        moves = [lambda tm, step=step: tm - step for step in steps]
        column = [shifted(stacked, "tm", step) for step in steps]
    early = [(kept, [(lambda tm: tm, 0)])]
    late = [(assemble(column, weights[-1:]), [(move, 0) for move in moves])]

    def across(blocks, bit):
        return [
            (exchange(block, "mp", bit), [(move, mp ^ bit) for move, mp in held])
            for block, held in blocks
        ]

    for bit in bits[:-1]:
        early, late = early + across(early, bit), late + across(late, bit)
    ready = early + late[:1]
    joined = (assemble([block for block, _ in ready]), sum([held for _, held in ready], []))
    groups = [joined] + across([joined], bits[-1])
    projected = [
        project_rows(block, weights, frames_local, len(early)) for block, _ in groups
    ]
    done = [group[-1] for group in projected]
    late = [(assemble([block], done), held) for block, held in late[1:]]
    groups += late + across(late, bits[-1])
    stacks, held = zip(*groups)
    places = sum(held, [])
    joined_slots = range(len(joined[1]), 2 * len(joined[1]))
    query_slots = [*range(len(early)), *joined_slots[: len(early)]]
    fixed, bounds = boundary_rows(places, starts, ends, stacks, tables, frames_local)
    projected += [project_rows(block, weights, frames_local, 0) for block in stacks[2:-1]]
    outs = project_rows(stacks[-1], weights, frames_local, 0, (places, stacks, fixed))
    extras = (outs[0], outs[2], outs[4])
    queries = [group[0] for group in projected[:2]]
    keys = [*(group[-2] for group in projected), outs[1]]
    values = [*(group[-1] for group in projected), outs[3]]

    far = list(range(2, parts, 2))
    outs = attend_far(
        places, query_slots, far, bounds, (queries, keys, values), extras, frames_local
    )
    windows, shared = outs[: 2 * len(far)], outs[2 * len(far) :]
    arrived = [exchange(window, "mp", 1) for window in windows[1::2]]
    w_rows = (w_output, w_near)
    shares = far_branch_own(windows[0::2], w_output)
    shares = far_branch(shares, arrived, w_near, frames_local + HALO)
    mine, other = attend_near(places, shares[0], *shared, frames_local)
    shares = [exchange(share, "mp", far[number // 2]) for number, share in enumerate(shares)]
    base = near_branch(
        places, (mine, exchange(other, "mp", 1)), w_rows, stacks, fixed, weights[0], frames_local
    )
    gain = gain_convolution[None, :]
    first = finish_first(base, shares[0::2], gain, w_depthwise)
    return finish_last(base, shares[1::2], first, gain, w_depthwise, frames_local)


def solution(mesh):
    placed = (
        P(("groups", "tm", "mp")),
        P(("groups", "tm")),
        P(("groups", "tm")),
        P(),
        P(None, None, "mp"),
        P("mp", None),
        P(),
        P(),
    )
    return jax.shard_map(
        shards,
        mesh=mesh,
        in_specs=placed,
        out_specs=P(("groups", "tm", "mp"), None),
        check_vma=False,
    )
```

```python
import math

import jax
import jax.numpy as jnp
import ml_dtypes
import numpy as np
from jax import lax
from jax.experimental import pallas as pl
from jax.experimental.pallas import tpu as pltpu
from jax.sharding import PartitionSpec as P

HD = 64
NMEL = 128
NFFT = 400
HOP = 160
BINS = 256
SUB = 4
KERNEL = 31
SEG_MAX = 750
LANES = 128
HALO = 16
EXTRA = 8
FLOPS_PER_MICRO = 2000000000
TAIL_LINES = 3
HEAD_LINES = 2
DIGIT = 128
FRAME_ROWS = SUB * HOP // LANES
WIDE = -(-NFFT // LANES) * LANES


def split_high_low(table):
    high = table.astype(ml_dtypes.bfloat16)
    low = (table - high.astype(np.float32)).astype(ml_dtypes.bfloat16)
    return high, low


def fourier_table():
    sample_index = np.arange(NFFT)[:, None]
    bin_index = np.arange(BINS)[None, :]
    angle = (sample_index * bin_index % NFFT) * (2.0 * math.pi / NFFT)
    window = 0.5 - 0.5 * np.cos(np.arange(NFFT) * (2.0 * math.pi / NFFT))
    kept = bin_index <= NFFT // 2
    cosine = np.where(kept, np.cos(angle), 0.0) * window[:, None]
    sine = np.where(kept, -np.sin(angle), 0.0) * window[:, None]
    return np.concatenate([cosine, sine], axis=1).astype(np.float32)


def mel_bank():
    mel_top = 2595.0 * math.log10(1.0 + 8000.0 / 700.0)
    mel_points = np.arange(NMEL + 2) * (mel_top / (NMEL + 1))
    edges = 700.0 * (np.power(10.0, mel_points / 2595.0) - 1.0) * (NFFT / 16000.0)
    widths = np.maximum(edges[2:] - edges[1:-1], 1.0)
    bin_value = np.arange(BINS)[:, None]
    triangle = np.maximum(0.0, 1.0 - np.abs(bin_value - edges[None, 1:-1]) / widths[None, :])
    return np.where(bin_value <= NFFT // 2, triangle, 0.0).astype(np.float32)


def front_tables():
    high, low = split_high_low(fourier_table())
    bank = np.concatenate(split_high_low(mel_bank()), axis=1)
    bank = np.pad(bank, ((0, 0), (0, high.shape[1] - bank.shape[1])))
    return np.concatenate([high, low, bank], axis=0)


def dot32(left, right):
    return jnp.dot(left, right, preferred_element_type=jnp.float32)


def dot_split(values, table_high, table_low):
    high = values.astype(jnp.bfloat16)
    low = (values - high.astype(jnp.float32)).astype(jnp.bfloat16)
    table = table_high()
    large, small = dot32(high, table), dot32(low, table)
    return large + (small + dot32(high, table_low()))


def normalize(values):
    center = jnp.mean(values, axis=-1, keepdims=True)
    shifted = values - center
    spread = jnp.mean(jnp.square(shifted), axis=-1, keepdims=True)
    return shifted * lax.rsqrt(spread + 1e-05)


def call(
    kernel, out_shape, operands, scratch=(), micros=1.0, remote=0, vmem=16, result=pltpu.VMEM
):
    specs = [pl.BlockSpec(memory_space=pltpu.VMEM)] * (len(operands) - remote)
    specs += [pl.BlockSpec(memory_space=pltpu.HBM)] * remote
    return pl.pallas_call(
        kernel,
        out_shape=out_shape,
        in_specs=specs,
        out_specs=jax.tree.map(lambda _: pl.BlockSpec(memory_space=result), out_shape),
        scratch_shapes=list(scratch),
        compiler_params=pltpu.CompilerParams(vmem_limit_bytes=vmem * 1024 * 1024),
        cost_estimate=pl.CostEstimate(
            flops=int(micros * FLOPS_PER_MICRO), bytes_accessed=1000000, transcendentals=0
        ),
    )(*operands)


def fetch(stacked, w_subsample, w_attention):
    parts, _, width = w_attention.shape

    def kernel(stack_ref, w_sub, w_att, out_sub, out_att, sums, out_stack, sems):
        out_stack[...] = stack_ref[...]
        copies = [
            pltpu.make_async_copy(w_att, out_att, sems.at[0]),
            pltpu.make_async_copy(w_sub, out_sub, sems.at[1]),
        ]
        for copy in copies:
            copy.start()
        for copy in copies:
            copy.wait()
        sums[...] = jnp.zeros_like(sums)
        for part in range(parts):
            columns = out_att[part].astype(jnp.float32)
            sums[part : part + 1, :] = jnp.sum(columns, axis=0, keepdims=True)

    return call(
        kernel,
        [jax.ShapeDtypeStruct(array.shape, array.dtype) for array in (w_subsample, w_attention)]
        + [
            jax.ShapeDtypeStruct((8, width), jnp.float32),
            jax.ShapeDtypeStruct(stacked.shape, stacked.dtype),
        ],
        (stacked, w_subsample, w_attention),
        scratch=[pltpu.SemaphoreType.DMA((2,))],
        remote=2,
    )


def stack_of(ref, block, begin, end):
    half = (ref.shape[1] - EXTRA) // 2
    return jnp.concatenate([ref[block, begin:end, :], ref[block, half + begin : half + end, :]], axis=1)


def log_mel(windows, tables, copies=()):
    lanes = lax.broadcasted_iota(jnp.int32, windows.shape, 1)
    windows = jnp.where(lanes < NFFT, windows, 0.0)

    def fetched(number, begin):
        def load():
            if copies:
                copies[number].wait()
            return tables[begin : begin + WIDE, :]

        return load

    spectrum = dot_split(windows, fetched(0, 0), fetched(1, NFFT))
    power = jnp.square(spectrum[:, :BINS]) + jnp.square(spectrum[:, BINS:])
    bank = [tables[2 * NFFT :, part * NMEL : (part + 1) * NMEL] for part in range(2)]
    return jnp.log(dot_split(power, lambda: bank[0], lambda: bank[1]) + 1e-06)


def log_mel_rows(starts, ends, samples, tables, frames_local):
    rows = frames_local * FRAME_ROWS
    frames_shard = starts.shape[1]

    spans = (pl.ds(0, WIDE), pl.ds(WIDE, tables.shape[0] - WIDE))

    def kernel(start, end, wave, table, out, held, start_ref, end_ref, tables_ref, sems):
        pairs = (
            (wave, held.at[pl.ds(0, rows)]),
            (start, start_ref),
            (end, end_ref),
        ) + tuple((table.at[span], tables_ref.at[span]) for span in spans)
        copies = [
            pltpu.make_async_copy(source, target, sems.at[slot])
            for slot, (source, target) in enumerate(pairs)
        ]
        for copy in copies:
            copy.start()
        held[rows : rows + 8, :] = jnp.zeros((8, LANES), jnp.float32)
        for copy in copies[:3]:
            copy.wait()
        lines = [held[pl.ds(j, frames_local, stride=FRAME_ROWS), :] for j in range(FRAME_ROWS + 2)]
        windows = []
        for sub in range(SUB):
            line, lane = divmod(sub * HOP, LANES)
            taken = jnp.concatenate(lines[line : line + WIDE // LANES], axis=1)
            windows.append(pltpu.roll(taken, WIDE - lane, axis=1) if lane else taken)
        pieces = []
        for taken in (range(rows - TAIL_LINES, rows), range(HEAD_LINES)):
            line = jnp.concatenate([held[row : row + 1, :] for row in taken], axis=1)
            high = line.astype(jnp.bfloat16).astype(jnp.float32)
            pieces += [high, line - high]
        for ref in (start_ref, end_ref):
            edge = jnp.concatenate([ref[:, :HALO], ref[:, frames_shard - HALO :]], axis=1)
            high = edge // DIGIT
            low = edge - high * DIGIT
            pieces += [digit.astype(jnp.float32) for digit in (high, low)]
        filled = sum(piece.shape[1] for piece in pieces)
        pieces.append(jnp.zeros((1, EXTRA * 2 * NMEL - filled), jnp.float32))
        flat = jnp.concatenate(pieces, axis=1)
        extras = [flat[:, row * 2 * NMEL : (row + 1) * 2 * NMEL] for row in range(EXTRA)]
        out[0, 2 * frames_local :, :] = jnp.concatenate(extras, axis=0).astype(jnp.bfloat16)
        mel = log_mel(jnp.concatenate(windows, axis=0), tables_ref, copies[3:])
        for sub in range(SUB):
            begin, lane = sub // 2 * frames_local, sub % 2 * NMEL
            out[0, begin : begin + frames_local, lane : lane + NMEL] = mel[
                sub * frames_local : (sub + 1) * frames_local
            ].astype(jnp.bfloat16)

    return call(
        kernel,
        jax.ShapeDtypeStruct((1, 2 * frames_local + EXTRA, 2 * NMEL), jnp.bfloat16),
        (starts, ends, samples, tables),
        scratch=[
            pltpu.VMEM((rows + 8, LANES), jnp.float32),
            pltpu.VMEM(starts.shape, starts.dtype),
            pltpu.VMEM(ends.shape, ends.dtype),
            pltpu.VMEM(tables.shape, tables.dtype),
            pltpu.SemaphoreType.DMA((5,)),
        ],
        remote=4,
        vmem=54,
        micros=1.0,
    )


def boundary_rows(places, starts, ends, stacks, tables, frames_local):
    counts = [stack.shape[0] for stack in stacks]
    slots = len(places)
    rows = -(-slots // HALO) * HALO
    frames_shard = starts.shape[1]
    parts = lax.axis_size("mp")
    final = lax.axis_size("tm") * parts - 1
    shift = final + 1

    def kernel(start_ref, end_ref, *refs):
        stack_refs, refs = refs[: len(counts)], refs[len(counts) :]
        tables_ref, out, bounds, tails, heads, nexts, edges, order = refs
        time_index, model_index = lax.axis_index("tm"), lax.axis_index("mp")
        tails[...] = jnp.zeros_like(tails)
        nexts[...] = jnp.zeros_like(nexts)
        slot = 0
        for stack_ref, count in zip(stack_refs, counts):
            for block in range(count):
                kept = stack_ref[block, 2 * frames_local :, :].astype(jnp.float32)
                flat = jnp.concatenate([kept[row : row + 1] for row in range(EXTRA)], axis=1)
                here = slice(slot, slot + 1)
                tail, head = TAIL_LINES * LANES, HEAD_LINES * LANES
                tails[here, :] = flat[:, :tail] + flat[:, tail : 2 * tail]
                heads[here, :] = flat[:, 2 * tail : 2 * tail + head] + flat[
                    :, 2 * tail + head : 2 * (tail + head)
                ]
                digits = flat[:, 2 * (tail + head) :]
                for line in range(2):
                    high = digits[:, 4 * line * HALO : (4 * line + 2) * HALO]
                    low = digits[:, (4 * line + 2) * HALO : (4 * line + 4) * HALO]
                    edges[line, here, 0 : 2 * HALO] = high * DIGIT + low
                slot += 1
        numbers = [
            slot_tm(time_index) * parts + (model_index ^ slot_mp) for slot_tm, slot_mp in places
        ]
        for number in numbers:
            order[number + 1 + shift] = jnp.int32(0)
        for slot, number in enumerate(numbers):
            order[number + shift] = jnp.int32(slot)
        for slot, number in enumerate(numbers):
            taken = heads[pl.ds(order[number + 1 + shift], 1), :]
            nexts[slot : slot + 1, :] = jnp.where(number == final, 0.0, taken)
        line = jnp.concatenate([tails[...], nexts[...]], axis=1)
        windows = []
        for sub in range(SUB - 2, SUB):
            skip, lane = divmod(sub * HOP - (FRAME_ROWS - TAIL_LINES) * LANES, LANES)
            windows.append(
                pltpu.roll(line[:, skip * LANES : skip * LANES + WIDE], WIDE - lane, axis=1)
            )
        mel = log_mel(jnp.concatenate(windows, axis=0), tables_ref).astype(jnp.bfloat16)
        for number in range(2):
            lane = number * NMEL
            out[:, lane : lane + NMEL] = mel[number * rows : (number + 1) * rows]
        left = slot_of(places, time_index - 1, model_index)
        right = slot_of(places, time_index + 1, model_index)
        for number, ref in enumerate((start_ref, end_ref)):
            bounds[number : number + 1, :] = jnp.concatenate(
                [
                    edges[number, pl.ds(left, 1), :][:, HALO : 2 * HALO],
                    ref[...].astype(jnp.float32),
                    edges[number, pl.ds(right, 1), :][:, 0:HALO],
                ],
                axis=1,
            )

    return call(
        kernel,
        (
            jax.ShapeDtypeStruct((rows, 2 * NMEL), jnp.bfloat16),
            jax.ShapeDtypeStruct((2, frames_shard + 2 * HALO), jnp.float32),
        ),
        (starts, ends, *stacks, tables),
        scratch=[
            pltpu.VMEM((rows, TAIL_LINES * LANES), jnp.float32),
            pltpu.VMEM((rows, HEAD_LINES * LANES), jnp.float32),
            pltpu.VMEM((rows, HEAD_LINES * LANES), jnp.float32),
            pltpu.VMEM((2, rows, LANES), jnp.float32),
            pltpu.SMEM((3 * shift,), jnp.int32),
        ],
        micros=0.9,
    )


def last_rows(stack_refs, counts, frames_local, fixed, rows):
    lasts = []
    for stack_ref, count in zip(stack_refs, counts):
        for block in range(count):
            kept = stack_ref[block, frames_local - HALO : frames_local, :]
            lasts.append(kept.astype(jnp.float32)[HALO - 1 : HALO])
    if len(lasts) < rows:
        lasts.append(jnp.zeros((rows - len(lasts), 2 * NMEL), jnp.float32))
    return jnp.concatenate([jnp.concatenate(lasts, axis=0).astype(jnp.bfloat16), fixed], axis=1)


def patch(held, fixed, slots, frames_local):
    fixed = fixed.astype(jnp.float32)
    for number, slot in enumerate(slots):
        here = slice((number + 1) * frames_local - HALO, (number + 1) * frames_local)
        kept = held[here, :].astype(jnp.float32)
        last = lax.broadcasted_iota(jnp.int32, kept.shape, 0) == HALO - 1
        held[here, :] = jnp.where(last, fixed[slot : slot + 1, :], kept).astype(held.dtype)


def assemble(parts, after=()):
    counts = [part.shape[0] for part in parts]

    def kernel(*refs):
        begin = 0
        for ref, count in zip(refs, counts):
            refs[-1][begin : begin + count] = ref[...]
            begin += count

    shape = jax.ShapeDtypeStruct((sum(counts), *parts[0].shape[1:]), parts[0].dtype)
    return call(kernel, shape, (*parts, *after))


def slot_of(places, tm, mp):
    found = jnp.int32(0)
    for slot, (slot_tm, slot_mp) in enumerate(places):
        here = (slot_tm(lax.axis_index("tm")) == tm) & (lax.axis_index("mp") ^ slot_mp == mp)
        found = jnp.where(here, slot, found)
    return found


def project_rows(stack, weights, frames_local, query_blocks, boundary=None):
    count = stack.shape[0]
    rows, width = count * frames_local, weights[1].shape[2]
    query_rows = query_blocks * frames_local
    places, every, fixed = boundary or ((), (), jnp.zeros((0, 2 * NMEL), jnp.bfloat16))
    counts = [block.shape[0] for block in every]
    last_count = fixed.shape[0]
    extra_rows = last_count + 2 * HALO if boundary else 0

    def boundary_stack(every_refs, fixed_ref, lasts, heads, tails):
        lasts[...] = last_rows(
            every_refs, counts, frames_local, fixed_ref[...], last_count
        ).astype(jnp.float32)
        slot = 0
        for ref, blocks in zip(every_refs, counts):
            for block in range(blocks):
                heads[slot] = stack_of(ref, block, 0, HALO)
                tails[slot] = stack_of(ref, block, frames_local - HALO, frames_local)
                slot += 1
        time_index, parts = lax.axis_index("tm"), lax.axis_size("mp")
        left = slot_of(places, time_index - 1, parts - 1)
        right = slot_of(places, time_index + 1, 0)
        tail = tails[left].astype(jnp.float32)
        final = lax.broadcasted_iota(jnp.int32, tail.shape, 0) == HALO - 1
        tail = jnp.where(final, lasts[pl.ds(left, 1), :], tail).astype(jnp.bfloat16)
        return [lasts[...].astype(jnp.bfloat16), tail, heads[right]]

    def kernel(stack_ref, w_sub, w_att, sums, *refs):
        stack_rows = [stack_of(stack_ref, block, 0, frames_local) for block in range(count)]
        if boundary:
            every_refs, refs = refs[: len(every)], refs[len(every) :]
            fixed_ref, *refs = refs
            refs, scratch = refs[:-3], refs[-3:]
            stack_rows += boundary_stack(every_refs, fixed_ref, *scratch)
        features = dot32(jnp.concatenate(stack_rows, axis=0), w_sub[...]).astype(jnp.bfloat16)
        wide = features.astype(jnp.float32)
        center = jnp.mean(wide, axis=-1, keepdims=True)
        spread = jnp.mean(jnp.square(wide - center), axis=-1, keepdims=True)
        scale = lax.rsqrt(spread + 1e-05)

        def projected(part, begin, end):
            product = dot32(features[begin:end], w_att[part])
            shifted = product - center[begin:end] * sums[part : part + 1, :]
            return (shifted * scale[begin:end]).astype(jnp.bfloat16)

        refs = list(refs)
        if query_rows:
            refs.pop(0)[...] = projected(0, 0, query_rows)
        if extra_rows:
            refs.pop(0)[...] = projected(0, rows, rows + extra_rows)
        for part in (1, 2):
            both = projected(part, 0, rows + extra_rows)
            refs.pop(0)[...] = both[:rows]
            if extra_rows:
                refs.pop(0)[...] = both[rows:]

    def shape(size):
        return jax.ShapeDtypeStruct((size, width), jnp.bfloat16)

    shapes = [shape(query_rows)] * bool(query_rows) + [shape(extra_rows)] * bool(extra_rows)
    shapes += ([shape(rows)] + [shape(extra_rows)] * bool(extra_rows)) * 2
    depth = weights[0].shape[0]
    return call(
        kernel,
        shapes,
        (stack, *weights, *every) + ((fixed,) if boundary else ()),
        scratch=[
            pltpu.VMEM((last_count, depth), jnp.float32),
            pltpu.VMEM((len(places), HALO, depth), jnp.bfloat16),
            pltpu.VMEM((len(places), HALO, depth), jnp.bfloat16),
        ]
        if boundary
        else [],
        micros=0.5 + 0.006 * (rows + extra_rows),
    )


def gather_rows(places, query_slots, bounds, sources, extras, frames_local, outs):
    q_rows, k_all, v_all, q_all, first, last = outs
    parts = lax.axis_size("mp")
    frames_shard = frames_local * parts
    last_count = extras[0].shape[0] - 2 * HALO
    slots = range(len(places))
    for held, group, extra, held_slots in zip(
        (q_all, k_all, v_all), sources, extras, (query_slots, slots, slots)
    ):
        begin = 0
        for source in group:
            held[begin : begin + source.shape[0], :] = source[...]
            begin += source.shape[0]
        patch(held, extra[0:last_count, :], held_slots, frames_local)
    query_places = [places[slot] for slot in query_slots]
    q_rows[0:HALO, :] = extras[0][last_count : last_count + HALO, :]
    for part in range(parts):
        begin = HALO + part * frames_local
        slot = slot_of(query_places, lax.axis_index("tm"), part)
        start = pl.multiple_of(slot * frames_local, HALO)
        q_rows[begin : begin + frames_local, :] = q_all[pl.ds(start, frames_local), :]
    q_rows[HALO + frames_shard :, :] = extras[0][last_count + HALO :, :]
    for line, ref in enumerate((first, last)):
        row = bounds[line : line + 1, :]
        ref[...] = jnp.transpose(jnp.broadcast_to(row, (LANES, row.shape[1])))


def attend_rows(places, begin, q_rows, k_all, v_all, first, last, frames_local, result, bias):
    count, width = result.shape
    rows = k_all.shape[0]
    time_index, model_index = lax.axis_index("tm"), lax.axis_index("mp")
    frames_shard = frames_local * lax.axis_size("mp")
    lows, highs = first[pl.ds(begin, count), :], last[pl.ds(begin, count), :]
    lanes = lax.broadcasted_iota(jnp.int32, (1, LANES), 1)
    for lane in range(0, rows, LANES):
        at = jnp.zeros((1, LANES), jnp.int32)
        for slot in range(lane // frames_local, -(-(lane + LANES) // frames_local)):
            if slot < len(places):
                slot_tm, slot_mp = places[slot]
                base = slot_tm(time_index) * frames_shard
                base += (model_index ^ slot_mp) * frames_local - slot * frames_local + lane
                at = jnp.where(lanes >= slot * frames_local - lane, lanes + base, at)
        at = at.astype(jnp.float32)
        bias[:, lane : lane + LANES] = jnp.where((at >= lows) & (at < highs), 0.0, -1e30)
    for lane in range(0, width, LANES):
        span = min(LANES, width - lane)
        q_pair = q_rows[pl.ds(begin, count), lane : lane + span]
        k_pair = k_all[:, lane : lane + span]
        v_pair = v_all[:, lane : lane + span]
        heads = span // HD
        head_of = lax.broadcasted_iota(jnp.int32, (count, span), 1) // HD
        scaled = q_pair * jnp.bfloat16(1.0 / math.sqrt(HD))
        stacked = jnp.concatenate(
            [jnp.where(head_of == head, scaled, jnp.zeros_like(scaled)) for head in range(heads)],
            axis=0,
        )
        scores = lax.dot_general(
            stacked, k_pair, (((1,), (1,)), ((), ())), preferred_element_type=jnp.float32
        )
        scores = scores + jnp.concatenate([bias[...]] * heads, axis=0)
        weights = jnp.exp(scores - jnp.max(scores, axis=1, keepdims=True))
        total = jnp.sum(weights, axis=1, keepdims=True)
        ratio = dot32(weights.astype(jnp.bfloat16), v_pair) / total
        merged = ratio[0:count]
        for head in range(1, heads):
            merged = jnp.where(head_of == head, ratio[head * count : (head + 1) * count], merged)
        result[:, lane : lane + span] = merged.astype(jnp.bfloat16)


def split_pair(model_index, result, mine, other, frames_local):
    window = mine.shape[0]
    place = lax.rem(model_index, 2) * frames_local
    mine[...] = result[pl.ds(pl.multiple_of(place, HALO), window), :]
    place = frames_local - place
    other[...] = result[pl.ds(pl.multiple_of(place, HALO), window), :]


def attend_far(places, query_slots, far, bounds, sources, extras, frames_local):
    width = sources[0][0].shape[1]
    query_count, rows = (sum(group.shape[0] for group in groups) for groups in sources[:2])
    sizes = [len(groups) for groups in sources]
    extended = frames_local * lax.axis_size("mp") + 2 * HALO
    window = frames_local + 2 * HALO
    pair = 2 * frames_local + 2 * HALO

    def kernel(bound_ref, *refs):
        groups = []
        for size in sizes:
            groups.append(refs[:size])
            refs = refs[size:]
        extra_refs, refs = refs[:3], refs[3:]
        windows, refs = refs[: 2 * len(far)], refs[2 * len(far) :]
        q_rows, k_all, v_all, first, last, q_all, result, bias = refs
        gather_rows(
            places,
            query_slots,
            bound_ref,
            groups,
            extra_refs,
            frames_local,
            (q_rows, k_all, v_all, q_all, first, last),
        )
        model_index = lax.axis_index("mp")
        for number, bit in enumerate(far):
            begin = pl.multiple_of((model_index ^ bit) // 2 * (2 * frames_local), HALO)
            attend_rows(
                places, begin, q_rows, k_all, v_all, first, last, frames_local, result, bias
            )
            split_pair(
                model_index, result, windows[2 * number], windows[2 * number + 1], frames_local
            )

    def shape(count, wide=width, dtype=jnp.bfloat16):
        return jax.ShapeDtypeStruct((count, wide), dtype)

    return call(
        kernel,
        [shape(window)] * (2 * len(far))
        + [shape(extended), shape(rows), shape(rows)]
        + [shape(extended, LANES, jnp.float32)] * 2,
        (bounds, *(array for groups in sources for array in groups), *extras),
        scratch=[
            pltpu.VMEM((query_count, width), jnp.bfloat16),
            pltpu.VMEM((pair, width), jnp.bfloat16),
            pltpu.VMEM((pair, rows), jnp.float32),
        ],
        micros=2.5 * len(far),
        vmem=16 + pair * rows * 20 // 1024 // 1024,
    )


def attend_near(places, after, q_rows, k_all, v_all, first, last, frames_local):
    rows, width = k_all.shape
    window = frames_local + 2 * HALO
    pair = 2 * frames_local + 2 * HALO

    def kernel(_, q_ref, k_ref, v_ref, first_ref, last_ref, mine, other, result, bias):
        model_index = lax.axis_index("mp")
        begin = pl.multiple_of(model_index // 2 * (2 * frames_local), HALO)
        attend_rows(
            places, begin, q_ref, k_ref, v_ref, first_ref, last_ref, frames_local, result, bias
        )
        split_pair(model_index, result, mine, other, frames_local)

    return call(
        kernel,
        [jax.ShapeDtypeStruct((window, width), jnp.bfloat16)] * 2,
        (after, q_rows, k_all, v_all, first, last),
        scratch=[
            pltpu.VMEM((pair, width), jnp.bfloat16),
            pltpu.VMEM((pair, rows), jnp.float32),
        ],
        micros=1.0,
        vmem=16 + pair * rows * 20 // 1024 // 1024,
    )


def far_branch_own(windows, w_own):
    count = len(windows)

    def kernel(*refs):
        for window, out in zip(refs[:count], refs[count + 1 :]):
            out[...] = dot32(window[...], refs[count][...])

    shape = jax.ShapeDtypeStruct((windows[0].shape[0], w_own.shape[1]), jnp.float32)
    return call(kernel, [shape] * count, (*windows, w_own), micros=0.4 * count)


def far_branch(shares, windows, w_near, cut):
    count = len(windows)

    def kernel(*refs):
        share_refs, window_refs, near, outs = (
            refs[:count],
            refs[count : 2 * count],
            refs[2 * count],
            refs[2 * count + 1 :],
        )
        for number, (share, window) in enumerate(zip(share_refs, window_refs)):
            total = (share[...] + dot32(window[...], near[...])).astype(jnp.bfloat16)
            outs[2 * number][...] = total[:cut]
            outs[2 * number + 1][...] = total[cut:]

    sizes = [cut, windows[0].shape[0] - cut] * count
    shapes = [jax.ShapeDtypeStruct((size, w_near.shape[1]), jnp.bfloat16) for size in sizes]
    return call(kernel, shapes, (*shares, *windows, w_near), micros=0.5 * count)


def near_branch(places, windows, w_rows, stacks, fixed, w_subsample, frames_local):
    counts = [stack.shape[0] for stack in stacks]
    depth, model = w_subsample.shape
    window = frames_local + 2 * HALO
    slots = len(places)

    def kernel(own, near, w_own, w_near, *refs):
        stack_refs, (fixed_ref, w_sub, out, held, taken) = refs[: len(counts)], refs[len(counts) :]
        begin = 0
        for stack_ref, count in zip(stack_refs, counts):
            for block in range(count):
                held[begin : begin + frames_local, :] = stack_of(stack_ref, block, 0, frames_local)
                begin += frames_local
        rows = last_rows(stack_refs, counts, frames_local, fixed_ref[...], fixed.shape[0])
        patch(held, rows, range(slots), frames_local)
        parts = lax.axis_size("mp")
        block = lax.axis_index("tm") * parts + lax.axis_index("mp") + parts

        def source(number, offset, count):
            slot = slot_of(places, number // parts - 1, lax.rem(number, parts))
            start = pl.multiple_of(slot * frames_local + offset, HALO)
            return held[pl.ds(start, count), :]

        taken[0:HALO, :] = source(block - 1, frames_local - HALO, HALO)
        taken[HALO : HALO + frames_local, :] = source(block, 0, frames_local)
        taken[HALO + frames_local : window, :] = source(block + 1, 0, HALO)
        features = dot32(taken[...], w_sub[...]).astype(jnp.bfloat16).astype(jnp.float32)
        share = dot32(own[...], w_own[...]) + dot32(near[...], w_near[...])
        out[...] = features + share

    return call(
        kernel,
        jax.ShapeDtypeStruct((window, model), jnp.float32),
        (*windows, *w_rows, *stacks, fixed, w_subsample),
        scratch=[
            pltpu.VMEM((slots * frames_local, depth), jnp.bfloat16),
            pltpu.VMEM((window, depth), jnp.bfloat16),
        ],
        micros=0.6,
    )


def convolve(held, taps, begin, count, here):
    offset = HALO - KERNEL // 2
    reach = count + 8
    rows = held[begin : begin + count + 2 * HALO, here]
    tap_rows = taps[:, here].astype(jnp.float32)
    total = jnp.zeros((count, rows.shape[1]), jnp.float32)
    for phase in range(8):
        share = jnp.zeros((reach, rows.shape[1]), jnp.float32)
        for tap in range(KERNEL):
            if (tap + offset) % 8 == phase:
                first = (tap + offset) // 8 * 8
                share += rows[first : first + reach] * tap_rows[tap : tap + 1]
        moved = pltpu.roll(share, reach - phase, axis=0) if phase else share
        total += moved[0:count]
    return total


def mix(base, shares, gain):
    mixed = base
    for share in shares:
        mixed += share[...].astype(jnp.float32)
    mixed = mixed.astype(jnp.bfloat16).astype(jnp.float32)
    return mixed, (normalize(mixed) * gain[...]).astype(jnp.bfloat16).astype(jnp.float32)


def silu(values):
    return values / (1.0 + jnp.exp(-values))


def finish_first(base, shares, gain, taps):
    count = len(shares)
    cut, model = shares[0].shape
    done = cut - 2 * HALO
    chunk = 2 * LANES

    def kernel(base_ref, *refs):
        share_refs, (gain_ref, tap_ref, out, held, mixed_rows) = refs[:count], refs[count:]
        mixed, conv_in = mix(base_ref[0:cut, :], share_refs, gain_ref)
        mixed_rows[...] = mixed
        held[...] = conv_in
        before = lax.axis_index("tm") * lax.axis_size("mp") + lax.axis_index("mp") > 0
        held[0:HALO, :] = jnp.where(before, conv_in[0:HALO], 0.0)
        for lane in range(0, model, chunk):
            here = slice(lane, lane + chunk)
            total = convolve(held, tap_ref, 0, done, here)
            out[:, here] = (mixed_rows[HALO : HALO + done, here] + silu(total)).astype(jnp.bfloat16)

    rows = jax.ShapeDtypeStruct((cut, model), jnp.float32)
    return call(
        kernel,
        (jax.ShapeDtypeStruct((done, model), jnp.bfloat16), rows, rows),
        (base, *shares, gain, taps),
        micros=0.5,
    )


def finish_last(base, shares, first, gain, taps, frames_local):
    count = len(shares)
    window, model = base.shape
    cut, done = first[1].shape[0], first[0].shape[0]
    left = frames_local - done
    chunk = 2 * LANES
    chunks = model // chunk

    def kernel(base_ref, *refs):
        share_refs, refs = refs[:count], refs[count:]
        out_ref, held_ref, mixed_ref, gain_ref, tap_ref, result, held, mixed_rows, staged, sems = refs
        copies = [pltpu.make_async_copy(out_ref, result.at[pl.ds(0, done)], sems.at[chunks])]
        copies[0].start()
        mixed, conv_in = mix(base_ref[cut:window, :], share_refs, gain_ref)
        mixed_rows[0:cut, :] = mixed_ref[...]
        mixed_rows[cut:window, :] = mixed
        held[0:cut, :] = held_ref[...]
        held[cut:window, :] = conv_in
        parts = lax.axis_size("mp")
        block = lax.axis_index("tm") * parts + lax.axis_index("mp")
        after = block < lax.axis_size("tm") * parts - 1
        held[window - HALO : window, :] = jnp.where(after, conv_in[window - HALO - cut :], 0.0)
        for number in range(chunks):
            here = slice(number * chunk, (number + 1) * chunk)
            total = convolve(held, tap_ref, done, left, here)
            kept = mixed_rows[HALO + done : HALO + frames_local, here]
            staged[:, here] = (kept + silu(total)).astype(jnp.bfloat16)
            copies.append(
                pltpu.make_async_copy(
                    staged.at[:, here], result.at[pl.ds(done, left), here], sems.at[number]
                )
            )
            copies[-1].start()
        for copy in copies:
            copy.wait()

    return call(
        kernel,
        jax.ShapeDtypeStruct((frames_local, model), jnp.bfloat16),
        (base, *shares, *first, gain, taps),
        scratch=[
            pltpu.VMEM((window, model), jnp.float32),
            pltpu.VMEM((window, model), jnp.float32),
            pltpu.VMEM((left, model), jnp.bfloat16),
            pltpu.SemaphoreType.DMA((chunks + 1,)),
        ],
        micros=1.5,
        result=pltpu.HBM,
    )


def exchange(block, axis, bit):
    return lax.ppermute(block, axis, [(i, i ^ bit) for i in range(lax.axis_size(axis))])


def shifted(block, axis, distance):
    count = lax.axis_size(axis)
    route = [(i - distance, i) for i in range(count) if 0 <= i - distance < count]
    return lax.ppermute(block, axis, route)


def shards(
    waveform,
    segment_start,
    segment_end,
    w_subsample,
    w_attention,
    w_output,
    gain_convolution,
    w_depthwise,
):
    frames_local = waveform.shape[0] // (SUB * HOP)
    frames_shard = segment_start.shape[0]
    parts, shards_total = lax.axis_size("mp"), lax.axis_size("tm")
    bits = [1 << b for b in reversed(range((parts - 1).bit_length()))]

    samples = waveform.reshape(-1, LANES)
    starts, ends = segment_start[None, :], segment_end[None, :]
    tables = jnp.asarray(front_tables())
    stacked = log_mel_rows(starts, ends, samples, tables, frames_local)
    *weights, kept = fetch(stacked, w_subsample, w_attention)

    w_near = exchange(w_output, "mp", bits[-1])

    reach = min((SEG_MAX + HALO - 2) // frames_shard + 1, shards_total - 1)
    whole = reach == shards_total - 1 and shards_total & (shards_total - 1) == 0
    if whole:
        order = [shards_total - 1, *range(1, shards_total - 1)]
        moves = [lambda tm, bit=bit: tm ^ bit for bit in order]
        column = [exchange(stacked, "tm", bit) for bit in order]
    else:
        steps = [sign * d for d in range(1, reach + 1) for sign in (1, -1)]
        moves = [lambda tm, step=step: tm - step for step in steps]
        column = [shifted(stacked, "tm", step) for step in steps]
    early = [(kept, [(lambda tm: tm, 0)])]
    late = [(assemble(column, weights[-1:]), [(move, 0) for move in moves])]

    def across(blocks, bit):
        return [
            (exchange(block, "mp", bit), [(move, mp ^ bit) for move, mp in held])
            for block, held in blocks
        ]

    for bit in bits[:-1]:
        early, late = early + across(early, bit), late + across(late, bit)
    ready = early + late[:1]
    joined = (assemble([block for block, _ in ready]), sum([held for _, held in ready], []))
    groups = [joined] + across([joined], bits[-1])
    projected = [
        project_rows(block, weights, frames_local, len(early)) for block, _ in groups
    ]
    done = [group[-1] for group in projected]
    late = [(assemble([block], done), held) for block, held in late[1:]]
    groups += late + across(late, bits[-1])
    stacks, held = zip(*groups)
    places = sum(held, [])
    joined_slots = range(len(joined[1]), 2 * len(joined[1]))
    query_slots = [*range(len(early)), *joined_slots[: len(early)]]
    fixed, bounds = boundary_rows(places, starts, ends, stacks, tables, frames_local)
    projected += [project_rows(block, weights, frames_local, 0) for block in stacks[2:-1]]
    outs = project_rows(stacks[-1], weights, frames_local, 0, (places, stacks, fixed))
    extras = (outs[0], outs[2], outs[4])
    queries = [group[0] for group in projected[:2]]
    keys = [*(group[-2] for group in projected), outs[1]]
    values = [*(group[-1] for group in projected), outs[3]]

    far = list(range(2, parts, 2))
    outs = attend_far(
        places, query_slots, far, bounds, (queries, keys, values), extras, frames_local
    )
    windows, shared = outs[: 2 * len(far)], outs[2 * len(far) :]
    arrived = [exchange(window, "mp", 1) for window in windows[1::2]]
    w_rows = (w_output, w_near)
    shares = far_branch_own(windows[0::2], w_output)
    shares = far_branch(shares, arrived, w_near, frames_local + HALO)
    mine, other = attend_near(places, shares[0], *shared, frames_local)
    shares = [exchange(share, "mp", far[number // 2]) for number, share in enumerate(shares)]
    base = near_branch(
        places, (mine, exchange(other, "mp", 1)), w_rows, stacks, fixed, weights[0], frames_local
    )
    gain = gain_convolution[None, :]
    first = finish_first(base, shares[0::2], gain, w_depthwise)
    return finish_last(base, shares[1::2], first, gain, w_depthwise, frames_local)


def solution(mesh):
    placed = (
        P(("groups", "tm", "mp")),
        P(("groups", "tm")),
        P(("groups", "tm")),
        P(),
        P(None, None, "mp"),
        P("mp", None),
        P(),
        P(),
    )
    return jax.shard_map(
        shards,
        mesh=mesh,
        in_specs=placed,
        out_specs=P(("groups", "tm", "mp"), None),
        check_vma=False,
    )
```

```python
import math

import jax
import jax.numpy as jnp
import ml_dtypes
import numpy as np
from jax import lax
from jax.experimental import pallas as pl
from jax.experimental.pallas import tpu as pltpu
from jax.sharding import PartitionSpec as P

HD = 64
NMEL = 128
NFFT = 400
HOP = 160
BINS = 256
SUB = 4
KERNEL = 31
SEG_MAX = 750
LANES = 128
HALO = 16
EXTRA = 8
FLOPS_PER_MICRO = 2000000000
TAIL_LINES = 3
HEAD_LINES = 2
DIGIT = 128
FRAME_ROWS = SUB * HOP // LANES
WIDE = -(-NFFT // LANES) * LANES


def split_high_low(table):
    high = table.astype(ml_dtypes.bfloat16)
    low = (table - high.astype(np.float32)).astype(ml_dtypes.bfloat16)
    return high, low


def fourier_table():
    sample_index = np.arange(NFFT)[:, None]
    bin_index = np.arange(BINS)[None, :]
    angle = (sample_index * bin_index % NFFT) * (2.0 * math.pi / NFFT)
    window = 0.5 - 0.5 * np.cos(np.arange(NFFT) * (2.0 * math.pi / NFFT))
    kept = bin_index <= NFFT // 2
    cosine = np.where(kept, np.cos(angle), 0.0) * window[:, None]
    sine = np.where(kept, -np.sin(angle), 0.0) * window[:, None]
    return np.concatenate([cosine, sine], axis=1).astype(np.float32)


def mel_bank():
    mel_top = 2595.0 * math.log10(1.0 + 8000.0 / 700.0)
    mel_points = np.arange(NMEL + 2) * (mel_top / (NMEL + 1))
    edges = 700.0 * (np.power(10.0, mel_points / 2595.0) - 1.0) * (NFFT / 16000.0)
    widths = np.maximum(edges[2:] - edges[1:-1], 1.0)
    bin_value = np.arange(BINS)[:, None]
    triangle = np.maximum(0.0, 1.0 - np.abs(bin_value - edges[None, 1:-1]) / widths[None, :])
    return np.where(bin_value <= NFFT // 2, triangle, 0.0).astype(np.float32)


def front_tables():
    high, low = split_high_low(fourier_table())
    bank = np.concatenate(split_high_low(mel_bank()), axis=1)
    bank = np.pad(bank, ((0, 0), (0, high.shape[1] - bank.shape[1])))
    return np.concatenate([high, low, bank], axis=0)


def dot32(left, right):
    return jnp.dot(left, right, preferred_element_type=jnp.float32)


def dot_split(values, table_high, table_low):
    high = values.astype(jnp.bfloat16)
    low = (values - high.astype(jnp.float32)).astype(jnp.bfloat16)
    table = table_high()
    large, small = dot32(high, table), dot32(low, table)
    return large + (small + dot32(high, table_low()))


def normalize(values):
    center = jnp.mean(values, axis=-1, keepdims=True)
    shifted = values - center
    spread = jnp.mean(jnp.square(shifted), axis=-1, keepdims=True)
    return shifted * lax.rsqrt(spread + 1e-05)


def call(
    kernel, out_shape, operands, scratch=(), micros=1.0, remote=0, vmem=16, result=pltpu.VMEM
):
    specs = [pl.BlockSpec(memory_space=pltpu.VMEM)] * (len(operands) - remote)
    specs += [pl.BlockSpec(memory_space=pltpu.HBM)] * remote
    return pl.pallas_call(
        kernel,
        out_shape=out_shape,
        in_specs=specs,
        out_specs=jax.tree.map(lambda _: pl.BlockSpec(memory_space=result), out_shape),
        scratch_shapes=list(scratch),
        compiler_params=pltpu.CompilerParams(vmem_limit_bytes=vmem * 1024 * 1024),
        cost_estimate=pl.CostEstimate(
            flops=int(micros * FLOPS_PER_MICRO), bytes_accessed=1000000, transcendentals=0
        ),
    )(*operands)


def fetch(stacked, w_subsample, w_attention):
    parts, _, width = w_attention.shape

    def kernel(stack_ref, w_sub, w_att, out_sub, out_att, sums, out_stack, sems):
        out_stack[...] = stack_ref[...]
        copies = [
            pltpu.make_async_copy(w_att, out_att, sems.at[0]),
            pltpu.make_async_copy(w_sub, out_sub, sems.at[1]),
        ]
        for copy in copies:
            copy.start()
        for copy in copies:
            copy.wait()
        sums[...] = jnp.zeros_like(sums)
        for part in range(parts):
            columns = out_att[part].astype(jnp.float32)
            sums[part : part + 1, :] = jnp.sum(columns, axis=0, keepdims=True)

    return call(
        kernel,
        [jax.ShapeDtypeStruct(array.shape, array.dtype) for array in (w_subsample, w_attention)]
        + [
            jax.ShapeDtypeStruct((8, width), jnp.float32),
            jax.ShapeDtypeStruct(stacked.shape, stacked.dtype),
        ],
        (stacked, w_subsample, w_attention),
        scratch=[pltpu.SemaphoreType.DMA((2,))],
        remote=2,
    )


def stack_of(ref, block, begin, end):
    half = (ref.shape[1] - EXTRA) // 2
    return jnp.concatenate([ref[block, begin:end, :], ref[block, half + begin : half + end, :]], axis=1)


def log_mel(windows, tables, copies=()):
    lanes = lax.broadcasted_iota(jnp.int32, windows.shape, 1)
    windows = jnp.where(lanes < NFFT, windows, 0.0)

    def fetched(number, begin):
        def load():
            if copies:
                copies[number].wait()
            return tables[begin : begin + WIDE, :]

        return load

    spectrum = dot_split(windows, fetched(0, 0), fetched(1, NFFT))
    power = jnp.square(spectrum[:, :BINS]) + jnp.square(spectrum[:, BINS:])
    bank = [tables[2 * NFFT :, part * NMEL : (part + 1) * NMEL] for part in range(2)]
    return jnp.log(dot_split(power, lambda: bank[0], lambda: bank[1]) + 1e-06)


def log_mel_rows(starts, ends, samples, tables, frames_local):
    rows = frames_local * FRAME_ROWS
    frames_shard = starts.shape[1]

    spans = (pl.ds(0, WIDE), pl.ds(WIDE, tables.shape[0] - WIDE))

    def kernel(start, end, wave, table, out, held, start_ref, end_ref, tables_ref, sems):
        pairs = (
            (wave, held.at[pl.ds(0, rows)]),
            (start, start_ref),
            (end, end_ref),
        ) + tuple((table.at[span], tables_ref.at[span]) for span in spans)
        copies = [
            pltpu.make_async_copy(source, target, sems.at[slot])
            for slot, (source, target) in enumerate(pairs)
        ]
        for copy in copies:
            copy.start()
        held[rows : rows + 8, :] = jnp.zeros((8, LANES), jnp.float32)
        for copy in copies[:3]:
            copy.wait()
        lines = [held[pl.ds(j, frames_local, stride=FRAME_ROWS), :] for j in range(FRAME_ROWS + 2)]
        windows = []
        for sub in range(SUB):
            line, lane = divmod(sub * HOP, LANES)
            taken = jnp.concatenate(lines[line : line + WIDE // LANES], axis=1)
            windows.append(pltpu.roll(taken, WIDE - lane, axis=1) if lane else taken)
        pieces = []
        for taken in (range(rows - TAIL_LINES, rows), range(HEAD_LINES)):
            line = jnp.concatenate([held[row : row + 1, :] for row in taken], axis=1)
            high = line.astype(jnp.bfloat16).astype(jnp.float32)
            pieces += [high, line - high]
        for ref in (start_ref, end_ref):
            edge = jnp.concatenate([ref[:, :HALO], ref[:, frames_shard - HALO :]], axis=1)
            high = edge // DIGIT
            low = edge - high * DIGIT
            pieces += [digit.astype(jnp.float32) for digit in (high, low)]
        filled = sum(piece.shape[1] for piece in pieces)
        pieces.append(jnp.zeros((1, EXTRA * 2 * NMEL - filled), jnp.float32))
        flat = jnp.concatenate(pieces, axis=1)
        extras = [flat[:, row * 2 * NMEL : (row + 1) * 2 * NMEL] for row in range(EXTRA)]
        out[0, 2 * frames_local :, :] = jnp.concatenate(extras, axis=0).astype(jnp.bfloat16)
        mel = log_mel(jnp.concatenate(windows, axis=0), tables_ref, copies[3:])
        for sub in range(SUB):
            begin, lane = sub // 2 * frames_local, sub % 2 * NMEL
            out[0, begin : begin + frames_local, lane : lane + NMEL] = mel[
                sub * frames_local : (sub + 1) * frames_local
            ].astype(jnp.bfloat16)

    return call(
        kernel,
        jax.ShapeDtypeStruct((1, 2 * frames_local + EXTRA, 2 * NMEL), jnp.bfloat16),
        (starts, ends, samples, tables),
        scratch=[
            pltpu.VMEM((rows + 8, LANES), jnp.float32),
            pltpu.VMEM(starts.shape, starts.dtype),
            pltpu.VMEM(ends.shape, ends.dtype),
            pltpu.VMEM(tables.shape, tables.dtype),
            pltpu.SemaphoreType.DMA((5,)),
        ],
        remote=4,
        vmem=54,
        micros=1.0,
    )


def boundary_rows(places, starts, ends, stacks, tables, frames_local):
    counts = [stack.shape[0] for stack in stacks]
    slots = len(places)
    rows = -(-slots // HALO) * HALO
    frames_shard = starts.shape[1]
    parts = lax.axis_size("mp")
    final = lax.axis_size("tm") * parts - 1
    shift = final + 1

    def kernel(start_ref, end_ref, *refs):
        stack_refs, refs = refs[: len(counts)], refs[len(counts) :]
        tables_ref, out, bounds, tails, heads, nexts, edges, order = refs
        time_index, model_index = lax.axis_index("tm"), lax.axis_index("mp")
        tails[...] = jnp.zeros_like(tails)
        nexts[...] = jnp.zeros_like(nexts)
        slot = 0
        for stack_ref, count in zip(stack_refs, counts):
            for block in range(count):
                kept = stack_ref[block, 2 * frames_local :, :].astype(jnp.float32)
                flat = jnp.concatenate([kept[row : row + 1] for row in range(EXTRA)], axis=1)
                here = slice(slot, slot + 1)
                tail, head = TAIL_LINES * LANES, HEAD_LINES * LANES
                tails[here, :] = flat[:, :tail] + flat[:, tail : 2 * tail]
                heads[here, :] = flat[:, 2 * tail : 2 * tail + head] + flat[
                    :, 2 * tail + head : 2 * (tail + head)
                ]
                digits = flat[:, 2 * (tail + head) :]
                for line in range(2):
                    high = digits[:, 4 * line * HALO : (4 * line + 2) * HALO]
                    low = digits[:, (4 * line + 2) * HALO : (4 * line + 4) * HALO]
                    edges[line, here, 0 : 2 * HALO] = high * DIGIT + low
                slot += 1
        numbers = [
            slot_tm(time_index) * parts + (model_index ^ slot_mp) for slot_tm, slot_mp in places
        ]
        for number in numbers:
            order[number + 1 + shift] = jnp.int32(0)
        for slot, number in enumerate(numbers):
            order[number + shift] = jnp.int32(slot)
        for slot, number in enumerate(numbers):
            taken = heads[pl.ds(order[number + 1 + shift], 1), :]
            nexts[slot : slot + 1, :] = jnp.where(number == final, 0.0, taken)
        line = jnp.concatenate([tails[...], nexts[...]], axis=1)
        windows = []
        for sub in range(SUB - 2, SUB):
            skip, lane = divmod(sub * HOP - (FRAME_ROWS - TAIL_LINES) * LANES, LANES)
            windows.append(
                pltpu.roll(line[:, skip * LANES : skip * LANES + WIDE], WIDE - lane, axis=1)
            )
        mel = log_mel(jnp.concatenate(windows, axis=0), tables_ref).astype(jnp.bfloat16)
        for number in range(2):
            lane = number * NMEL
            out[:, lane : lane + NMEL] = mel[number * rows : (number + 1) * rows]
        left = slot_of(places, time_index - 1, model_index)
        right = slot_of(places, time_index + 1, model_index)
        for number, ref in enumerate((start_ref, end_ref)):
            bounds[number : number + 1, :] = jnp.concatenate(
                [
                    edges[number, pl.ds(left, 1), :][:, HALO : 2 * HALO],
                    ref[...].astype(jnp.float32),
                    edges[number, pl.ds(right, 1), :][:, 0:HALO],
                ],
                axis=1,
            )

    return call(
        kernel,
        (
            jax.ShapeDtypeStruct((rows, 2 * NMEL), jnp.bfloat16),
            jax.ShapeDtypeStruct((2, frames_shard + 2 * HALO), jnp.float32),
        ),
        (starts, ends, *stacks, tables),
        scratch=[
            pltpu.VMEM((rows, TAIL_LINES * LANES), jnp.float32),
            pltpu.VMEM((rows, HEAD_LINES * LANES), jnp.float32),
            pltpu.VMEM((rows, HEAD_LINES * LANES), jnp.float32),
            pltpu.VMEM((2, rows, LANES), jnp.float32),
            pltpu.SMEM((3 * shift,), jnp.int32),
        ],
        micros=0.9,
    )


def last_rows(stack_refs, counts, frames_local, fixed, rows):
    lasts = []
    for stack_ref, count in zip(stack_refs, counts):
        for block in range(count):
            kept = stack_ref[block, frames_local - HALO : frames_local, :]
            lasts.append(kept.astype(jnp.float32)[HALO - 1 : HALO])
    if len(lasts) < rows:
        lasts.append(jnp.zeros((rows - len(lasts), 2 * NMEL), jnp.float32))
    return jnp.concatenate([jnp.concatenate(lasts, axis=0).astype(jnp.bfloat16), fixed], axis=1)


def patch(held, fixed, slots, frames_local):
    fixed = fixed.astype(jnp.float32)
    for number, slot in enumerate(slots):
        here = slice((number + 1) * frames_local - HALO, (number + 1) * frames_local)
        kept = held[here, :].astype(jnp.float32)
        last = lax.broadcasted_iota(jnp.int32, kept.shape, 0) == HALO - 1
        held[here, :] = jnp.where(last, fixed[slot : slot + 1, :], kept).astype(held.dtype)


def assemble(parts, after=()):
    counts = [part.shape[0] for part in parts]

    def kernel(*refs):
        begin = 0
        for ref, count in zip(refs, counts):
            refs[-1][begin : begin + count] = ref[...]
            begin += count

    shape = jax.ShapeDtypeStruct((sum(counts), *parts[0].shape[1:]), parts[0].dtype)
    return call(kernel, shape, (*parts, *after))


def slot_of(places, tm, mp):
    found = jnp.int32(0)
    for slot, (slot_tm, slot_mp) in enumerate(places):
        here = (slot_tm(lax.axis_index("tm")) == tm) & (lax.axis_index("mp") ^ slot_mp == mp)
        found = jnp.where(here, slot, found)
    return found


def project_rows(stack, weights, frames_local, query_blocks, boundary=None):
    count = stack.shape[0]
    rows, width = count * frames_local, weights[1].shape[2]
    query_rows = query_blocks * frames_local
    places, every, fixed = boundary or ((), (), jnp.zeros((0, 2 * NMEL), jnp.bfloat16))
    counts = [block.shape[0] for block in every]
    last_count = fixed.shape[0]
    extra_rows = last_count + 2 * HALO if boundary else 0

    def boundary_stack(every_refs, fixed_ref, lasts, heads, tails):
        lasts[...] = last_rows(
            every_refs, counts, frames_local, fixed_ref[...], last_count
        ).astype(jnp.float32)
        slot = 0
        for ref, blocks in zip(every_refs, counts):
            for block in range(blocks):
                heads[slot] = stack_of(ref, block, 0, HALO)
                tails[slot] = stack_of(ref, block, frames_local - HALO, frames_local)
                slot += 1
        time_index, parts = lax.axis_index("tm"), lax.axis_size("mp")
        left = slot_of(places, time_index - 1, parts - 1)
        right = slot_of(places, time_index + 1, 0)
        tail = tails[left].astype(jnp.float32)
        final = lax.broadcasted_iota(jnp.int32, tail.shape, 0) == HALO - 1
        tail = jnp.where(final, lasts[pl.ds(left, 1), :], tail).astype(jnp.bfloat16)
        return [lasts[...].astype(jnp.bfloat16), tail, heads[right]]

    def kernel(stack_ref, w_sub, w_att, sums, *refs):
        stack_rows = [stack_of(stack_ref, block, 0, frames_local) for block in range(count)]
        if boundary:
            every_refs, refs = refs[: len(every)], refs[len(every) :]
            fixed_ref, *refs = refs
            refs, scratch = refs[:-3], refs[-3:]
            stack_rows += boundary_stack(every_refs, fixed_ref, *scratch)
        features = dot32(jnp.concatenate(stack_rows, axis=0), w_sub[...]).astype(jnp.bfloat16)
        wide = features.astype(jnp.float32)
        center = jnp.mean(wide, axis=-1, keepdims=True)
        spread = jnp.mean(jnp.square(wide - center), axis=-1, keepdims=True)
        scale = lax.rsqrt(spread + 1e-05)

        def projected(part, begin, end):
            product = dot32(features[begin:end], w_att[part])
            shifted = product - center[begin:end] * sums[part : part + 1, :]
            return (shifted * scale[begin:end]).astype(jnp.bfloat16)

        refs = list(refs)
        if query_rows:
            refs.pop(0)[...] = projected(0, 0, query_rows)
        if extra_rows:
            refs.pop(0)[...] = projected(0, rows, rows + extra_rows)
        for part in (1, 2):
            both = projected(part, 0, rows + extra_rows)
            refs.pop(0)[...] = both[:rows]
            if extra_rows:
                refs.pop(0)[...] = both[rows:]

    def shape(size):
        return jax.ShapeDtypeStruct((size, width), jnp.bfloat16)

    shapes = [shape(query_rows)] * bool(query_rows) + [shape(extra_rows)] * bool(extra_rows)
    shapes += ([shape(rows)] + [shape(extra_rows)] * bool(extra_rows)) * 2
    depth = weights[0].shape[0]
    return call(
        kernel,
        shapes,
        (stack, *weights, *every) + ((fixed,) if boundary else ()),
        scratch=[
            pltpu.VMEM((last_count, depth), jnp.float32),
            pltpu.VMEM((len(places), HALO, depth), jnp.bfloat16),
            pltpu.VMEM((len(places), HALO, depth), jnp.bfloat16),
        ]
        if boundary
        else [],
        micros=0.5 + 0.006 * (rows + extra_rows),
    )


def gather_rows(places, query_slots, bounds, sources, extras, frames_local, outs):
    q_rows, k_all, v_all, q_all, first, last = outs
    parts = lax.axis_size("mp")
    frames_shard = frames_local * parts
    last_count = extras[0].shape[0] - 2 * HALO
    slots = range(len(places))
    for held, group, extra, held_slots in zip(
        (q_all, k_all, v_all), sources, extras, (query_slots, slots, slots)
    ):
        begin = 0
        for source in group:
            held[begin : begin + source.shape[0], :] = source[...]
            begin += source.shape[0]
        patch(held, extra[0:last_count, :], held_slots, frames_local)
    query_places = [places[slot] for slot in query_slots]
    q_rows[0:HALO, :] = extras[0][last_count : last_count + HALO, :]
    for part in range(parts):
        begin = HALO + part * frames_local
        slot = slot_of(query_places, lax.axis_index("tm"), part)
        start = pl.multiple_of(slot * frames_local, HALO)
        q_rows[begin : begin + frames_local, :] = q_all[pl.ds(start, frames_local), :]
    q_rows[HALO + frames_shard :, :] = extras[0][last_count + HALO :, :]
    for line, ref in enumerate((first, last)):
        row = bounds[line : line + 1, :]
        ref[...] = jnp.transpose(jnp.broadcast_to(row, (LANES, row.shape[1])))


def attend_rows(places, begin, q_rows, k_all, v_all, first, last, frames_local, result, bias):
    count, width = result.shape
    rows = k_all.shape[0]
    time_index, model_index = lax.axis_index("tm"), lax.axis_index("mp")
    frames_shard = frames_local * lax.axis_size("mp")
    lows, highs = first[pl.ds(begin, count), :], last[pl.ds(begin, count), :]
    lanes = lax.broadcasted_iota(jnp.int32, (1, LANES), 1)
    for lane in range(0, rows, LANES):
        at = jnp.zeros((1, LANES), jnp.int32)
        for slot in range(lane // frames_local, -(-(lane + LANES) // frames_local)):
            if slot < len(places):
                slot_tm, slot_mp = places[slot]
                base = slot_tm(time_index) * frames_shard
                base += (model_index ^ slot_mp) * frames_local - slot * frames_local + lane
                at = jnp.where(lanes >= slot * frames_local - lane, lanes + base, at)
        at = at.astype(jnp.float32)
        bias[:, lane : lane + LANES] = jnp.where((at >= lows) & (at < highs), 0.0, -1e30)
    for lane in range(0, width, LANES):
        span = min(LANES, width - lane)
        q_pair = q_rows[pl.ds(begin, count), lane : lane + span]
        k_pair = k_all[:, lane : lane + span]
        v_pair = v_all[:, lane : lane + span]
        heads = span // HD
        head_of = lax.broadcasted_iota(jnp.int32, (count, span), 1) // HD
        scaled = q_pair * jnp.bfloat16(1.0 / math.sqrt(HD))
        stacked = jnp.concatenate(
            [jnp.where(head_of == head, scaled, jnp.zeros_like(scaled)) for head in range(heads)],
            axis=0,
        )
        scores = lax.dot_general(
            stacked, k_pair, (((1,), (1,)), ((), ())), preferred_element_type=jnp.float32
        )
        scores = scores + jnp.concatenate([bias[...]] * heads, axis=0)
        weights = jnp.exp(scores - jnp.max(scores, axis=1, keepdims=True))
        total = jnp.sum(weights, axis=1, keepdims=True)
        ratio = dot32(weights.astype(jnp.bfloat16), v_pair) / total
        merged = ratio[0:count]
        for head in range(1, heads):
            merged = jnp.where(head_of == head, ratio[head * count : (head + 1) * count], merged)
        result[:, lane : lane + span] = merged.astype(jnp.bfloat16)


def split_pair(model_index, result, mine, other, frames_local):
    window = mine.shape[0]
    place = lax.rem(model_index, 2) * frames_local
    mine[...] = result[pl.ds(pl.multiple_of(place, HALO), window), :]
    place = frames_local - place
    other[...] = result[pl.ds(pl.multiple_of(place, HALO), window), :]


def attend_far(places, query_slots, far, bounds, sources, extras, frames_local):
    width = sources[0][0].shape[1]
    query_count, rows = (sum(group.shape[0] for group in groups) for groups in sources[:2])
    sizes = [len(groups) for groups in sources]
    extended = frames_local * lax.axis_size("mp") + 2 * HALO
    window = frames_local + 2 * HALO
    pair = 2 * frames_local + 2 * HALO

    def kernel(bound_ref, *refs):
        groups = []
        for size in sizes:
            groups.append(refs[:size])
            refs = refs[size:]
        extra_refs, refs = refs[:3], refs[3:]
        windows, refs = refs[: 2 * len(far)], refs[2 * len(far) :]
        q_rows, k_all, v_all, first, last, q_all, result, bias = refs
        gather_rows(
            places,
            query_slots,
            bound_ref,
            groups,
            extra_refs,
            frames_local,
            (q_rows, k_all, v_all, q_all, first, last),
        )
        model_index = lax.axis_index("mp")
        for number, bit in enumerate(far):
            begin = pl.multiple_of((model_index ^ bit) // 2 * (2 * frames_local), HALO)
            attend_rows(
                places, begin, q_rows, k_all, v_all, first, last, frames_local, result, bias
            )
            split_pair(
                model_index, result, windows[2 * number], windows[2 * number + 1], frames_local
            )

    def shape(count, wide=width, dtype=jnp.bfloat16):
        return jax.ShapeDtypeStruct((count, wide), dtype)

    return call(
        kernel,
        [shape(window)] * (2 * len(far))
        + [shape(extended), shape(rows), shape(rows)]
        + [shape(extended, LANES, jnp.float32)] * 2,
        (bounds, *(array for groups in sources for array in groups), *extras),
        scratch=[
            pltpu.VMEM((query_count, width), jnp.bfloat16),
            pltpu.VMEM((pair, width), jnp.bfloat16),
            pltpu.VMEM((pair, rows), jnp.float32),
        ],
        micros=2.5 * len(far),
        vmem=16 + pair * rows * 20 // 1024 // 1024,
    )


def attend_near(places, after, q_rows, k_all, v_all, first, last, frames_local):
    rows, width = k_all.shape
    window = frames_local + 2 * HALO
    pair = 2 * frames_local + 2 * HALO

    def kernel(_, q_ref, k_ref, v_ref, first_ref, last_ref, mine, other, result, bias):
        model_index = lax.axis_index("mp")
        begin = pl.multiple_of(model_index // 2 * (2 * frames_local), HALO)
        attend_rows(
            places, begin, q_ref, k_ref, v_ref, first_ref, last_ref, frames_local, result, bias
        )
        split_pair(model_index, result, mine, other, frames_local)

    return call(
        kernel,
        [jax.ShapeDtypeStruct((window, width), jnp.bfloat16)] * 2,
        (after, q_rows, k_all, v_all, first, last),
        scratch=[
            pltpu.VMEM((pair, width), jnp.bfloat16),
            pltpu.VMEM((pair, rows), jnp.float32),
        ],
        micros=1.0,
        vmem=16 + pair * rows * 20 // 1024 // 1024,
    )


def far_branch_own(windows, w_own):
    count = len(windows)

    def kernel(*refs):
        for window, out in zip(refs[:count], refs[count + 1 :]):
            out[...] = dot32(window[...], refs[count][...])

    shape = jax.ShapeDtypeStruct((windows[0].shape[0], w_own.shape[1]), jnp.float32)
    return call(kernel, [shape] * count, (*windows, w_own), micros=0.4 * count)


def far_branch(shares, windows, w_near, cut):
    count = len(windows)

    def kernel(*refs):
        share_refs, window_refs, near, outs = (
            refs[:count],
            refs[count : 2 * count],
            refs[2 * count],
            refs[2 * count + 1 :],
        )
        for number, (share, window) in enumerate(zip(share_refs, window_refs)):
            total = (share[...] + dot32(window[...], near[...])).astype(jnp.bfloat16)
            outs[2 * number][...] = total[:cut]
            outs[2 * number + 1][...] = total[cut:]

    sizes = [cut, windows[0].shape[0] - cut] * count
    shapes = [jax.ShapeDtypeStruct((size, w_near.shape[1]), jnp.bfloat16) for size in sizes]
    return call(kernel, shapes, (*shares, *windows, w_near), micros=0.5 * count)


def near_branch(places, windows, w_rows, stacks, fixed, w_subsample, frames_local):
    counts = [stack.shape[0] for stack in stacks]
    depth, model = w_subsample.shape
    window = frames_local + 2 * HALO
    slots = len(places)

    def kernel(own, near, w_own, w_near, *refs):
        stack_refs, (fixed_ref, w_sub, out, held, taken) = refs[: len(counts)], refs[len(counts) :]
        begin = 0
        for stack_ref, count in zip(stack_refs, counts):
            for block in range(count):
                held[begin : begin + frames_local, :] = stack_of(stack_ref, block, 0, frames_local)
                begin += frames_local
        rows = last_rows(stack_refs, counts, frames_local, fixed_ref[...], fixed.shape[0])
        patch(held, rows, range(slots), frames_local)
        parts = lax.axis_size("mp")
        block = lax.axis_index("tm") * parts + lax.axis_index("mp") + parts

        def source(number, offset, count):
            slot = slot_of(places, number // parts - 1, lax.rem(number, parts))
            start = pl.multiple_of(slot * frames_local + offset, HALO)
            return held[pl.ds(start, count), :]

        taken[0:HALO, :] = source(block - 1, frames_local - HALO, HALO)
        taken[HALO : HALO + frames_local, :] = source(block, 0, frames_local)
        taken[HALO + frames_local : window, :] = source(block + 1, 0, HALO)
        features = dot32(taken[...], w_sub[...]).astype(jnp.bfloat16).astype(jnp.float32)
        share = dot32(own[...], w_own[...]) + dot32(near[...], w_near[...])
        out[...] = features + share

    return call(
        kernel,
        jax.ShapeDtypeStruct((window, model), jnp.float32),
        (*windows, *w_rows, *stacks, fixed, w_subsample),
        scratch=[
            pltpu.VMEM((slots * frames_local, depth), jnp.bfloat16),
            pltpu.VMEM((window, depth), jnp.bfloat16),
        ],
        micros=0.6,
    )


def convolve(held, taps, begin, count, here):
    offset = HALO - KERNEL // 2
    reach = count + 8
    rows = held[begin : begin + count + 2 * HALO, here]
    tap_rows = taps[:, here].astype(jnp.float32)
    total = jnp.zeros((count, rows.shape[1]), jnp.float32)
    for phase in range(8):
        share = jnp.zeros((reach, rows.shape[1]), jnp.float32)
        for tap in range(KERNEL):
            if (tap + offset) % 8 == phase:
                first = (tap + offset) // 8 * 8
                share += rows[first : first + reach] * tap_rows[tap : tap + 1]
        moved = pltpu.roll(share, reach - phase, axis=0) if phase else share
        total += moved[0:count]
    return total


def mix(base, shares, gain):
    mixed = base
    for share in shares:
        mixed += share[...].astype(jnp.float32)
    mixed = mixed.astype(jnp.bfloat16).astype(jnp.float32)
    return mixed, (normalize(mixed) * gain[...]).astype(jnp.bfloat16).astype(jnp.float32)


def silu(values):
    return values / (1.0 + jnp.exp(-values))


def finish_first(base, shares, gain, taps):
    count = len(shares)
    cut, model = shares[0].shape
    done = cut - 2 * HALO
    chunk = 2 * LANES

    def kernel(base_ref, *refs):
        share_refs, (gain_ref, tap_ref, out, held, mixed_rows) = refs[:count], refs[count:]
        mixed, conv_in = mix(base_ref[0:cut, :], share_refs, gain_ref)
        mixed_rows[...] = mixed
        held[...] = conv_in
        before = lax.axis_index("tm") * lax.axis_size("mp") + lax.axis_index("mp") > 0
        held[0:HALO, :] = jnp.where(before, conv_in[0:HALO], 0.0)
        for lane in range(0, model, chunk):
            here = slice(lane, lane + chunk)
            total = convolve(held, tap_ref, 0, done, here)
            out[:, here] = (mixed_rows[HALO : HALO + done, here] + silu(total)).astype(jnp.bfloat16)

    rows = jax.ShapeDtypeStruct((cut, model), jnp.float32)
    return call(
        kernel,
        (jax.ShapeDtypeStruct((done, model), jnp.bfloat16), rows, rows),
        (base, *shares, gain, taps),
        micros=0.5,
    )


def finish_last(base, shares, first, gain, taps, frames_local):
    count = len(shares)
    window, model = base.shape
    cut, done = first[1].shape[0], first[0].shape[0]
    left = frames_local - done
    chunk = 2 * LANES
    chunks = model // chunk

    def kernel(base_ref, *refs):
        share_refs, refs = refs[:count], refs[count:]
        out_ref, held_ref, mixed_ref, gain_ref, tap_ref, result, held, mixed_rows, staged, sems = refs
        copies = [pltpu.make_async_copy(out_ref, result.at[pl.ds(0, done)], sems.at[chunks])]
        copies[0].start()
        mixed, conv_in = mix(base_ref[cut:window, :], share_refs, gain_ref)
        mixed_rows[0:cut, :] = mixed_ref[...]
        mixed_rows[cut:window, :] = mixed
        held[0:cut, :] = held_ref[...]
        held[cut:window, :] = conv_in
        parts = lax.axis_size("mp")
        block = lax.axis_index("tm") * parts + lax.axis_index("mp")
        after = block < lax.axis_size("tm") * parts - 1
        held[window - HALO : window, :] = jnp.where(after, conv_in[window - HALO - cut :], 0.0)
        for number in range(chunks):
            here = slice(number * chunk, (number + 1) * chunk)
            total = convolve(held, tap_ref, done, left, here)
            kept = mixed_rows[HALO + done : HALO + frames_local, here]
            staged[:, here] = (kept + silu(total)).astype(jnp.bfloat16)
            copies.append(
                pltpu.make_async_copy(
                    staged.at[:, here], result.at[pl.ds(done, left), here], sems.at[number]
                )
            )
            copies[-1].start()
        for copy in copies:
            copy.wait()

    return call(
        kernel,
        jax.ShapeDtypeStruct((frames_local, model), jnp.bfloat16),
        (base, *shares, *first, gain, taps),
        scratch=[
            pltpu.VMEM((window, model), jnp.float32),
            pltpu.VMEM((window, model), jnp.float32),
            pltpu.VMEM((left, model), jnp.bfloat16),
            pltpu.SemaphoreType.DMA((chunks + 1,)),
        ],
        micros=1.5,
        result=pltpu.HBM,
    )


def exchange(block, axis, bit):
    return lax.ppermute(block, axis, [(i, i ^ bit) for i in range(lax.axis_size(axis))])


def shifted(block, axis, distance):
    count = lax.axis_size(axis)
    route = [(i - distance, i) for i in range(count) if 0 <= i - distance < count]
    return lax.ppermute(block, axis, route)


def shards(
    waveform,
    segment_start,
    segment_end,
    w_subsample,
    w_attention,
    w_output,
    gain_convolution,
    w_depthwise,
):
    frames_local = waveform.shape[0] // (SUB * HOP)
    frames_shard = segment_start.shape[0]
    parts, shards_total = lax.axis_size("mp"), lax.axis_size("tm")
    bits = [1 << b for b in reversed(range((parts - 1).bit_length()))]

    samples = waveform.reshape(-1, LANES)
    starts, ends = segment_start[None, :], segment_end[None, :]
    tables = jnp.asarray(front_tables())
    stacked = log_mel_rows(starts, ends, samples, tables, frames_local)
    *weights, kept = fetch(stacked, w_subsample, w_attention)

    w_near = exchange(w_output, "mp", bits[-1])

    reach = min((SEG_MAX + HALO - 2) // frames_shard + 1, shards_total - 1)
    whole = reach == shards_total - 1 and shards_total & (shards_total - 1) == 0
    if whole:
        order = dict.fromkeys([shards_total // 2, shards_total - 1, *range(1, shards_total)])
        moves = [lambda tm, bit=bit: tm ^ bit for bit in order]
        column = [exchange(stacked, "tm", bit) for bit in order]
    else:
        steps = [sign * d for d in range(1, reach + 1) for sign in (1, -1)]
        moves = [lambda tm, step=step: tm - step for step in steps]
        column = [shifted(stacked, "tm", step) for step in steps]
    early = [(kept, [(lambda tm: tm, 0)])]
    late = [(assemble(column, weights[-1:]), [(move, 0) for move in moves])]

    def across(blocks, bit):
        return [
            (exchange(block, "mp", bit), [(move, mp ^ bit) for move, mp in held])
            for block, held in blocks
        ]

    for bit in bits[:-1]:
        early, late = early + across(early, bit), late + across(late, bit)
    ready = early + late[:1]
    joined = (assemble([block for block, _ in ready]), sum([held for _, held in ready], []))
    groups = [joined] + across([joined], bits[-1])
    projected = [
        project_rows(block, weights, frames_local, len(early)) for block, _ in groups
    ]
    done = [group[-1] for group in projected]
    late = [(assemble([block], done), held) for block, held in late[1:]]
    groups += late + across(late, bits[-1])
    stacks, held = zip(*groups)
    places = sum(held, [])
    joined_slots = range(len(joined[1]), 2 * len(joined[1]))
    query_slots = [*range(len(early)), *joined_slots[: len(early)]]
    fixed, bounds = boundary_rows(places, starts, ends, stacks, tables, frames_local)
    projected += [project_rows(block, weights, frames_local, 0) for block in stacks[2:-1]]
    outs = project_rows(stacks[-1], weights, frames_local, 0, (places, stacks, fixed))
    extras = (outs[0], outs[2], outs[4])
    queries = [group[0] for group in projected[:2]]
    keys = [*(group[-2] for group in projected), outs[1]]
    values = [*(group[-1] for group in projected), outs[3]]

    far = list(range(2, parts, 2))
    outs = attend_far(
        places, query_slots, far, bounds, (queries, keys, values), extras, frames_local
    )
    windows, shared = outs[: 2 * len(far)], outs[2 * len(far) :]
    arrived = [exchange(window, "mp", 1) for window in windows[1::2]]
    w_rows = (w_output, w_near)
    shares = far_branch_own(windows[0::2], w_output)
    shares = far_branch(shares, arrived, w_near, frames_local)
    mine, other = attend_near(places, shares[0], *shared, frames_local)
    shares = [exchange(share, "mp", far[number // 2]) for number, share in enumerate(shares)]
    base = near_branch(
        places, (mine, exchange(other, "mp", 1)), w_rows, stacks, fixed, weights[0], frames_local
    )
    gain = gain_convolution[None, :]
    first = finish_first(base, shares[0::2], gain, w_depthwise)
    return finish_last(base, shares[1::2], first, gain, w_depthwise, frames_local)


def solution(mesh):
    placed = (
        P(("groups", "tm", "mp")),
        P(("groups", "tm")),
        P(("groups", "tm")),
        P(),
        P(None, None, "mp"),
        P("mp", None),
        P(),
        P(),
    )
    return jax.shard_map(
        shards,
        mesh=mesh,
        in_specs=placed,
        out_specs=P(("groups", "tm", "mp"), None),
        check_vma=False,
    )
```

```python
import math

import jax
import jax.numpy as jnp
import ml_dtypes
import numpy as np
from jax import lax
from jax.experimental import pallas as pl
from jax.experimental.pallas import tpu as pltpu
from jax.sharding import PartitionSpec as P

HD = 64
NMEL = 128
NFFT = 400
HOP = 160
BINS = 256
SUB = 4
KERNEL = 31
SEG_MAX = 750
LANES = 128
HALO = 16
EXTRA = 8
FLOPS_PER_MICRO = 2000000000
TAIL_LINES = 3
HEAD_LINES = 2
DIGIT = 128
FRAME_ROWS = SUB * HOP // LANES
WIDE = -(-NFFT // LANES) * LANES


def split_high_low(table):
    high = table.astype(ml_dtypes.bfloat16)
    low = (table - high.astype(np.float32)).astype(ml_dtypes.bfloat16)
    return high, low


def fourier_table():
    sample_index = np.arange(NFFT)[:, None]
    bin_index = np.arange(BINS)[None, :]
    angle = (sample_index * bin_index % NFFT) * (2.0 * math.pi / NFFT)
    window = 0.5 - 0.5 * np.cos(np.arange(NFFT) * (2.0 * math.pi / NFFT))
    kept = bin_index <= NFFT // 2
    cosine = np.where(kept, np.cos(angle), 0.0) * window[:, None]
    sine = np.where(kept, -np.sin(angle), 0.0) * window[:, None]
    return np.concatenate([cosine, sine], axis=1).astype(np.float32)


def mel_bank():
    mel_top = 2595.0 * math.log10(1.0 + 8000.0 / 700.0)
    mel_points = np.arange(NMEL + 2) * (mel_top / (NMEL + 1))
    edges = 700.0 * (np.power(10.0, mel_points / 2595.0) - 1.0) * (NFFT / 16000.0)
    widths = np.maximum(edges[2:] - edges[1:-1], 1.0)
    bin_value = np.arange(BINS)[:, None]
    triangle = np.maximum(0.0, 1.0 - np.abs(bin_value - edges[None, 1:-1]) / widths[None, :])
    return np.where(bin_value <= NFFT // 2, triangle, 0.0).astype(np.float32)


def front_tables():
    high, low = split_high_low(fourier_table())
    bank = np.concatenate(split_high_low(mel_bank()), axis=1)
    bank = np.pad(bank, ((0, 0), (0, high.shape[1] - bank.shape[1])))
    return np.concatenate([high, low, bank], axis=0)


def dot32(left, right):
    return jnp.dot(left, right, preferred_element_type=jnp.float32)


def dot_split(values, table_high, table_low):
    high = values.astype(jnp.bfloat16)
    low = (values - high.astype(jnp.float32)).astype(jnp.bfloat16)
    table = table_high()
    large, small = dot32(high, table), dot32(low, table)
    return large + (small + dot32(high, table_low()))


def normalize(values):
    center = jnp.mean(values, axis=-1, keepdims=True)
    shifted = values - center
    spread = jnp.mean(jnp.square(shifted), axis=-1, keepdims=True)
    return shifted * lax.rsqrt(spread + 1e-05)


def call(
    kernel, out_shape, operands, scratch=(), micros=1.0, remote=0, vmem=16, result=pltpu.VMEM
):
    specs = [pl.BlockSpec(memory_space=pltpu.VMEM)] * (len(operands) - remote)
    specs += [pl.BlockSpec(memory_space=pltpu.HBM)] * remote
    return pl.pallas_call(
        kernel,
        out_shape=out_shape,
        in_specs=specs,
        out_specs=jax.tree.map(lambda _: pl.BlockSpec(memory_space=result), out_shape),
        scratch_shapes=list(scratch),
        compiler_params=pltpu.CompilerParams(vmem_limit_bytes=vmem * 1024 * 1024),
        cost_estimate=pl.CostEstimate(
            flops=int(micros * FLOPS_PER_MICRO), bytes_accessed=1000000, transcendentals=0
        ),
    )(*operands)


def fetch(stacked, w_subsample, w_attention):
    parts, _, width = w_attention.shape

    def kernel(stack_ref, w_sub, w_att, out_sub, out_att, sums, out_stack, sems):
        out_stack[...] = stack_ref[...]
        copies = [
            pltpu.make_async_copy(w_att, out_att, sems.at[0]),
            pltpu.make_async_copy(w_sub, out_sub, sems.at[1]),
        ]
        for copy in copies:
            copy.start()
        for copy in copies:
            copy.wait()
        sums[...] = jnp.zeros_like(sums)
        for part in range(parts):
            columns = out_att[part].astype(jnp.float32)
            sums[part : part + 1, :] = jnp.sum(columns, axis=0, keepdims=True)

    return call(
        kernel,
        [jax.ShapeDtypeStruct(array.shape, array.dtype) for array in (w_subsample, w_attention)]
        + [
            jax.ShapeDtypeStruct((8, width), jnp.float32),
            jax.ShapeDtypeStruct(stacked.shape, stacked.dtype),
        ],
        (stacked, w_subsample, w_attention),
        scratch=[pltpu.SemaphoreType.DMA((2,))],
        remote=2,
    )


def stack_of(ref, block, begin, end):
    half = (ref.shape[1] - EXTRA) // 2
    return jnp.concatenate([ref[block, begin:end, :], ref[block, half + begin : half + end, :]], axis=1)


def log_mel(windows, tables, copies=()):
    lanes = lax.broadcasted_iota(jnp.int32, windows.shape, 1)
    windows = jnp.where(lanes < NFFT, windows, 0.0)

    def fetched(number, begin):
        def load():
            if copies:
                copies[number].wait()
            return tables[begin : begin + WIDE, :]

        return load

    spectrum = dot_split(windows, fetched(0, 0), fetched(1, NFFT))
    power = jnp.square(spectrum[:, :BINS]) + jnp.square(spectrum[:, BINS:])
    bank = [tables[2 * NFFT :, part * NMEL : (part + 1) * NMEL] for part in range(2)]
    return jnp.log(dot_split(power, lambda: bank[0], lambda: bank[1]) + 1e-06)


def log_mel_rows(starts, ends, samples, tables, frames_local):
    rows = frames_local * FRAME_ROWS
    frames_shard = starts.shape[1]

    spans = (pl.ds(0, WIDE), pl.ds(WIDE, tables.shape[0] - WIDE))

    def kernel(start, end, wave, table, out, held, start_ref, end_ref, tables_ref, sems):
        pairs = (
            (wave, held.at[pl.ds(0, rows)]),
            (start, start_ref),
            (end, end_ref),
        ) + tuple((table.at[span], tables_ref.at[span]) for span in spans)
        copies = [
            pltpu.make_async_copy(source, target, sems.at[slot])
            for slot, (source, target) in enumerate(pairs)
        ]
        for copy in copies:
            copy.start()
        held[rows : rows + 8, :] = jnp.zeros((8, LANES), jnp.float32)
        for copy in copies[:3]:
            copy.wait()
        lines = [held[pl.ds(j, frames_local, stride=FRAME_ROWS), :] for j in range(FRAME_ROWS + 2)]
        windows = []
        for sub in range(SUB):
            line, lane = divmod(sub * HOP, LANES)
            taken = jnp.concatenate(lines[line : line + WIDE // LANES], axis=1)
            windows.append(pltpu.roll(taken, WIDE - lane, axis=1) if lane else taken)
        pieces = []
        for taken in (range(rows - TAIL_LINES, rows), range(HEAD_LINES)):
            line = jnp.concatenate([held[row : row + 1, :] for row in taken], axis=1)
            high = line.astype(jnp.bfloat16).astype(jnp.float32)
            pieces += [high, line - high]
        for ref in (start_ref, end_ref):
            edge = jnp.concatenate([ref[:, :HALO], ref[:, frames_shard - HALO :]], axis=1)
            high = edge // DIGIT
            low = edge - high * DIGIT
            pieces += [digit.astype(jnp.float32) for digit in (high, low)]
        filled = sum(piece.shape[1] for piece in pieces)
        pieces.append(jnp.zeros((1, EXTRA * 2 * NMEL - filled), jnp.float32))
        flat = jnp.concatenate(pieces, axis=1)
        extras = [flat[:, row * 2 * NMEL : (row + 1) * 2 * NMEL] for row in range(EXTRA)]
        out[0, 2 * frames_local :, :] = jnp.concatenate(extras, axis=0).astype(jnp.bfloat16)
        mel = log_mel(jnp.concatenate(windows, axis=0), tables_ref, copies[3:])
        for sub in range(SUB):
            begin, lane = sub // 2 * frames_local, sub % 2 * NMEL
            out[0, begin : begin + frames_local, lane : lane + NMEL] = mel[
                sub * frames_local : (sub + 1) * frames_local
            ].astype(jnp.bfloat16)

    return call(
        kernel,
        jax.ShapeDtypeStruct((1, 2 * frames_local + EXTRA, 2 * NMEL), jnp.bfloat16),
        (starts, ends, samples, tables),
        scratch=[
            pltpu.VMEM((rows + 8, LANES), jnp.float32),
            pltpu.VMEM(starts.shape, starts.dtype),
            pltpu.VMEM(ends.shape, ends.dtype),
            pltpu.VMEM(tables.shape, tables.dtype),
            pltpu.SemaphoreType.DMA((5,)),
        ],
        remote=4,
        vmem=54,
        micros=1.0,
    )


def boundary_rows(places, starts, ends, stacks, tables, frames_local):
    counts = [stack.shape[0] for stack in stacks]
    slots = len(places)
    rows = -(-slots // HALO) * HALO
    frames_shard = starts.shape[1]
    parts = lax.axis_size("mp")
    final = lax.axis_size("tm") * parts - 1
    shift = final + 1

    def kernel(start_ref, end_ref, *refs):
        stack_refs, refs = refs[: len(counts)], refs[len(counts) :]
        tables_ref, out, bounds, tails, heads, nexts, edges, order = refs
        time_index, model_index = lax.axis_index("tm"), lax.axis_index("mp")
        tails[...] = jnp.zeros_like(tails)
        nexts[...] = jnp.zeros_like(nexts)
        slot = 0
        for stack_ref, count in zip(stack_refs, counts):
            for block in range(count):
                kept = stack_ref[block, 2 * frames_local :, :].astype(jnp.float32)
                flat = jnp.concatenate([kept[row : row + 1] for row in range(EXTRA)], axis=1)
                here = slice(slot, slot + 1)
                tail, head = TAIL_LINES * LANES, HEAD_LINES * LANES
                tails[here, :] = flat[:, :tail] + flat[:, tail : 2 * tail]
                heads[here, :] = flat[:, 2 * tail : 2 * tail + head] + flat[
                    :, 2 * tail + head : 2 * (tail + head)
                ]
                digits = flat[:, 2 * (tail + head) :]
                for line in range(2):
                    high = digits[:, 4 * line * HALO : (4 * line + 2) * HALO]
                    low = digits[:, (4 * line + 2) * HALO : (4 * line + 4) * HALO]
                    edges[line, here, 0 : 2 * HALO] = high * DIGIT + low
                slot += 1
        numbers = [
            slot_tm(time_index) * parts + (model_index ^ slot_mp) for slot_tm, slot_mp in places
        ]
        for number in numbers:
            order[number + 1 + shift] = jnp.int32(0)
        for slot, number in enumerate(numbers):
            order[number + shift] = jnp.int32(slot)
        for slot, number in enumerate(numbers):
            taken = heads[pl.ds(order[number + 1 + shift], 1), :]
            nexts[slot : slot + 1, :] = jnp.where(number == final, 0.0, taken)
        line = jnp.concatenate([tails[...], nexts[...]], axis=1)
        windows = []
        for sub in range(SUB - 2, SUB):
            skip, lane = divmod(sub * HOP - (FRAME_ROWS - TAIL_LINES) * LANES, LANES)
            windows.append(
                pltpu.roll(line[:, skip * LANES : skip * LANES + WIDE], WIDE - lane, axis=1)
            )
        mel = log_mel(jnp.concatenate(windows, axis=0), tables_ref).astype(jnp.bfloat16)
        for number in range(2):
            lane = number * NMEL
            out[:, lane : lane + NMEL] = mel[number * rows : (number + 1) * rows]
        left = slot_of(places, time_index - 1, model_index)
        right = slot_of(places, time_index + 1, model_index)
        for number, ref in enumerate((start_ref, end_ref)):
            bounds[number : number + 1, :] = jnp.concatenate(
                [
                    edges[number, pl.ds(left, 1), :][:, HALO : 2 * HALO],
                    ref[...].astype(jnp.float32),
                    edges[number, pl.ds(right, 1), :][:, 0:HALO],
                ],
                axis=1,
            )

    return call(
        kernel,
        (
            jax.ShapeDtypeStruct((rows, 2 * NMEL), jnp.bfloat16),
            jax.ShapeDtypeStruct((2, frames_shard + 2 * HALO), jnp.float32),
        ),
        (starts, ends, *stacks, tables),
        scratch=[
            pltpu.VMEM((rows, TAIL_LINES * LANES), jnp.float32),
            pltpu.VMEM((rows, HEAD_LINES * LANES), jnp.float32),
            pltpu.VMEM((rows, HEAD_LINES * LANES), jnp.float32),
            pltpu.VMEM((2, rows, LANES), jnp.float32),
            pltpu.SMEM((3 * shift,), jnp.int32),
        ],
        micros=0.9,
    )


def last_rows(stack_refs, counts, frames_local, fixed, rows):
    lasts = []
    for stack_ref, count in zip(stack_refs, counts):
        for block in range(count):
            kept = stack_ref[block, frames_local - HALO : frames_local, :]
            lasts.append(kept.astype(jnp.float32)[HALO - 1 : HALO])
    if len(lasts) < rows:
        lasts.append(jnp.zeros((rows - len(lasts), 2 * NMEL), jnp.float32))
    return jnp.concatenate([jnp.concatenate(lasts, axis=0).astype(jnp.bfloat16), fixed], axis=1)


def patch(held, fixed, slots, frames_local):
    fixed = fixed.astype(jnp.float32)
    for number, slot in enumerate(slots):
        here = slice((number + 1) * frames_local - HALO, (number + 1) * frames_local)
        kept = held[here, :].astype(jnp.float32)
        last = lax.broadcasted_iota(jnp.int32, kept.shape, 0) == HALO - 1
        held[here, :] = jnp.where(last, fixed[slot : slot + 1, :], kept).astype(held.dtype)


def assemble(parts, after=()):
    counts = [part.shape[0] for part in parts]

    def kernel(*refs):
        begin = 0
        for ref, count in zip(refs, counts):
            refs[-1][begin : begin + count] = ref[...]
            begin += count

    shape = jax.ShapeDtypeStruct((sum(counts), *parts[0].shape[1:]), parts[0].dtype)
    return call(kernel, shape, (*parts, *after))


def slot_of(places, tm, mp):
    found = jnp.int32(0)
    for slot, (slot_tm, slot_mp) in enumerate(places):
        here = (slot_tm(lax.axis_index("tm")) == tm) & (lax.axis_index("mp") ^ slot_mp == mp)
        found = jnp.where(here, slot, found)
    return found


def project_rows(stack, weights, frames_local, query_blocks, boundary=None):
    count = stack.shape[0]
    rows, width = count * frames_local, weights[1].shape[2]
    query_rows = query_blocks * frames_local
    places, every, fixed = boundary or ((), (), jnp.zeros((0, 2 * NMEL), jnp.bfloat16))
    counts = [block.shape[0] for block in every]
    last_count = fixed.shape[0]
    extra_rows = last_count + 2 * HALO if boundary else 0

    def boundary_stack(every_refs, fixed_ref, lasts, heads, tails):
        lasts[...] = last_rows(
            every_refs, counts, frames_local, fixed_ref[...], last_count
        ).astype(jnp.float32)
        slot = 0
        for ref, blocks in zip(every_refs, counts):
            for block in range(blocks):
                heads[slot] = stack_of(ref, block, 0, HALO)
                tails[slot] = stack_of(ref, block, frames_local - HALO, frames_local)
                slot += 1
        time_index, parts = lax.axis_index("tm"), lax.axis_size("mp")
        left = slot_of(places, time_index - 1, parts - 1)
        right = slot_of(places, time_index + 1, 0)
        tail = tails[left].astype(jnp.float32)
        final = lax.broadcasted_iota(jnp.int32, tail.shape, 0) == HALO - 1
        tail = jnp.where(final, lasts[pl.ds(left, 1), :], tail).astype(jnp.bfloat16)
        return [lasts[...].astype(jnp.bfloat16), tail, heads[right]]

    def kernel(stack_ref, w_sub, w_att, sums, *refs):
        stack_rows = [stack_of(stack_ref, block, 0, frames_local) for block in range(count)]
        if boundary:
            every_refs, refs = refs[: len(every)], refs[len(every) :]
            fixed_ref, *refs = refs
            refs, scratch = refs[:-3], refs[-3:]
            stack_rows += boundary_stack(every_refs, fixed_ref, *scratch)
        features = dot32(jnp.concatenate(stack_rows, axis=0), w_sub[...]).astype(jnp.bfloat16)
        wide = features.astype(jnp.float32)
        center = jnp.mean(wide, axis=-1, keepdims=True)
        spread = jnp.mean(jnp.square(wide - center), axis=-1, keepdims=True)
        scale = lax.rsqrt(spread + 1e-05)

        def projected(part, begin, end):
            product = dot32(features[begin:end], w_att[part])
            shifted = product - center[begin:end] * sums[part : part + 1, :]
            return (shifted * scale[begin:end]).astype(jnp.bfloat16)

        refs = list(refs)
        if query_rows:
            refs.pop(0)[...] = projected(0, 0, query_rows)
        if extra_rows:
            refs.pop(0)[...] = projected(0, rows, rows + extra_rows)
        for part in (1, 2):
            both = projected(part, 0, rows + extra_rows)
            refs.pop(0)[...] = both[:rows]
            if extra_rows:
                refs.pop(0)[...] = both[rows:]

    def shape(size):
        return jax.ShapeDtypeStruct((size, width), jnp.bfloat16)

    shapes = [shape(query_rows)] * bool(query_rows) + [shape(extra_rows)] * bool(extra_rows)
    shapes += ([shape(rows)] + [shape(extra_rows)] * bool(extra_rows)) * 2
    depth = weights[0].shape[0]
    return call(
        kernel,
        shapes,
        (stack, *weights, *every) + ((fixed,) if boundary else ()),
        scratch=[
            pltpu.VMEM((last_count, depth), jnp.float32),
            pltpu.VMEM((len(places), HALO, depth), jnp.bfloat16),
            pltpu.VMEM((len(places), HALO, depth), jnp.bfloat16),
        ]
        if boundary
        else [],
        micros=0.5 + 0.006 * (rows + extra_rows),
    )


def gather_rows(places, query_slots, bounds, sources, extras, frames_local, outs):
    q_rows, k_all, v_all, q_all, first, last = outs
    parts = lax.axis_size("mp")
    frames_shard = frames_local * parts
    last_count = extras[0].shape[0] - 2 * HALO
    slots = range(len(places))
    for held, group, extra, held_slots in zip(
        (q_all, k_all, v_all), sources, extras, (query_slots, slots, slots)
    ):
        begin = 0
        for source in group:
            held[begin : begin + source.shape[0], :] = source[...]
            begin += source.shape[0]
        patch(held, extra[0:last_count, :], held_slots, frames_local)
    query_places = [places[slot] for slot in query_slots]
    q_rows[0:HALO, :] = extras[0][last_count : last_count + HALO, :]
    for part in range(parts):
        begin = HALO + part * frames_local
        slot = slot_of(query_places, lax.axis_index("tm"), part)
        start = pl.multiple_of(slot * frames_local, HALO)
        q_rows[begin : begin + frames_local, :] = q_all[pl.ds(start, frames_local), :]
    q_rows[HALO + frames_shard :, :] = extras[0][last_count + HALO :, :]
    for line, ref in enumerate((first, last)):
        row = bounds[line : line + 1, :]
        ref[...] = jnp.transpose(jnp.broadcast_to(row, (LANES, row.shape[1])))


def attend_rows(places, begin, q_rows, k_all, v_all, first, last, frames_local, result, most):
    count, width = result.shape
    rows = k_all.shape[0]
    time_index, model_index = lax.axis_index("tm"), lax.axis_index("mp")
    frames_shard = frames_local * lax.axis_size("mp")
    lows, highs = first[pl.ds(begin, count), :], last[pl.ds(begin, count), :]
    lanes = lax.broadcasted_iota(jnp.int32, (1, LANES), 1)
    for lane in range(0, rows, LANES):
        at = jnp.zeros((1, LANES), jnp.int32)
        for slot in range(lane // frames_local, -(-(lane + LANES) // frames_local)):
            if slot < len(places):
                slot_tm, slot_mp = places[slot]
                base = slot_tm(time_index) * frames_shard
                base += (model_index ^ slot_mp) * frames_local - slot * frames_local + lane
                at = jnp.where(lanes >= slot * frames_local - lane, lanes + base, at)
        at = at.astype(jnp.float32)
        most[:, lane : lane + LANES] = jnp.where((at >= lows) & (at < highs), jnp.inf, -1e30)
    for lane in range(0, width, LANES):
        span = min(LANES, width - lane)
        q_pair = q_rows[pl.ds(begin, count), lane : lane + span]
        k_pair = k_all[:, lane : lane + span]
        v_pair = v_all[:, lane : lane + span]
        heads = span // HD
        head_of = lax.broadcasted_iota(jnp.int32, (count, span), 1) // HD
        scaled = q_pair * jnp.bfloat16(1.0 / math.sqrt(HD))
        stacked = jnp.concatenate(
            [jnp.where(head_of == head, scaled, jnp.zeros_like(scaled)) for head in range(heads)],
            axis=0,
        )
        scores = lax.dot_general(
            stacked, k_pair, (((1,), (1,)), ((), ())), preferred_element_type=jnp.float32
        )
        scores = jnp.minimum(scores, jnp.concatenate([most[...]] * heads, axis=0))
        weights = jnp.exp(scores - jnp.max(scores, axis=1, keepdims=True))
        total = jnp.sum(weights, axis=1, keepdims=True)
        ratio = dot32(weights.astype(jnp.bfloat16), v_pair) / total
        merged = ratio[0:count]
        for head in range(1, heads):
            merged = jnp.where(head_of == head, ratio[head * count : (head + 1) * count], merged)
        result[:, lane : lane + span] = merged.astype(jnp.bfloat16)


def split_pair(model_index, result, mine, other, frames_local):
    window = mine.shape[0]
    place = lax.rem(model_index, 2) * frames_local
    mine[...] = result[pl.ds(pl.multiple_of(place, HALO), window), :]
    place = frames_local - place
    other[...] = result[pl.ds(pl.multiple_of(place, HALO), window), :]


def attend_far(places, query_slots, far, bounds, sources, extras, frames_local):
    width = sources[0][0].shape[1]
    query_count, rows = (sum(group.shape[0] for group in groups) for groups in sources[:2])
    sizes = [len(groups) for groups in sources]
    extended = frames_local * lax.axis_size("mp") + 2 * HALO
    window = frames_local + 2 * HALO
    pair = 2 * frames_local + 2 * HALO

    def kernel(bound_ref, *refs):
        groups = []
        for size in sizes:
            groups.append(refs[:size])
            refs = refs[size:]
        extra_refs, refs = refs[:3], refs[3:]
        windows, refs = refs[: 2 * len(far)], refs[2 * len(far) :]
        q_rows, k_all, v_all, first, last, q_all, result, most = refs
        gather_rows(
            places,
            query_slots,
            bound_ref,
            groups,
            extra_refs,
            frames_local,
            (q_rows, k_all, v_all, q_all, first, last),
        )
        model_index = lax.axis_index("mp")
        for number, bit in enumerate(far):
            begin = pl.multiple_of((model_index ^ bit) // 2 * (2 * frames_local), HALO)
            attend_rows(
                places, begin, q_rows, k_all, v_all, first, last, frames_local, result, most
            )
            split_pair(
                model_index, result, windows[2 * number], windows[2 * number + 1], frames_local
            )

    def shape(count, wide=width, dtype=jnp.bfloat16):
        return jax.ShapeDtypeStruct((count, wide), dtype)

    return call(
        kernel,
        [shape(window)] * (2 * len(far))
        + [shape(extended), shape(rows), shape(rows)]
        + [shape(extended, LANES, jnp.float32)] * 2,
        (bounds, *(array for groups in sources for array in groups), *extras),
        scratch=[
            pltpu.VMEM((query_count, width), jnp.bfloat16),
            pltpu.VMEM((pair, width), jnp.bfloat16),
            pltpu.VMEM((pair, rows), jnp.float32),
        ],
        micros=2.5 * len(far),
        vmem=16 + pair * rows * 20 // 1024 // 1024,
    )


def attend_near(places, after, q_rows, k_all, v_all, first, last, frames_local):
    rows, width = k_all.shape
    window = frames_local + 2 * HALO
    pair = 2 * frames_local + 2 * HALO

    def kernel(_, q_ref, k_ref, v_ref, first_ref, last_ref, mine, other, result, most):
        model_index = lax.axis_index("mp")
        begin = pl.multiple_of(model_index // 2 * (2 * frames_local), HALO)
        attend_rows(
            places, begin, q_ref, k_ref, v_ref, first_ref, last_ref, frames_local, result, most
        )
        split_pair(model_index, result, mine, other, frames_local)

    return call(
        kernel,
        [jax.ShapeDtypeStruct((window, width), jnp.bfloat16)] * 2,
        (after, q_rows, k_all, v_all, first, last),
        scratch=[
            pltpu.VMEM((pair, width), jnp.bfloat16),
            pltpu.VMEM((pair, rows), jnp.float32),
        ],
        micros=1.0,
        vmem=16 + pair * rows * 20 // 1024 // 1024,
    )


def far_branch_own(windows, w_own):
    count = len(windows)

    def kernel(*refs):
        for window, out in zip(refs[:count], refs[count + 1 :]):
            out[...] = dot32(window[...], refs[count][...])

    shape = jax.ShapeDtypeStruct((windows[0].shape[0], w_own.shape[1]), jnp.float32)
    return call(kernel, [shape] * count, (*windows, w_own), micros=0.4 * count)


def far_branch(shares, windows, w_near, cut):
    count = len(windows)

    def kernel(*refs):
        share_refs, window_refs, near, outs = (
            refs[:count],
            refs[count : 2 * count],
            refs[2 * count],
            refs[2 * count + 1 :],
        )
        for number, (share, window) in enumerate(zip(share_refs, window_refs)):
            total = (share[...] + dot32(window[...], near[...])).astype(jnp.bfloat16)
            outs[2 * number][...] = total[:cut]
            outs[2 * number + 1][...] = total[cut:]

    sizes = [cut, windows[0].shape[0] - cut] * count
    shapes = [jax.ShapeDtypeStruct((size, w_near.shape[1]), jnp.bfloat16) for size in sizes]
    return call(kernel, shapes, (*shares, *windows, w_near), micros=0.5 * count)


def near_branch(places, windows, w_rows, stacks, fixed, w_subsample, frames_local):
    counts = [stack.shape[0] for stack in stacks]
    depth, model = w_subsample.shape
    window = frames_local + 2 * HALO
    slots = len(places)

    def kernel(own, near, w_own, w_near, *refs):
        stack_refs, (fixed_ref, w_sub, out, held, taken) = refs[: len(counts)], refs[len(counts) :]
        begin = 0
        for stack_ref, count in zip(stack_refs, counts):
            for block in range(count):
                held[begin : begin + frames_local, :] = stack_of(stack_ref, block, 0, frames_local)
                begin += frames_local
        rows = last_rows(stack_refs, counts, frames_local, fixed_ref[...], fixed.shape[0])
        patch(held, rows, range(slots), frames_local)
        parts = lax.axis_size("mp")
        block = lax.axis_index("tm") * parts + lax.axis_index("mp") + parts

        def source(number, offset, count):
            slot = slot_of(places, number // parts - 1, lax.rem(number, parts))
            start = pl.multiple_of(slot * frames_local + offset, HALO)
            return held[pl.ds(start, count), :]

        taken[0:HALO, :] = source(block - 1, frames_local - HALO, HALO)
        taken[HALO : HALO + frames_local, :] = source(block, 0, frames_local)
        taken[HALO + frames_local : window, :] = source(block + 1, 0, HALO)
        features = dot32(taken[...], w_sub[...]).astype(jnp.bfloat16).astype(jnp.float32)
        share = dot32(own[...], w_own[...]) + dot32(near[...], w_near[...])
        out[...] = features + share

    return call(
        kernel,
        jax.ShapeDtypeStruct((window, model), jnp.float32),
        (*windows, *w_rows, *stacks, fixed, w_subsample),
        scratch=[
            pltpu.VMEM((slots * frames_local, depth), jnp.bfloat16),
            pltpu.VMEM((window, depth), jnp.bfloat16),
        ],
        micros=0.6,
    )


def convolve(held, taps, begin, count, here):
    offset = HALO - KERNEL // 2
    reach = count + 8
    rows = held[begin : begin + count + 2 * HALO, here]
    tap_rows = taps[:, here].astype(jnp.float32)
    total = jnp.zeros((count, rows.shape[1]), jnp.float32)
    for phase in range(8):
        share = jnp.zeros((reach, rows.shape[1]), jnp.float32)
        for tap in range(KERNEL):
            if (tap + offset) % 8 == phase:
                first = (tap + offset) // 8 * 8
                share += rows[first : first + reach] * tap_rows[tap : tap + 1]
        moved = pltpu.roll(share, reach - phase, axis=0) if phase else share
        total += moved[0:count]
    return total


def mix(base, shares, gain):
    mixed = base
    for share in shares:
        mixed += share[...].astype(jnp.float32)
    mixed = mixed.astype(jnp.bfloat16).astype(jnp.float32)
    return mixed, (normalize(mixed) * gain[...]).astype(jnp.bfloat16).astype(jnp.float32)


def silu(values):
    return values / (1.0 + jnp.exp(-values))


def finish_first(base, shares, gain, taps):
    count = len(shares)
    cut, model = shares[0].shape
    done = cut - 2 * HALO
    chunk = 2 * LANES

    def kernel(base_ref, *refs):
        share_refs, (gain_ref, tap_ref, out, held, mixed_rows) = refs[:count], refs[count:]
        mixed, conv_in = mix(base_ref[0:cut, :], share_refs, gain_ref)
        mixed_rows[...] = mixed
        held[...] = conv_in
        before = lax.axis_index("tm") * lax.axis_size("mp") + lax.axis_index("mp") > 0
        held[0:HALO, :] = jnp.where(before, conv_in[0:HALO], 0.0)
        for lane in range(0, model, chunk):
            here = slice(lane, lane + chunk)
            total = convolve(held, tap_ref, 0, done, here)
            out[:, here] = (mixed_rows[HALO : HALO + done, here] + silu(total)).astype(jnp.bfloat16)

    rows = jax.ShapeDtypeStruct((cut, model), jnp.float32)
    return call(
        kernel,
        (jax.ShapeDtypeStruct((done, model), jnp.bfloat16), rows, rows),
        (base, *shares, gain, taps),
        micros=0.5,
    )


def finish_last(base, shares, first, gain, taps, frames_local):
    count = len(shares)
    window, model = base.shape
    cut, done = first[1].shape[0], first[0].shape[0]
    left = frames_local - done
    chunk = 2 * LANES
    chunks = model // chunk

    def kernel(base_ref, *refs):
        share_refs, refs = refs[:count], refs[count:]
        out_ref, held_ref, mixed_ref, gain_ref, tap_ref, result, held, mixed_rows, staged, sems = refs
        copies = [pltpu.make_async_copy(out_ref, result.at[pl.ds(0, done)], sems.at[chunks])]
        copies[0].start()
        mixed, conv_in = mix(base_ref[cut:window, :], share_refs, gain_ref)
        mixed_rows[0:cut, :] = mixed_ref[...]
        mixed_rows[cut:window, :] = mixed
        held[0:cut, :] = held_ref[...]
        held[cut:window, :] = conv_in
        parts = lax.axis_size("mp")
        block = lax.axis_index("tm") * parts + lax.axis_index("mp")
        after = block < lax.axis_size("tm") * parts - 1
        held[window - HALO : window, :] = jnp.where(after, conv_in[window - HALO - cut :], 0.0)
        for number in range(chunks):
            here = slice(number * chunk, (number + 1) * chunk)
            total = convolve(held, tap_ref, done, left, here)
            kept = mixed_rows[HALO + done : HALO + frames_local, here]
            staged[:, here] = (kept + silu(total)).astype(jnp.bfloat16)
            copies.append(
                pltpu.make_async_copy(
                    staged.at[:, here], result.at[pl.ds(done, left), here], sems.at[number]
                )
            )
            copies[-1].start()
        for copy in copies:
            copy.wait()

    return call(
        kernel,
        jax.ShapeDtypeStruct((frames_local, model), jnp.bfloat16),
        (base, *shares, *first, gain, taps),
        scratch=[
            pltpu.VMEM((window, model), jnp.float32),
            pltpu.VMEM((window, model), jnp.float32),
            pltpu.VMEM((left, model), jnp.bfloat16),
            pltpu.SemaphoreType.DMA((chunks + 1,)),
        ],
        micros=1.5,
        result=pltpu.HBM,
    )


def exchange(block, axis, bit):
    return lax.ppermute(block, axis, [(i, i ^ bit) for i in range(lax.axis_size(axis))])


def shifted(block, axis, distance):
    count = lax.axis_size(axis)
    route = [(i - distance, i) for i in range(count) if 0 <= i - distance < count]
    return lax.ppermute(block, axis, route)


def shards(
    waveform,
    segment_start,
    segment_end,
    w_subsample,
    w_attention,
    w_output,
    gain_convolution,
    w_depthwise,
):
    frames_local = waveform.shape[0] // (SUB * HOP)
    frames_shard = segment_start.shape[0]
    parts, shards_total = lax.axis_size("mp"), lax.axis_size("tm")
    bits = [1 << b for b in reversed(range((parts - 1).bit_length()))]

    samples = waveform.reshape(-1, LANES)
    starts, ends = segment_start[None, :], segment_end[None, :]
    tables = jnp.asarray(front_tables())
    stacked = log_mel_rows(starts, ends, samples, tables, frames_local)
    *weights, kept = fetch(stacked, w_subsample, w_attention)

    w_near = exchange(w_output, "mp", bits[-1])

    reach = min((SEG_MAX + HALO - 2) // frames_shard + 1, shards_total - 1)
    whole = reach == shards_total - 1 and shards_total & (shards_total - 1) == 0
    if whole:
        order = dict.fromkeys([shards_total // 2, shards_total - 1, *range(1, shards_total)])
        moves = [lambda tm, bit=bit: tm ^ bit for bit in order]
        column = [exchange(stacked, "tm", bit) for bit in order]
    else:
        steps = [sign * d for d in range(1, reach + 1) for sign in (1, -1)]
        moves = [lambda tm, step=step: tm - step for step in steps]
        column = [shifted(stacked, "tm", step) for step in steps]
    early = [(kept, [(lambda tm: tm, 0)])]
    late = [(assemble(column, weights[-1:]), [(move, 0) for move in moves])]

    def across(blocks, bit):
        return [
            (exchange(block, "mp", bit), [(move, mp ^ bit) for move, mp in held])
            for block, held in blocks
        ]

    for bit in bits[:-1]:
        early, late = early + across(early, bit), late + across(late, bit)
    ready = early + late[:1]
    joined = (assemble([block for block, _ in ready]), sum([held for _, held in ready], []))
    groups = [joined] + across([joined], bits[-1])
    projected = [
        project_rows(block, weights, frames_local, len(early)) for block, _ in groups
    ]
    done = [group[-1] for group in projected]
    late = [(assemble([block], done), held) for block, held in late[1:]]
    groups += late + across(late, bits[-1])
    stacks, held = zip(*groups)
    places = sum(held, [])
    joined_slots = range(len(joined[1]), 2 * len(joined[1]))
    query_slots = [*range(len(early)), *joined_slots[: len(early)]]
    fixed, bounds = boundary_rows(places, starts, ends, stacks, tables, frames_local)
    projected += [project_rows(block, weights, frames_local, 0) for block in stacks[2:-1]]
    outs = project_rows(stacks[-1], weights, frames_local, 0, (places, stacks, fixed))
    extras = (outs[0], outs[2], outs[4])
    queries = [group[0] for group in projected[:2]]
    keys = [*(group[-2] for group in projected), outs[1]]
    values = [*(group[-1] for group in projected), outs[3]]

    far = list(range(2, parts, 2))
    outs = attend_far(
        places, query_slots, far, bounds, (queries, keys, values), extras, frames_local
    )
    windows, shared = outs[: 2 * len(far)], outs[2 * len(far) :]
    arrived = [exchange(window, "mp", 1) for window in windows[1::2]]
    w_rows = (w_output, w_near)
    shares = far_branch_own(windows[0::2], w_output)
    shares = far_branch(shares, arrived, w_near, frames_local)
    mine, other = attend_near(places, shares[0], *shared, frames_local)
    shares = [exchange(share, "mp", far[number // 2]) for number, share in enumerate(shares)]
    base = near_branch(
        places, (mine, exchange(other, "mp", 1)), w_rows, stacks, fixed, weights[0], frames_local
    )
    gain = gain_convolution[None, :]
    first = finish_first(base, shares[0::2], gain, w_depthwise)
    return finish_last(base, shares[1::2], first, gain, w_depthwise, frames_local)


def solution(mesh):
    placed = (
        P(("groups", "tm", "mp")),
        P(("groups", "tm")),
        P(("groups", "tm")),
        P(),
        P(None, None, "mp"),
        P("mp", None),
        P(),
        P(),
    )
    return jax.shard_map(
        shards,
        mesh=mesh,
        in_specs=placed,
        out_specs=P(("groups", "tm", "mp"), None),
        check_vma=False,
    )
```

```python
import math

import jax
import jax.numpy as jnp
import ml_dtypes
import numpy as np
from jax import lax
from jax.experimental import pallas as pl
from jax.experimental.pallas import tpu as pltpu
from jax.sharding import PartitionSpec as P

HD = 64
NMEL = 128
NFFT = 400
HOP = 160
BINS = 256
SUB = 4
KERNEL = 31
SEG_MAX = 750
LANES = 128
HALO = 16
EXTRA = 8
FLOPS_PER_MICRO = 2000000000
TAIL_LINES = 3
HEAD_LINES = 2
DIGIT = 128
FRAME_ROWS = SUB * HOP // LANES
WIDE = -(-NFFT // LANES) * LANES


def split_high_low(table):
    high = table.astype(ml_dtypes.bfloat16)
    low = (table - high.astype(np.float32)).astype(ml_dtypes.bfloat16)
    return high, low


def fourier_table():
    sample_index = np.arange(NFFT)[:, None]
    bin_index = np.arange(BINS)[None, :]
    angle = (sample_index * bin_index % NFFT) * (2.0 * math.pi / NFFT)
    window = 0.5 - 0.5 * np.cos(np.arange(NFFT) * (2.0 * math.pi / NFFT))
    kept = bin_index <= NFFT // 2
    cosine = np.where(kept, np.cos(angle), 0.0) * window[:, None]
    sine = np.where(kept, -np.sin(angle), 0.0) * window[:, None]
    return np.concatenate([cosine, sine], axis=1).astype(np.float32)


def mel_bank():
    mel_top = 2595.0 * math.log10(1.0 + 8000.0 / 700.0)
    mel_points = np.arange(NMEL + 2) * (mel_top / (NMEL + 1))
    edges = 700.0 * (np.power(10.0, mel_points / 2595.0) - 1.0) * (NFFT / 16000.0)
    widths = np.maximum(edges[2:] - edges[1:-1], 1.0)
    bin_value = np.arange(BINS)[:, None]
    triangle = np.maximum(0.0, 1.0 - np.abs(bin_value - edges[None, 1:-1]) / widths[None, :])
    return np.where(bin_value <= NFFT // 2, triangle, 0.0).astype(np.float32)


def front_tables():
    high, low = split_high_low(fourier_table())
    bank = np.concatenate(split_high_low(mel_bank()), axis=1)
    bank = np.pad(bank, ((0, 0), (0, high.shape[1] - bank.shape[1])))
    return np.concatenate([high, low, bank], axis=0)


def dot32(left, right):
    return jnp.dot(left, right, preferred_element_type=jnp.float32)


def dot_split(values, table_high, table_low):
    high = values.astype(jnp.bfloat16)
    low = (values - high.astype(jnp.float32)).astype(jnp.bfloat16)
    table = table_high()
    large, small = dot32(high, table), dot32(low, table)
    return large + (small + dot32(high, table_low()))


def normalize(values):
    center = jnp.mean(values, axis=-1, keepdims=True)
    shifted = values - center
    spread = jnp.mean(jnp.square(shifted), axis=-1, keepdims=True)
    return shifted * lax.rsqrt(spread + 1e-05)


def call(
    kernel, out_shape, operands, scratch=(), micros=1.0, remote=0, vmem=16, result=pltpu.VMEM
):
    specs = [pl.BlockSpec(memory_space=pltpu.VMEM)] * (len(operands) - remote)
    specs += [pl.BlockSpec(memory_space=pltpu.HBM)] * remote
    return pl.pallas_call(
        kernel,
        out_shape=out_shape,
        in_specs=specs,
        out_specs=jax.tree.map(lambda _: pl.BlockSpec(memory_space=result), out_shape),
        scratch_shapes=list(scratch),
        compiler_params=pltpu.CompilerParams(vmem_limit_bytes=vmem * 1024 * 1024),
        cost_estimate=pl.CostEstimate(
            flops=int(micros * FLOPS_PER_MICRO), bytes_accessed=1000000, transcendentals=0
        ),
    )(*operands)


def fetch(stacked, w_subsample, w_attention):
    parts, _, width = w_attention.shape

    def kernel(stack_ref, w_sub, w_att, out_sub, out_att, sums, out_stack, sems):
        out_stack[...] = stack_ref[...]
        copies = [
            pltpu.make_async_copy(w_att, out_att, sems.at[0]),
            pltpu.make_async_copy(w_sub, out_sub, sems.at[1]),
        ]
        for copy in copies:
            copy.start()
        for copy in copies:
            copy.wait()
        sums[...] = jnp.zeros_like(sums)
        for part in range(parts):
            columns = out_att[part].astype(jnp.float32)
            sums[part : part + 1, :] = jnp.sum(columns, axis=0, keepdims=True)

    return call(
        kernel,
        [jax.ShapeDtypeStruct(array.shape, array.dtype) for array in (w_subsample, w_attention)]
        + [
            jax.ShapeDtypeStruct((8, width), jnp.float32),
            jax.ShapeDtypeStruct(stacked.shape, stacked.dtype),
        ],
        (stacked, w_subsample, w_attention),
        scratch=[pltpu.SemaphoreType.DMA((2,))],
        remote=2,
    )


def stack_of(ref, block, begin, end):
    half = (ref.shape[1] - EXTRA) // 2
    return jnp.concatenate([ref[block, begin:end, :], ref[block, half + begin : half + end, :]], axis=1)


def log_mel(windows, tables, copies=()):
    lanes = lax.broadcasted_iota(jnp.int32, windows.shape, 1)
    windows = jnp.where(lanes < NFFT, windows, 0.0)

    def fetched(number, begin):
        def load():
            if copies:
                copies[number].wait()
            return tables[begin : begin + WIDE, :]

        return load

    spectrum = dot_split(windows, fetched(0, 0), fetched(1, NFFT))
    power = jnp.square(spectrum[:, :BINS]) + jnp.square(spectrum[:, BINS:])
    bank = [tables[2 * NFFT :, part * NMEL : (part + 1) * NMEL] for part in range(2)]
    return jnp.log(dot_split(power, lambda: bank[0], lambda: bank[1]) + 1e-06)


def log_mel_rows(starts, ends, samples, tables, frames_local):
    rows = frames_local * FRAME_ROWS
    frames_shard = starts.shape[1]

    spans = (pl.ds(0, WIDE), pl.ds(WIDE, tables.shape[0] - WIDE))

    def kernel(start, end, wave, table, out, held, start_ref, end_ref, tables_ref, sems):
        pairs = (
            (wave, held.at[pl.ds(0, rows)]),
            (start, start_ref),
            (end, end_ref),
        ) + tuple((table.at[span], tables_ref.at[span]) for span in spans)
        copies = [
            pltpu.make_async_copy(source, target, sems.at[slot])
            for slot, (source, target) in enumerate(pairs)
        ]
        for copy in copies:
            copy.start()
        held[rows : rows + 8, :] = jnp.zeros((8, LANES), jnp.float32)
        for copy in copies[:3]:
            copy.wait()
        lines = [held[pl.ds(j, frames_local, stride=FRAME_ROWS), :] for j in range(FRAME_ROWS + 2)]
        windows = []
        for sub in range(SUB):
            line, lane = divmod(sub * HOP, LANES)
            taken = jnp.concatenate(lines[line : line + WIDE // LANES], axis=1)
            windows.append(pltpu.roll(taken, WIDE - lane, axis=1) if lane else taken)
        pieces = []
        for taken in (range(rows - TAIL_LINES, rows), range(HEAD_LINES)):
            line = jnp.concatenate([held[row : row + 1, :] for row in taken], axis=1)
            high = line.astype(jnp.bfloat16).astype(jnp.float32)
            pieces += [high, line - high]
        for ref in (start_ref, end_ref):
            edge = jnp.concatenate([ref[:, :HALO], ref[:, frames_shard - HALO :]], axis=1)
            high = edge // DIGIT
            low = edge - high * DIGIT
            pieces += [digit.astype(jnp.float32) for digit in (high, low)]
        filled = sum(piece.shape[1] for piece in pieces)
        pieces.append(jnp.zeros((1, EXTRA * 2 * NMEL - filled), jnp.float32))
        flat = jnp.concatenate(pieces, axis=1)
        extras = [flat[:, row * 2 * NMEL : (row + 1) * 2 * NMEL] for row in range(EXTRA)]
        out[0, 2 * frames_local :, :] = jnp.concatenate(extras, axis=0).astype(jnp.bfloat16)
        mel = log_mel(jnp.concatenate(windows, axis=0), tables_ref, copies[3:])
        for sub in range(SUB):
            begin, lane = sub // 2 * frames_local, sub % 2 * NMEL
            out[0, begin : begin + frames_local, lane : lane + NMEL] = mel[
                sub * frames_local : (sub + 1) * frames_local
            ].astype(jnp.bfloat16)

    return call(
        kernel,
        jax.ShapeDtypeStruct((1, 2 * frames_local + EXTRA, 2 * NMEL), jnp.bfloat16),
        (starts, ends, samples, tables),
        scratch=[
            pltpu.VMEM((rows + 8, LANES), jnp.float32),
            pltpu.VMEM(starts.shape, starts.dtype),
            pltpu.VMEM(ends.shape, ends.dtype),
            pltpu.VMEM(tables.shape, tables.dtype),
            pltpu.SemaphoreType.DMA((5,)),
        ],
        remote=4,
        vmem=54,
        micros=1.0,
    )


def boundary_rows(places, starts, ends, stacks, tables, frames_local):
    counts = [stack.shape[0] for stack in stacks]
    slots = len(places)
    rows = -(-slots // HALO) * HALO
    frames_shard = starts.shape[1]
    parts = lax.axis_size("mp")
    final = lax.axis_size("tm") * parts - 1
    shift = final + 1

    def kernel(start_ref, end_ref, *refs):
        stack_refs, refs = refs[: len(counts)], refs[len(counts) :]
        tables_ref, out, bounds, tails, heads, nexts, edges, order = refs
        time_index, model_index = lax.axis_index("tm"), lax.axis_index("mp")
        tails[...] = jnp.zeros_like(tails)
        nexts[...] = jnp.zeros_like(nexts)
        slot = 0
        for stack_ref, count in zip(stack_refs, counts):
            for block in range(count):
                kept = stack_ref[block, 2 * frames_local :, :].astype(jnp.float32)
                flat = jnp.concatenate([kept[row : row + 1] for row in range(EXTRA)], axis=1)
                here = slice(slot, slot + 1)
                tail, head = TAIL_LINES * LANES, HEAD_LINES * LANES
                tails[here, :] = flat[:, :tail] + flat[:, tail : 2 * tail]
                heads[here, :] = flat[:, 2 * tail : 2 * tail + head] + flat[
                    :, 2 * tail + head : 2 * (tail + head)
                ]
                digits = flat[:, 2 * (tail + head) :]
                for line in range(2):
                    high = digits[:, 4 * line * HALO : (4 * line + 2) * HALO]
                    low = digits[:, (4 * line + 2) * HALO : (4 * line + 4) * HALO]
                    edges[line, here, 0 : 2 * HALO] = high * DIGIT + low
                slot += 1
        numbers = [
            slot_tm(time_index) * parts + (model_index ^ slot_mp) for slot_tm, slot_mp in places
        ]
        for number in numbers:
            order[number + 1 + shift] = jnp.int32(0)
        for slot, number in enumerate(numbers):
            order[number + shift] = jnp.int32(slot)
        for slot, number in enumerate(numbers):
            taken = heads[pl.ds(order[number + 1 + shift], 1), :]
            nexts[slot : slot + 1, :] = jnp.where(number == final, 0.0, taken)
        line = jnp.concatenate([tails[...], nexts[...]], axis=1)
        windows = []
        for sub in range(SUB - 2, SUB):
            skip, lane = divmod(sub * HOP - (FRAME_ROWS - TAIL_LINES) * LANES, LANES)
            windows.append(
                pltpu.roll(line[:, skip * LANES : skip * LANES + WIDE], WIDE - lane, axis=1)
            )
        mel = log_mel(jnp.concatenate(windows, axis=0), tables_ref).astype(jnp.bfloat16)
        for number in range(2):
            lane = number * NMEL
            out[:, lane : lane + NMEL] = mel[number * rows : (number + 1) * rows]
        left = slot_of(places, time_index - 1, model_index)
        right = slot_of(places, time_index + 1, model_index)
        for number, ref in enumerate((start_ref, end_ref)):
            bounds[number : number + 1, :] = jnp.concatenate(
                [
                    edges[number, pl.ds(left, 1), :][:, HALO : 2 * HALO],
                    ref[...].astype(jnp.float32),
                    edges[number, pl.ds(right, 1), :][:, 0:HALO],
                ],
                axis=1,
            )

    return call(
        kernel,
        (
            jax.ShapeDtypeStruct((rows, 2 * NMEL), jnp.bfloat16),
            jax.ShapeDtypeStruct((2, frames_shard + 2 * HALO), jnp.float32),
        ),
        (starts, ends, *stacks, tables),
        scratch=[
            pltpu.VMEM((rows, TAIL_LINES * LANES), jnp.float32),
            pltpu.VMEM((rows, HEAD_LINES * LANES), jnp.float32),
            pltpu.VMEM((rows, HEAD_LINES * LANES), jnp.float32),
            pltpu.VMEM((2, rows, LANES), jnp.float32),
            pltpu.SMEM((3 * shift,), jnp.int32),
        ],
        micros=0.9,
    )


def last_rows(stack_refs, counts, frames_local, fixed, rows):
    lasts = []
    for stack_ref, count in zip(stack_refs, counts):
        for block in range(count):
            kept = stack_ref[block, frames_local - HALO : frames_local, :]
            lasts.append(kept.astype(jnp.float32)[HALO - 1 : HALO])
    if len(lasts) < rows:
        lasts.append(jnp.zeros((rows - len(lasts), 2 * NMEL), jnp.float32))
    return jnp.concatenate([jnp.concatenate(lasts, axis=0).astype(jnp.bfloat16), fixed], axis=1)


def patch(held, fixed, slots, frames_local):
    fixed = fixed.astype(jnp.float32)
    for number, slot in enumerate(slots):
        here = slice((number + 1) * frames_local - HALO, (number + 1) * frames_local)
        kept = held[here, :].astype(jnp.float32)
        last = lax.broadcasted_iota(jnp.int32, kept.shape, 0) == HALO - 1
        held[here, :] = jnp.where(last, fixed[slot : slot + 1, :], kept).astype(held.dtype)


def assemble(parts, after=()):
    counts = [part.shape[0] for part in parts]

    def kernel(*refs):
        begin = 0
        for ref, count in zip(refs, counts):
            refs[-1][begin : begin + count] = ref[...]
            begin += count

    shape = jax.ShapeDtypeStruct((sum(counts), *parts[0].shape[1:]), parts[0].dtype)
    return call(kernel, shape, (*parts, *after))


def slot_of(places, tm, mp):
    found = jnp.int32(0)
    for slot, (slot_tm, slot_mp) in enumerate(places):
        here = (slot_tm(lax.axis_index("tm")) == tm) & (lax.axis_index("mp") ^ slot_mp == mp)
        found = jnp.where(here, slot, found)
    return found


def project_rows(stack, weights, frames_local, query_blocks, boundary=None):
    count = stack.shape[0]
    rows, width = count * frames_local, weights[1].shape[2]
    query_rows = query_blocks * frames_local
    places, every, fixed = boundary or ((), (), jnp.zeros((0, 2 * NMEL), jnp.bfloat16))
    counts = [block.shape[0] for block in every]
    last_count = fixed.shape[0]
    extra_rows = last_count + 2 * HALO if boundary else 0

    def boundary_stack(every_refs, fixed_ref, lasts, heads, tails):
        lasts[...] = last_rows(
            every_refs, counts, frames_local, fixed_ref[...], last_count
        ).astype(jnp.float32)
        slot = 0
        for ref, blocks in zip(every_refs, counts):
            for block in range(blocks):
                heads[slot] = stack_of(ref, block, 0, HALO)
                tails[slot] = stack_of(ref, block, frames_local - HALO, frames_local)
                slot += 1
        time_index, parts = lax.axis_index("tm"), lax.axis_size("mp")
        left = slot_of(places, time_index - 1, parts - 1)
        right = slot_of(places, time_index + 1, 0)
        tail = tails[left].astype(jnp.float32)
        final = lax.broadcasted_iota(jnp.int32, tail.shape, 0) == HALO - 1
        tail = jnp.where(final, lasts[pl.ds(left, 1), :], tail).astype(jnp.bfloat16)
        return [lasts[...].astype(jnp.bfloat16), tail, heads[right]]

    def kernel(stack_ref, w_sub, w_att, sums, *refs):
        stack_rows = [stack_of(stack_ref, block, 0, frames_local) for block in range(count)]
        if boundary:
            every_refs, refs = refs[: len(every)], refs[len(every) :]
            fixed_ref, *refs = refs
            refs, scratch = refs[:-3], refs[-3:]
            stack_rows += boundary_stack(every_refs, fixed_ref, *scratch)
        features = dot32(jnp.concatenate(stack_rows, axis=0), w_sub[...]).astype(jnp.bfloat16)
        wide = features.astype(jnp.float32)
        center = jnp.mean(wide, axis=-1, keepdims=True)
        spread = jnp.mean(jnp.square(wide - center), axis=-1, keepdims=True)
        scale = lax.rsqrt(spread + 1e-05)

        def projected(part, begin, end):
            product = dot32(features[begin:end], w_att[part])
            shifted = product - center[begin:end] * sums[part : part + 1, :]
            return (shifted * scale[begin:end]).astype(jnp.bfloat16)

        refs = list(refs)
        if query_rows:
            refs.pop(0)[...] = projected(0, 0, query_rows)
        if extra_rows:
            refs.pop(0)[...] = projected(0, rows, rows + extra_rows)
        for part in (1, 2):
            both = projected(part, 0, rows + extra_rows)
            refs.pop(0)[...] = both[:rows]
            if extra_rows:
                refs.pop(0)[...] = both[rows:]

    def shape(size):
        return jax.ShapeDtypeStruct((size, width), jnp.bfloat16)

    shapes = [shape(query_rows)] * bool(query_rows) + [shape(extra_rows)] * bool(extra_rows)
    shapes += ([shape(rows)] + [shape(extra_rows)] * bool(extra_rows)) * 2
    depth = weights[0].shape[0]
    return call(
        kernel,
        shapes,
        (stack, *weights, *every) + ((fixed,) if boundary else ()),
        scratch=[
            pltpu.VMEM((last_count, depth), jnp.float32),
            pltpu.VMEM((len(places), HALO, depth), jnp.bfloat16),
            pltpu.VMEM((len(places), HALO, depth), jnp.bfloat16),
        ]
        if boundary
        else [],
        micros=0.5 + 0.006 * (rows + extra_rows),
    )


def gather_rows(places, query_slots, bounds, sources, extras, frames_local, outs):
    q_rows, k_all, v_all, q_all, first, last = outs
    parts = lax.axis_size("mp")
    frames_shard = frames_local * parts
    last_count = extras[0].shape[0] - 2 * HALO
    slots = range(len(places))
    for held, group, extra, held_slots in zip(
        (q_all, k_all, v_all), sources, extras, (query_slots, slots, slots)
    ):
        begin = 0
        for source in group:
            held[begin : begin + source.shape[0], :] = source[...]
            begin += source.shape[0]
        patch(held, extra[0:last_count, :], held_slots, frames_local)
    query_places = [places[slot] for slot in query_slots]
    q_rows[0:HALO, :] = extras[0][last_count : last_count + HALO, :]
    for part in range(parts):
        begin = HALO + part * frames_local
        slot = slot_of(query_places, lax.axis_index("tm"), part)
        start = pl.multiple_of(slot * frames_local, HALO)
        q_rows[begin : begin + frames_local, :] = q_all[pl.ds(start, frames_local), :]
    q_rows[HALO + frames_shard :, :] = extras[0][last_count + HALO :, :]
    for line, ref in enumerate((first, last)):
        row = bounds[line : line + 1, :]
        ref[...] = jnp.transpose(jnp.broadcast_to(row, (LANES, row.shape[1])))


def attend_rows(places, begin, q_rows, k_all, v_all, first, last, frames_local, result, most):
    count, width = result.shape
    rows = k_all.shape[0]
    time_index, model_index = lax.axis_index("tm"), lax.axis_index("mp")
    frames_shard = frames_local * lax.axis_size("mp")
    lows, highs = first[pl.ds(begin, count), :], last[pl.ds(begin, count), :]
    lanes = lax.broadcasted_iota(jnp.int32, (1, LANES), 1)
    for lane in range(0, rows, LANES):
        at = jnp.zeros((1, LANES), jnp.int32)
        for slot in range(lane // frames_local, -(-(lane + LANES) // frames_local)):
            if slot < len(places):
                slot_tm, slot_mp = places[slot]
                base = slot_tm(time_index) * frames_shard
                base += (model_index ^ slot_mp) * frames_local - slot * frames_local + lane
                at = jnp.where(lanes >= slot * frames_local - lane, lanes + base, at)
        at = at.astype(jnp.float32)
        most[:, lane : lane + LANES] = jnp.where((at >= lows) & (at < highs), jnp.inf, -1e30)
    for lane in range(0, width, LANES):
        span = min(LANES, width - lane)
        q_pair = q_rows[pl.ds(begin, count), lane : lane + span]
        k_pair = k_all[:, lane : lane + span]
        v_pair = v_all[:, lane : lane + span]
        heads = span // HD
        head_of = lax.broadcasted_iota(jnp.int32, (count, span), 1) // HD
        scaled = q_pair * jnp.bfloat16(1.0 / math.sqrt(HD))
        stacked = jnp.concatenate(
            [jnp.where(head_of == head, scaled, jnp.zeros_like(scaled)) for head in range(heads)],
            axis=0,
        )
        scores = lax.dot_general(
            stacked, k_pair, (((1,), (1,)), ((), ())), preferred_element_type=jnp.float32
        )
        scores = jnp.minimum(scores, jnp.concatenate([most[...]] * heads, axis=0))
        weights = jnp.exp(scores - jnp.max(scores, axis=1, keepdims=True))
        summed = dot32(
            weights.astype(jnp.bfloat16), jnp.concatenate([v_pair, jnp.ones_like(v_pair)], axis=1)
        )
        ratio = summed[:, :span] / summed[:, span:]
        merged = ratio[0:count]
        for head in range(1, heads):
            merged = jnp.where(head_of == head, ratio[head * count : (head + 1) * count], merged)
        result[:, lane : lane + span] = merged.astype(jnp.bfloat16)


def split_pair(model_index, result, mine, other, frames_local):
    window = mine.shape[0]
    place = lax.rem(model_index, 2) * frames_local
    mine[...] = result[pl.ds(pl.multiple_of(place, HALO), window), :]
    place = frames_local - place
    other[...] = result[pl.ds(pl.multiple_of(place, HALO), window), :]


def attend_far(places, query_slots, far, bounds, sources, extras, frames_local):
    width = sources[0][0].shape[1]
    query_count, rows = (sum(group.shape[0] for group in groups) for groups in sources[:2])
    sizes = [len(groups) for groups in sources]
    extended = frames_local * lax.axis_size("mp") + 2 * HALO
    window = frames_local + 2 * HALO
    pair = 2 * frames_local + 2 * HALO

    def kernel(bound_ref, *refs):
        groups = []
        for size in sizes:
            groups.append(refs[:size])
            refs = refs[size:]
        extra_refs, refs = refs[:3], refs[3:]
        windows, refs = refs[: 2 * len(far)], refs[2 * len(far) :]
        q_rows, k_all, v_all, first, last, q_all, result, most = refs
        gather_rows(
            places,
            query_slots,
            bound_ref,
            groups,
            extra_refs,
            frames_local,
            (q_rows, k_all, v_all, q_all, first, last),
        )
        model_index = lax.axis_index("mp")
        for number, bit in enumerate(far):
            begin = pl.multiple_of((model_index ^ bit) // 2 * (2 * frames_local), HALO)
            attend_rows(
                places, begin, q_rows, k_all, v_all, first, last, frames_local, result, most
            )
            split_pair(
                model_index, result, windows[2 * number], windows[2 * number + 1], frames_local
            )

    def shape(count, wide=width, dtype=jnp.bfloat16):
        return jax.ShapeDtypeStruct((count, wide), dtype)

    return call(
        kernel,
        [shape(window)] * (2 * len(far))
        + [shape(extended), shape(rows), shape(rows)]
        + [shape(extended, LANES, jnp.float32)] * 2,
        (bounds, *(array for groups in sources for array in groups), *extras),
        scratch=[
            pltpu.VMEM((query_count, width), jnp.bfloat16),
            pltpu.VMEM((pair, width), jnp.bfloat16),
            pltpu.VMEM((pair, rows), jnp.float32),
        ],
        micros=2.5 * len(far),
        vmem=16 + pair * rows * 20 // 1024 // 1024,
    )


def attend_near(places, after, q_rows, k_all, v_all, first, last, frames_local):
    rows, width = k_all.shape
    window = frames_local + 2 * HALO
    pair = 2 * frames_local + 2 * HALO

    def kernel(_, q_ref, k_ref, v_ref, first_ref, last_ref, mine, other, result, most):
        model_index = lax.axis_index("mp")
        begin = pl.multiple_of(model_index // 2 * (2 * frames_local), HALO)
        attend_rows(
            places, begin, q_ref, k_ref, v_ref, first_ref, last_ref, frames_local, result, most
        )
        split_pair(model_index, result, mine, other, frames_local)

    return call(
        kernel,
        [jax.ShapeDtypeStruct((window, width), jnp.bfloat16)] * 2,
        (after, q_rows, k_all, v_all, first, last),
        scratch=[
            pltpu.VMEM((pair, width), jnp.bfloat16),
            pltpu.VMEM((pair, rows), jnp.float32),
        ],
        micros=1.0,
        vmem=16 + pair * rows * 20 // 1024 // 1024,
    )


def far_branch_own(windows, w_own):
    count = len(windows)

    def kernel(*refs):
        for window, out in zip(refs[:count], refs[count + 1 :]):
            out[...] = dot32(window[...], refs[count][...])

    shape = jax.ShapeDtypeStruct((windows[0].shape[0], w_own.shape[1]), jnp.float32)
    return call(kernel, [shape] * count, (*windows, w_own), micros=0.4 * count)


def far_branch(shares, windows, w_near, cut):
    count = len(windows)

    def kernel(*refs):
        share_refs, window_refs, near, outs = (
            refs[:count],
            refs[count : 2 * count],
            refs[2 * count],
            refs[2 * count + 1 :],
        )
        for number, (share, window) in enumerate(zip(share_refs, window_refs)):
            total = (share[...] + dot32(window[...], near[...])).astype(jnp.bfloat16)
            outs[2 * number][...] = total[:cut]
            outs[2 * number + 1][...] = total[cut:]

    sizes = [cut, windows[0].shape[0] - cut] * count
    shapes = [jax.ShapeDtypeStruct((size, w_near.shape[1]), jnp.bfloat16) for size in sizes]
    return call(kernel, shapes, (*shares, *windows, w_near), micros=0.5 * count)


def near_branch(places, windows, w_rows, stacks, fixed, w_subsample, frames_local):
    counts = [stack.shape[0] for stack in stacks]
    depth, model = w_subsample.shape
    window = frames_local + 2 * HALO
    slots = len(places)

    def kernel(own, near, w_own, w_near, *refs):
        stack_refs, (fixed_ref, w_sub, out, held, taken) = refs[: len(counts)], refs[len(counts) :]
        begin = 0
        for stack_ref, count in zip(stack_refs, counts):
            for block in range(count):
                held[begin : begin + frames_local, :] = stack_of(stack_ref, block, 0, frames_local)
                begin += frames_local
        rows = last_rows(stack_refs, counts, frames_local, fixed_ref[...], fixed.shape[0])
        patch(held, rows, range(slots), frames_local)
        parts = lax.axis_size("mp")
        block = lax.axis_index("tm") * parts + lax.axis_index("mp") + parts

        def source(number, offset, count):
            slot = slot_of(places, number // parts - 1, lax.rem(number, parts))
            start = pl.multiple_of(slot * frames_local + offset, HALO)
            return held[pl.ds(start, count), :]

        taken[0:HALO, :] = source(block - 1, frames_local - HALO, HALO)
        taken[HALO : HALO + frames_local, :] = source(block, 0, frames_local)
        taken[HALO + frames_local : window, :] = source(block + 1, 0, HALO)
        features = dot32(taken[...], w_sub[...]).astype(jnp.bfloat16).astype(jnp.float32)
        share = dot32(own[...], w_own[...]) + dot32(near[...], w_near[...])
        out[...] = features + share

    return call(
        kernel,
        jax.ShapeDtypeStruct((window, model), jnp.float32),
        (*windows, *w_rows, *stacks, fixed, w_subsample),
        scratch=[
            pltpu.VMEM((slots * frames_local, depth), jnp.bfloat16),
            pltpu.VMEM((window, depth), jnp.bfloat16),
        ],
        micros=0.6,
    )


def convolve(held, taps, begin, count, here):
    offset = HALO - KERNEL // 2
    reach = count + 8
    rows = held[begin : begin + count + 2 * HALO, here]
    tap_rows = taps[:, here].astype(jnp.float32)
    total = jnp.zeros((count, rows.shape[1]), jnp.float32)
    for phase in range(8):
        share = jnp.zeros((reach, rows.shape[1]), jnp.float32)
        for tap in range(KERNEL):
            if (tap + offset) % 8 == phase:
                first = (tap + offset) // 8 * 8
                share += rows[first : first + reach] * tap_rows[tap : tap + 1]
        moved = pltpu.roll(share, reach - phase, axis=0) if phase else share
        total += moved[0:count]
    return total


def mix(base, shares, gain):
    mixed = base
    for share in shares:
        mixed += share[...].astype(jnp.float32)
    mixed = mixed.astype(jnp.bfloat16).astype(jnp.float32)
    return mixed, (normalize(mixed) * gain[...]).astype(jnp.bfloat16).astype(jnp.float32)


def silu(values):
    return values / (1.0 + jnp.exp(-values))


def finish_first(base, shares, gain, taps):
    count = len(shares)
    cut, model = shares[0].shape
    done = cut - 2 * HALO
    chunk = 2 * LANES

    def kernel(base_ref, *refs):
        share_refs, (gain_ref, tap_ref, out, held, mixed_rows) = refs[:count], refs[count:]
        mixed, conv_in = mix(base_ref[0:cut, :], share_refs, gain_ref)
        mixed_rows[...] = mixed
        held[...] = conv_in
        before = lax.axis_index("tm") * lax.axis_size("mp") + lax.axis_index("mp") > 0
        held[0:HALO, :] = jnp.where(before, conv_in[0:HALO], 0.0)
        for lane in range(0, model, chunk):
            here = slice(lane, lane + chunk)
            total = convolve(held, tap_ref, 0, done, here)
            out[:, here] = (mixed_rows[HALO : HALO + done, here] + silu(total)).astype(jnp.bfloat16)

    rows = jax.ShapeDtypeStruct((cut, model), jnp.float32)
    return call(
        kernel,
        (jax.ShapeDtypeStruct((done, model), jnp.bfloat16), rows, rows),
        (base, *shares, gain, taps),
        micros=0.5,
    )


def finish_last(base, shares, first, gain, taps, frames_local):
    count = len(shares)
    window, model = base.shape
    cut, done = first[1].shape[0], first[0].shape[0]
    left = frames_local - done
    chunk = 2 * LANES
    chunks = model // chunk

    def kernel(base_ref, *refs):
        share_refs, refs = refs[:count], refs[count:]
        out_ref, held_ref, mixed_ref, gain_ref, tap_ref, result, held, mixed_rows, staged, sems = refs
        copies = [pltpu.make_async_copy(out_ref, result.at[pl.ds(0, done)], sems.at[chunks])]
        copies[0].start()
        mixed, conv_in = mix(base_ref[cut:window, :], share_refs, gain_ref)
        mixed_rows[0:cut, :] = mixed_ref[...]
        mixed_rows[cut:window, :] = mixed
        held[0:cut, :] = held_ref[...]
        held[cut:window, :] = conv_in
        parts = lax.axis_size("mp")
        block = lax.axis_index("tm") * parts + lax.axis_index("mp")
        after = block < lax.axis_size("tm") * parts - 1
        held[window - HALO : window, :] = jnp.where(after, conv_in[window - HALO - cut :], 0.0)
        for number in range(chunks):
            here = slice(number * chunk, (number + 1) * chunk)
            total = convolve(held, tap_ref, done, left, here)
            kept = mixed_rows[HALO + done : HALO + frames_local, here]
            staged[:, here] = (kept + silu(total)).astype(jnp.bfloat16)
            copies.append(
                pltpu.make_async_copy(
                    staged.at[:, here], result.at[pl.ds(done, left), here], sems.at[number]
                )
            )
            copies[-1].start()
        for copy in copies:
            copy.wait()

    return call(
        kernel,
        jax.ShapeDtypeStruct((frames_local, model), jnp.bfloat16),
        (base, *shares, *first, gain, taps),
        scratch=[
            pltpu.VMEM((window, model), jnp.float32),
            pltpu.VMEM((window, model), jnp.float32),
            pltpu.VMEM((left, model), jnp.bfloat16),
            pltpu.SemaphoreType.DMA((chunks + 1,)),
        ],
        micros=1.5,
        result=pltpu.HBM,
    )


def exchange(block, axis, bit):
    return lax.ppermute(block, axis, [(i, i ^ bit) for i in range(lax.axis_size(axis))])


def shifted(block, axis, distance):
    count = lax.axis_size(axis)
    route = [(i - distance, i) for i in range(count) if 0 <= i - distance < count]
    return lax.ppermute(block, axis, route)


def shards(
    waveform,
    segment_start,
    segment_end,
    w_subsample,
    w_attention,
    w_output,
    gain_convolution,
    w_depthwise,
):
    frames_local = waveform.shape[0] // (SUB * HOP)
    frames_shard = segment_start.shape[0]
    parts, shards_total = lax.axis_size("mp"), lax.axis_size("tm")
    bits = [1 << b for b in reversed(range((parts - 1).bit_length()))]

    samples = waveform.reshape(-1, LANES)
    starts, ends = segment_start[None, :], segment_end[None, :]
    tables = jnp.asarray(front_tables())
    stacked = log_mel_rows(starts, ends, samples, tables, frames_local)
    *weights, kept = fetch(stacked, w_subsample, w_attention)

    w_near = exchange(w_output, "mp", bits[-1])

    reach = min((SEG_MAX + HALO - 2) // frames_shard + 1, shards_total - 1)
    whole = reach == shards_total - 1 and shards_total & (shards_total - 1) == 0
    if whole:
        order = dict.fromkeys([shards_total // 2, shards_total - 1, *range(1, shards_total)])
        moves = [lambda tm, bit=bit: tm ^ bit for bit in order]
        column = [exchange(stacked, "tm", bit) for bit in order]
    else:
        steps = [sign * d for d in range(1, reach + 1) for sign in (1, -1)]
        moves = [lambda tm, step=step: tm - step for step in steps]
        column = [shifted(stacked, "tm", step) for step in steps]
    early = [(kept, [(lambda tm: tm, 0)])]
    late = [(assemble(column, weights[-1:]), [(move, 0) for move in moves])]

    def across(blocks, bit):
        return [
            (exchange(block, "mp", bit), [(move, mp ^ bit) for move, mp in held])
            for block, held in blocks
        ]

    for bit in bits[:-1]:
        early, late = early + across(early, bit), late + across(late, bit)
    ready = early + late[:1]
    joined = (assemble([block for block, _ in ready]), sum([held for _, held in ready], []))
    groups = [joined] + across([joined], bits[-1])
    projected = [
        project_rows(block, weights, frames_local, len(early)) for block, _ in groups
    ]
    done = [group[-1] for group in projected]
    late = [(assemble([block], done), held) for block, held in late[1:]]
    groups += late + across(late, bits[-1])
    stacks, held = zip(*groups)
    places = sum(held, [])
    joined_slots = range(len(joined[1]), 2 * len(joined[1]))
    query_slots = [*range(len(early)), *joined_slots[: len(early)]]
    fixed, bounds = boundary_rows(places, starts, ends, stacks, tables, frames_local)
    projected += [project_rows(block, weights, frames_local, 0) for block in stacks[2:-1]]
    outs = project_rows(stacks[-1], weights, frames_local, 0, (places, stacks, fixed))
    extras = (outs[0], outs[2], outs[4])
    queries = [group[0] for group in projected[:2]]
    keys = [*(group[-2] for group in projected), outs[1]]
    values = [*(group[-1] for group in projected), outs[3]]

    far = list(range(2, parts, 2))
    outs = attend_far(
        places, query_slots, far, bounds, (queries, keys, values), extras, frames_local
    )
    windows, shared = outs[: 2 * len(far)], outs[2 * len(far) :]
    arrived = [exchange(window, "mp", 1) for window in windows[1::2]]
    w_rows = (w_output, w_near)
    shares = far_branch_own(windows[0::2], w_output)
    shares = far_branch(shares, arrived, w_near, frames_local)
    mine, other = attend_near(places, shares[0], *shared, frames_local)
    shares = [exchange(share, "mp", far[number // 2]) for number, share in enumerate(shares)]
    base = near_branch(
        places, (mine, exchange(other, "mp", 1)), w_rows, stacks, fixed, weights[0], frames_local
    )
    gain = gain_convolution[None, :]
    first = finish_first(base, shares[0::2], gain, w_depthwise)
    return finish_last(base, shares[1::2], first, gain, w_depthwise, frames_local)


def solution(mesh):
    placed = (
        P(("groups", "tm", "mp")),
        P(("groups", "tm")),
        P(("groups", "tm")),
        P(),
        P(None, None, "mp"),
        P("mp", None),
        P(),
        P(),
    )
    return jax.shard_map(
        shards,
        mesh=mesh,
        in_specs=placed,
        out_specs=P(("groups", "tm", "mp"), None),
        check_vma=False,
    )
```
